32 devices in a mesh: seq: 8 (over z, y), tp: 4 (over x, core).
Axes of the slice: x: 2, y: 2, z: 4, core: 2. Of those that a mesh axis runs over, the one named last changes fastest.
Arguments:
- tokens: bfloat16 [128, 1536], replicated, may hold values from -6 to 6
- attn_gain: float32 [1536], replicated, may hold values from 0.25 to 1.75
- qkv_weight: bfloat16 [1536, 2560], P(None, 'tp'), may hold values from -0.15625 to 0.15625
- out_weight: bfloat16 [1536, 1536], P(None, 'tp'), may hold values from -0.15625 to 0.15625
- moe_gain: float32 [1536], P('tp'), may hold values from 0.25 to 1.75
- router_weight: bfloat16 [1536, 40], P('tp'), may hold values from -0.3125 to 0.3125
- expert_gate: bfloat16 [40, 1536, 512], P(None, 'tp', 'seq'), may hold values from -0.15625 to 0.15625
- expert_up: bfloat16 [40, 1536, 512], P(None, 'tp', 'seq'), may hold values from -0.15625 to 0.15625
- expert_down: bfloat16 [40, 512, 1536], P(None, 'seq', 'tp'), may hold values from -0.375 to 0.375
- cache_keys: bfloat16 [32, 256, 512], P(None, 'seq', 'tp'), may hold values from -240 to 240, as said below
- cache_values: bfloat16 [32, 256, 512], P(None, 'seq', 'tp'), may hold values from -8 to 8
- lengths: int32 [32], replicated, may hold values from 1 to 32768, as said below
- routes: int32 [128, 8], replicated, may hold values from 0 to 39, all different within a row
Outputs:
- layer_out: bfloat16 [128, 1536], P(None, 'tp')
The draws below stay inside these ranges and needn't reach their ends.
Inputs may be any that keep to these rules, and one draw needn't show every extreme that they name: `lengths`: one request has exactly 32768 cached positions. `cache_keys`: cached keys are already rotated.
All inputs are finite; a program needn't handle non-finite values.
Results may differ from the reference program's by a relative error of at most 0.014.
Values may be sent and summed in bfloat16 or wider, within the bound.
A program may use at most 128 MiB of HBM per device.

```python
import jax
import jax.numpy as jnp
from jax import lax

D = 1536
HEADS = 24
KV_HEADS = 8
HEAD = 64
EXPERTS = 40
FF_E = 512
TOP = 8
SINK = 4
NEW = 4
MAXLEN = 32768
REQS = 32
GROUP = 3
CACHE = 256
WINDOW = 252
TOKENS = 128


def draw_cache_keys(key, part):
    base = jax.random.truncated_normal(key, -6.0, 6.0, (REQS, CACHE, KV_HEADS * HEAD), jnp.float32)
    return base.astype(jnp.bfloat16)


def draw_cache_values(key, part):
    slope = (jnp.arange(CACHE, dtype=jnp.float32) * (2.0 / (CACHE - 1)) - 1.0)[None, :, None]
    signs = jnp.where(jax.random.uniform(jax.random.fold_in(key, 3), (REQS, 1, KV_HEADS * HEAD)) < 0.5, -1.0, 1.0)
    base = jax.random.truncated_normal(key, -5.0, 5.0, (REQS, CACHE, KV_HEADS * HEAD), jnp.float32)
    amount = jnp.full((REQS, 1, KV_HEADS * HEAD), 1.5, jnp.float32)
    return (base + amount * slope * signs).astype(jnp.bfloat16)


def draw_lengths(key, part):
    exponents = jax.random.randint(jax.random.fold_in(key, 1), (REQS,), 1, 16)
    upper = jnp.left_shift(jnp.ones((REQS,), jnp.int32), exponents) + 1
    drawn = jax.random.randint(jax.random.fold_in(key, 2), (REQS,), 1, upper)
    return drawn.at[0].set(MAXLEN).astype(jnp.int32)


def level_of(own_key, dims, pieces, least, high):
    level = 1.0
    for axis_at, shards_of in pieces:
        draws = jax.random.uniform(jax.random.fold_in(jax.random.fold_in(own_key, 6), axis_at), (shards_of,), jnp.float32, least / len(pieces), high / len(pieces))
        level = level * jnp.repeat(jnp.exp(draws), dims[axis_at] // shards_of).reshape((-1,) + (1,) * (len(dims) - 1 - axis_at))
    return level


def choose_distinct(key, rows, number_of, top, lift):
    sequence = jax.random.permutation(jax.random.fold_in(key, 1), number_of)
    boost = sequence
    for power in range(3):
        boost = boost * boost // number_of
    boost = boost * lift // number_of
    chance = jax.random.randint(jax.random.fold_in(key, 2), (rows, number_of), 0, 4096) + boost
    sure = jax.random.permutation(jax.random.fold_in(key, 3), rows)[jnp.arange(number_of) % rows]
    chance = jnp.where(jnp.arange(rows)[:, None] == sure[None, :], 1 << 14, chance)
    priority = chance * number_of + jnp.arange(number_of)
    return lax.top_k(priority.astype(jnp.int32), top)[1].astype(jnp.int32)


def centred(own_key, extent, width, most, split=(), kind=jnp.bfloat16):
    loudness = level_of(own_key, extent, split, -0.22, 0.18) if split else 1.0
    result = jax.random.normal(own_key, extent, jnp.float32) * width * loudness
    return jnp.minimum(jnp.maximum(result, -most), most).astype(kind)


def setup_inputs(seed: int = 0) -> dict:
    keys = jax.random.split(jax.random.key(seed), 14)
    return {
        "tokens": centred(keys[0], (TOKENS, D), 1.0, 6.0),
        "attn_gain": jnp.clip(1.0 + 0.15 * jax.random.normal(keys[1], (D,), jnp.float32), 0.25, 1.75),
        "qkv_weight": centred(keys[2], (D, KV_HEADS * (GROUP + 2) * HEAD), D ** -0.5, 0.15625, ((1, 4),)),
        "out_weight": centred(keys[3], (HEADS * HEAD, D), (HEADS * HEAD) ** -0.5, 0.15625, ((1, 4),)),
        "moe_gain": jnp.clip(1.0 + 0.15 * jax.random.normal(keys[4], (D,), jnp.float32), 0.25, 1.75),
        "router_weight": centred(keys[5], (D, EXPERTS), (D // 4) ** -0.5, 0.3125, ((0, 4),)),
        "expert_gate": centred(keys[6], (EXPERTS, D, FF_E), D ** -0.5, 0.15625, ((1, 4), (2, 8))),
        "expert_up": centred(keys[7], (EXPERTS, D, FF_E), D ** -0.5, 0.15625, ((1, 4), (2, 8))),
        "expert_down": centred(keys[8], (EXPERTS, FF_E, D), (FF_E // 2) ** -0.5, 0.375, ((1, 8), (2, 4))),
        "cache_keys": draw_cache_keys(jax.random.fold_in(keys[13], 71), 0),
        "cache_values": draw_cache_values(jax.random.fold_in(keys[13], 71), 0),
        "lengths": draw_lengths(jax.random.fold_in(keys[13], 71), 0),
        "routes": choose_distinct(keys[12], TOKENS, EXPERTS, TOP, 1638),
    }


EPSILON = 1e-06
ROPE_BASE = 10000.0

def rms_scale(values, gain):
    return values * lax.rsqrt(lax.optimization_barrier(jnp.mean(values * values, axis=-1, keepdims=True)) + EPSILON) * gain

def rotate(values, places):
    half_dim = values.shape[-1] // 2
    freqs = jnp.exp(-jnp.log(ROPE_BASE) * jnp.arange(half_dim, dtype=jnp.float32) / half_dim)
    angles = places.reshape((-1,) + (1,) * (values.ndim - 1)) * freqs
    cosine = jnp.cos(angles)
    sine = jnp.sin(angles)
    first = values[..., :half_dim]
    second = values[..., half_dim:]
    return jnp.concatenate([first * cosine - second * sine, first * sine + second * cosine], axis=-1)

def visible(slots, lengths, window):
    lens = lengths[:, None].astype(jnp.int32)
    slot_row = slots[None, :].astype(jnp.int32)
    live = slot_row < lens
    older = lens - 1 - jnp.mod(lens - 1 - slot_row, window)
    placed = jnp.where(slot_row < SINK, slot_row, older)
    offsets = jnp.arange(NEW, dtype=jnp.int32)
    inside = (slot_row[:, None, :] < SINK) | (placed[:, None, :] >= lens[:, :, None] + offsets[None, :, None] - window)
    return live[:, None, :] & inside

def reference(tokens, attn_gain, qkv_weight, out_weight, moe_gain, router_weight, expert_gate, expert_up, expert_down, cache_keys, cache_values, lengths, routes):
    token_full = tokens.astype(jnp.float32)
    normed = rms_scale(token_full, attn_gain.astype(jnp.float32)).astype(jnp.bfloat16)
    projected = jnp.dot(normed, qkv_weight, preferred_element_type=jnp.float32).reshape(TOKENS, KV_HEADS, GROUP + 2, HEAD)
    places = (lengths[:, None] + jnp.arange(NEW, dtype=jnp.int32)[None, :]).reshape(TOKENS).astype(jnp.float32)
    queries = rotate(projected[:, :, :GROUP], places).astype(jnp.bfloat16)
    new_keys = rotate(projected[:, :, GROUP], places).astype(jnp.bfloat16)
    new_values = projected[:, :, GROUP + 1].astype(jnp.bfloat16)
    seen_all = visible(jnp.arange(CACHE, dtype=jnp.int32), lengths, WINDOW)
    causal = jnp.arange(NEW)[:, None] >= jnp.arange(NEW)[None, :]
    factor = 1.0 / HEAD ** 0.5

    def one_request(packed):
        query, key_new, value_new, key_old, value_old, seen = packed
        query_f = query.astype(jnp.float32)
        old_scores = jnp.einsum('tgqd,sgd->tgqs', query_f, key_old.reshape(CACHE, KV_HEADS, HEAD).astype(jnp.float32)) * factor
        new_scores = jnp.einsum('tgqd,ugd->tgqu', query_f, key_new.astype(jnp.float32)) * factor
        old_scores = jnp.where(seen[:, None, None, :], old_scores, -jnp.inf)
        new_scores = jnp.where(causal[:, None, None, :], new_scores, -jnp.inf)
        scores = jnp.concatenate([old_scores, new_scores], axis=-1)
        top_score = lax.optimization_barrier(jnp.max(scores, axis=-1, keepdims=True))
        weights = jnp.exp(scores - top_score)
        total = lax.optimization_barrier(jnp.sum(weights, axis=-1, keepdims=True))
        values_all = jnp.concatenate([value_old.reshape(CACHE, KV_HEADS, HEAD), value_new], axis=0).astype(jnp.float32)
        return jnp.einsum('tgqs,sgd->tgqd', weights, values_all) / total
    attended = lax.map(one_request, (queries.reshape(REQS, NEW, KV_HEADS, GROUP, HEAD), new_keys.reshape(REQS, NEW, KV_HEADS, HEAD), new_values.reshape(REQS, NEW, KV_HEADS, HEAD), cache_keys, cache_values, seen_all))
    attended = attended.reshape(TOKENS, HEADS * HEAD).astype(jnp.bfloat16)
    residual = token_full + jnp.dot(attended, out_weight, preferred_element_type=jnp.float32)
    scale = lax.rsqrt(lax.optimization_barrier(jnp.mean(residual * residual, axis=-1)) + EPSILON)
    gained = residual * moe_gain.astype(jnp.float32)
    logits = scale[:, None] * jnp.dot(gained, router_weight.astype(jnp.float32), precision=lax.Precision.HIGHEST)
    moe_in = (gained * scale[:, None]).astype(jnp.bfloat16)
    chosen = jnp.take_along_axis(logits, routes, axis=1)
    gate_prob = jax.nn.softmax(chosen, axis=-1)
    gate_all = jnp.einsum('td,edf->tef', moe_in.astype(jnp.float32), expert_gate.astype(jnp.float32))
    up_all = jnp.einsum('td,edf->tef', moe_in.astype(jnp.float32), expert_up.astype(jnp.float32))
    gate_pick = jnp.take_along_axis(gate_all, routes[:, :, None], axis=1)
    up_pick = jnp.take_along_axis(up_all, routes[:, :, None], axis=1)
    activated = (jax.nn.silu(gate_pick) * up_pick).astype(jnp.bfloat16)
    scaled = (gate_prob[:, :, None] * activated.astype(jnp.float32)).astype(jnp.bfloat16)
    onehot = (routes[:, :, None] == jnp.arange(EXPERTS, dtype=jnp.int32)[None, None, :]).astype(jnp.float32)
    spread = jnp.einsum('tke,tkf->tef', onehot, scaled.astype(jnp.float32))
    moe_out = jnp.einsum('tef,efd->td', spread, expert_down.astype(jnp.float32))
    return (residual + moe_out).astype(jnp.bfloat16)
```

```python
import jax
import jax.numpy as jnp
from jax import lax
from jax.experimental import pallas as pl
from jax.experimental.pallas import tpu as pltpu
from jax.sharding import PartitionSpec as P

D = 1536
HEAD = 64
EXPERTS = 40
SINK = 4
NEW = 4
GROUP = 3


EPSILON = 1e-06
ROPE_BASE = 10000.0
FLOOR_SCORE = -1e30


def joined(shard, axis, combine):
    everything = jax.tree.map(lambda part: lax.all_gather(part, axis), shard)
    initial = jax.tree.map(lambda part: part[0], everything)

    def lap(k, so_far):
        return combine(so_far, jax.tree.map(lambda part: part[k], everything))

    return lax.fori_loop(1, lax.axis_size(axis), lap, initial)


def rms_scale(values, gain):
    return values * lax.rsqrt(jnp.mean(values * values, axis=-1, keepdims=True) + EPSILON) * gain


def rotate(values, places):
    half_dim = values.shape[-1] // 2
    freqs = jnp.exp(-jnp.log(ROPE_BASE) * jnp.arange(half_dim, dtype=jnp.float32) / half_dim)
    angles = places.reshape((-1,) + (1,) * (values.ndim - 1)) * freqs
    cosine = jnp.cos(angles)
    sine = jnp.sin(angles)
    first = values[..., :half_dim]
    second = values[..., half_dim:]
    return jnp.concatenate(
        [first * cosine - second * sine, first * sine + second * cosine], axis=-1
    )


def visible(slots, lengths, window):
    lens = lengths[:, None]
    slot_row = slots[None, :]
    live = slot_row < lens
    older = lens - 1 - jnp.mod(lens - 1 - slot_row, window)
    placed = jnp.where(slot_row < SINK, slot_row, older)
    offsets = jnp.arange(NEW, dtype=jnp.int32)
    inside = (slot_row[:, None, :] < SINK) | (
        placed[:, None, :] >= lens[:, :, None] + offsets[None, :, None] - window
    )
    return live[:, None, :] & inside


def combine_parts(earlier, later):
    top_a, mass_a, weighted_a = earlier
    top_b, mass_b, weighted_b = later
    top_both = jnp.maximum(top_a, top_b)
    factor_a = jnp.exp(top_a - top_both)
    factor_b = jnp.exp(top_b - top_both)
    return (
        top_both,
        mass_a * factor_a + mass_b * factor_b,
        weighted_a * factor_a[..., None] + weighted_b * factor_b[..., None],
    )


def on_device(
    tokens,
    attn_gain,
    qkv_weight,
    out_weight,
    moe_gain,
    router_weight,
    expert_gate,
    expert_up,
    expert_down,
    cache_keys,
    cache_values,
    lengths,
    routes,
):
    seq_count = lax.axis_size("seq")
    seq_index = lax.axis_index("seq")
    tp_index = lax.axis_index("tp")
    token_count = tokens.shape[0]
    requests = cache_keys.shape[0]
    slot_count = cache_keys.shape[1]
    window = slot_count * seq_count - SINK
    local_kv = cache_keys.shape[2] // HEAD
    token_full = tokens.astype(jnp.float32)
    normed = rms_scale(token_full, attn_gain).astype(jnp.bfloat16)
    projected = jnp.dot(normed, qkv_weight, preferred_element_type=jnp.float32)
    projected = projected.reshape(token_count, local_kv, GROUP + 2, HEAD)
    places = (
        (lengths[:, None] + jnp.arange(NEW, dtype=jnp.int32)[None, :])
        .reshape(token_count)
        .astype(jnp.float32)
    )
    queries = rotate(projected[:, :, :GROUP], places).astype(jnp.bfloat16)
    new_keys = rotate(projected[:, :, GROUP], places).astype(jnp.bfloat16)
    new_values = projected[:, :, GROUP + 1].astype(jnp.bfloat16)
    query_b = queries.reshape(requests, NEW, local_kv, GROUP, HEAD)
    key_new = new_keys.reshape(requests, NEW, local_kv, HEAD)
    value_new = new_values.reshape(requests, NEW, local_kv, HEAD)
    slots = seq_index * slot_count + jnp.arange(slot_count, dtype=jnp.int32)
    seen = visible(slots, lengths, window)[:, :, None, None, :]
    factor = 1.0 / HEAD**0.5
    key_old = cache_keys.reshape(requests, slot_count, local_kv, HEAD)
    value_old = cache_values.reshape(requests, slot_count, local_kv, HEAD)
    old_scores = (
        jnp.einsum("rtgqd,rsgd->rtgqs", query_b, key_old, preferred_element_type=jnp.float32)
        * factor
    )
    new_scores = (
        jnp.einsum("rtgqd,rugd->rtgqu", query_b, key_new, preferred_element_type=jnp.float32)
        * factor
    )
    causal = jnp.arange(NEW)[:, None] >= jnp.arange(NEW)[None, :]
    own_mask = causal[None, :, None, None, :] & (seq_index == 0)
    old_masked = jnp.where(seen, old_scores, FLOOR_SCORE)
    new_masked = jnp.where(own_mask, new_scores, FLOOR_SCORE)
    top_score = jnp.maximum(jnp.max(old_masked, axis=-1), jnp.max(new_masked, axis=-1))
    old_weights = jnp.where(seen, jnp.exp(old_masked - top_score[..., None]), 0.0)
    new_weights = jnp.where(own_mask, jnp.exp(new_masked - top_score[..., None]), 0.0)
    mass = jnp.sum(old_weights, axis=-1) + jnp.sum(new_weights, axis=-1)
    weighted = jnp.einsum(
        "rtgqs,rsgd->rtgqd", old_weights, value_old.astype(jnp.float32)
    ) + jnp.einsum("rtgqu,rugd->rtgqd", new_weights, value_new.astype(jnp.float32))
    top_score, mass, weighted = joined((top_score, mass, weighted), "seq", combine_parts)
    attended = (weighted / mass[..., None]).reshape(token_count, -1).astype(jnp.bfloat16)
    feature_part = out_weight.shape[1]
    attn_out = jnp.dot(
        lax.all_gather(attended, "tp", axis=1, tiled=True),
        out_weight,
        preferred_element_type=jnp.float32,
    )
    residual = (
        lax.dynamic_slice_in_dim(token_full, tp_index * feature_part, feature_part, 1) + attn_out
    )
    gained = residual * moe_gain
    squares_local = jnp.sum(residual * residual, axis=-1)
    router_f = router_weight.astype(jnp.float32)
    squares_total = lax.psum(squares_local, "tp")
    scale = lax.rsqrt(squares_total / D + EPSILON)
    logits = lax.psum(
        jnp.dot(gained * scale[:, None], router_f, precision=lax.Precision.HIGHEST), "tp"
    )
    moe_in = (gained * scale[:, None]).astype(jnp.bfloat16)
    chosen = jnp.take_along_axis(logits, routes, axis=1)
    gate_prob = jax.nn.softmax(chosen, axis=-1)
    gate_part = jnp.einsum("td,edf->tef", moe_in, expert_gate, preferred_element_type=jnp.float32)
    up_part = jnp.einsum("td,edf->tef", moe_in, expert_up, preferred_element_type=jnp.float32)
    gate_pick = jnp.take_along_axis(gate_part, routes[:, :, None], axis=1)
    up_pick = jnp.take_along_axis(up_part, routes[:, :, None], axis=1)
    gate_sum, up_sum = (
        lax.psum(gate_pick.astype(jnp.bfloat16), "tp").astype(jnp.float32),
        lax.psum(up_pick.astype(jnp.bfloat16), "tp").astype(jnp.float32),
    )
    activated = (jax.nn.silu(gate_sum) * up_sum).astype(jnp.bfloat16)
    scaled = (gate_prob[:, :, None] * activated.astype(jnp.float32)).astype(jnp.bfloat16)
    onehot = (routes[:, :, None] == jnp.arange(EXPERTS, dtype=jnp.int32)[None, None, :]).astype(
        jnp.bfloat16
    )
    spread = jnp.einsum("tke,tkf->tef", onehot, scaled, preferred_element_type=jnp.float32).astype(
        jnp.bfloat16
    )
    moe_part = jnp.einsum("tef,efd->td", spread, expert_down, preferred_element_type=jnp.float32)
    moe_out = lax.psum(moe_part, "seq")
    return (residual + moe_out).astype(jnp.bfloat16)


TOP = 8
TILE = 16
LANES = 128
SEQ = 8
TP = 4
MESH = pl.DeviceIdType.MESH


def fits_fused(mesh):
    return mesh.shape["seq"] == SEQ and mesh.shape["tp"] == TP


def lane_of(shape):
    return lax.broadcasted_iota(jnp.int32, shape, len(shape) - 1)


def swap_half(values):
    return pltpu.roll(values, 64, 1)


def split_pair(values):
    high = values.astype(jnp.bfloat16).astype(jnp.float32)
    return jnp.where(lane_of(values.shape) < 64, high, values - high).astype(jnp.bfloat16)


def join_pair(packed):
    values = packed.astype(jnp.float32)
    return values + swap_half(values)


def layer_kernel(
    tokens_ref,
    attn_gain_ref,
    moe_gain_ref,
    cos_ref,
    sin_ref,
    bias_ref,
    routes_ref,
    router_ref,
    qkv_hbm,
    keys_hbm,
    values_hbm,
    out_w_hbm,
    gate_hbm,
    up_hbm,
    down_hbm,
    out_ref,
    qkv_ref,
    keys_ref,
    values_ref,
    out_w_ref,
    gate_ref,
    up_ref,
    down_ref,
    att_send,
    att_recv,
    att_all,
    res_own,
    res_all,
    pair_w,
    dense,
    onehot,
    shifted,
    picks,
    picks_recv,
    picks_half,
    picks_far,
    logit_rows,
    scaled,
    scaled_f,
    total,
    part_send,
    part_recv,
    out_own,
    local_sem,
    seq_send,
    seq_recv,
    tp_send,
    tp_recv,
):
    me = lax.axis_index("seq")
    tp = lax.axis_index("tp")
    core = lax.rem(tp, 2)
    core_peer = tp + 1 - 2 * core
    far_peer = lax.rem(tp + 2, TP)
    f32, bf16 = jnp.float32, jnp.bfloat16

    barrier = pltpu.get_barrier_semaphore()
    for step in range(1, SEQ):
        pl.semaphore_signal(
            barrier, inc=1, device_id=(lax.rem(me + step, SEQ), tp), device_id_type=MESH
        )
    for step in range(1, TP):
        pl.semaphore_signal(
            barrier, inc=1, device_id=(me, lax.rem(tp + step, TP)), device_id_type=MESH
        )

    loads = [
        pltpu.make_async_copy(src, dst, local_sem.at[n])
        for n, (src, dst) in enumerate(
            [
                (qkv_hbm, qkv_ref),
                (keys_hbm, keys_ref),
                (values_hbm, values_ref),
                (gate_hbm, gate_ref),
                (up_hbm, up_ref),
                (out_w_hbm, out_w_ref),
                (down_hbm, down_ref),
            ]
        )
    ]
    for load in loads:
        load.start()

    def seq_copies(phase, source, target):
        copies = []
        for step in range(1, SEQ):
            peer = lax.rem(me + step, SEQ)
            copies.append(
                pltpu.make_async_remote_copy(
                    src_ref=source(peer),
                    dst_ref=target(me),
                    send_sem=seq_send.at[phase, step],
                    recv_sem=seq_recv.at[phase, step],
                    device_id=(peer, tp),
                    device_id_type=MESH,
                )
            )
        for copy in copies:
            copy.start()
        return copies

    def tp_copy(slot, source, target, peer):
        copy = pltpu.make_async_remote_copy(
            src_ref=source,
            dst_ref=target,
            send_sem=tp_send.at[slot],
            recv_sem=tp_recv.at[slot],
            device_id=(me, peer),
            device_id_type=MESH,
        )
        copy.start()
        return copy

    def rows_of(index):
        return pl.ds(pl.multiple_of(index * TILE, TILE), TILE)

    token_full = tokens_ref[...].astype(f32)
    normed = rms_scale(token_full, attn_gain_ref[...]).astype(bf16)
    loads[0].wait()
    projected = jnp.dot(normed, qkv_ref[...], preferred_element_type=f32)
    tiles = [projected[:, LANES * n : LANES * (n + 1)] for n in range(5)]
    lane = lane_of(tiles[0].shape)
    low = lane < 64
    cosine, sine = cos_ref[...], sin_ref[...]

    def turned(x):
        swapped = jnp.where(lane % 64 < 32, pltpu.roll(x, 96, 1), pltpu.roll(x, 32, 1))
        return x * cosine + swapped * sine

    turn = [turned(x) for x in tiles]
    factor = 1.0 / HEAD**0.5
    queries = [
        jnp.where(low, turn[0], 0.0),
        jnp.where(low, swap_half(turn[0]), 0.0),
        jnp.where(low, turn[1], 0.0),
        jnp.where(low, 0.0, turn[2]),
        jnp.where(low, 0.0, swap_half(turn[3])),
        jnp.where(low, 0.0, turn[3]),
    ]
    queries = [(q * factor).astype(bf16) for q in queries]
    new_keys = jnp.where(low, swap_half(turn[1]), swap_half(turn[4])).astype(bf16)
    new_values = jnp.where(low, tiles[2], tiles[4]).astype(bf16)

    loads[1].wait()
    loads[2].wait()
    row32 = lax.broadcasted_iota(jnp.int32, (32, 32), 0)
    col32 = lax.broadcasted_iota(jnp.int32, (32, 32), 1)
    own = (row32 // NEW == col32 // NEW) & (col32 <= row32) & (me == 0)
    own_bias = jnp.where(own, 0.0, FLOOR_SCORE).astype(f32)
    own_bias = jnp.concatenate([own_bias] * 6, axis=0)
    contract = (((1,), (1,)), ((), ()))
    for block in range(4):
        at = slice(32 * block, 32 * block + 32)
        slots = slice(256 * block, 256 * block + 256)
        query = jnp.concatenate([q[at] for q in queries], axis=0)
        old_bias = jnp.concatenate([bias_ref[at, :]] * 6, axis=0)
        old = lax.dot_general(query, keys_ref[slots, :], contract, preferred_element_type=f32)
        new = lax.dot_general(query, new_keys[at], contract, preferred_element_type=f32)
        old = old + old_bias
        new = new + own_bias
        top = jnp.maximum(
            jnp.max(old, axis=-1, keepdims=True), jnp.max(new, axis=-1, keepdims=True)
        )
        old = jnp.exp(old - top)
        new = jnp.exp(new - top)
        mass = jnp.sum(old, axis=-1, keepdims=True) + jnp.sum(new, axis=-1, keepdims=True)
        mixed = jnp.dot(
            old.astype(bf16), values_ref[slots, :], preferred_element_type=f32
        ) + jnp.dot(new.astype(bf16), new_values[at], preferred_element_type=f32)
        mixed = mixed / mass
        level = top + jnp.log(mass)
        head = [mixed[32 * n : 32 * n + 32] for n in range(6)]
        lane32 = lane_of((32, LANES))
        low32 = lane32 < 64
        att_send[at, 0:128] = jnp.where(low32, head[0], swap_half(head[1])).astype(bf16)
        att_send[at, 128:256] = jnp.where(low32, head[2], head[3]).astype(bf16)
        att_send[at, 256:384] = jnp.where(low32, swap_half(head[4]), head[5]).astype(bf16)
        levels = jnp.zeros((32, LANES), f32)
        for n in range(6):
            levels = jnp.where(lane32 % 8 == n, level[32 * n : 32 * n + 32], levels)
        high = levels.astype(bf16).astype(f32)
        rest = levels - high
        middle = rest.astype(bf16).astype(f32)
        levels = jnp.where(
            lane32 < 8, high, jnp.where(lane32 < 16, middle, rest - middle)
        )
        att_send[at, 384:512] = jnp.where(lane32 < 24, levels, 0.0).astype(bf16)

    pl.semaphore_wait(barrier, SEQ + TP - 2)
    copies = seq_copies(
        0, lambda peer: att_send.at[rows_of(peer), :], lambda index: att_recv.at[index]
    )
    att_recv[me] = att_send[rows_of(me), :]

    loads[3].wait()
    loads[4].wait()

    def pack(n, carry):
        pair_w[n] = jnp.concatenate(
            [gate_ref[2 * n], up_ref[2 * n], gate_ref[2 * n + 1], up_ref[2 * n + 1]], axis=-1
        )
        return carry

    lax.fori_loop(0, EXPERTS // 2, pack, 0)
    spread_col = lax.broadcasted_iota(jnp.int32, (TILE, EXPERTS * TILE), 1)
    spread_row = lax.broadcasted_iota(jnp.int32, (TILE, EXPERTS * TILE), 0)
    expert_at = jnp.where(spread_col % TILE == spread_row, spread_col // TILE, -1)

    def mark(n, carry):
        routes = routes_ref[rows_of(n), :]
        for k in range(TOP):
            hit = routes[:, k : k + 1] == expert_at
            onehot[n, TILE * k : TILE * (k + 1), :] = jnp.where(hit, 1.0, 0.0).astype(bf16)
        return carry

    lax.fori_loop(0, 8, mark, 0)
    half_lane = jnp.where(low, 0, 1)
    for k in range(TOP):
        shifted[k] = routes_ref[:, k : k + 1] - half_lane

    for copy in copies:
        copy.wait()
    own_level = []
    for n in range(SEQ):
        packed = att_recv[n, :, 384:512].astype(f32)
        own_level.append(packed + pltpu.roll(packed, 120, 1) + pltpu.roll(packed, 112, 1))
    top = own_level[0]
    for n in range(1, SEQ):
        top = jnp.maximum(top, own_level[n])
    weights = [jnp.exp(x - top) for x in own_level]
    mass = weights[0]
    for n in range(1, SEQ):
        mass = mass + weights[n]
    low16 = lane_of((TILE, LANES)) < 64
    parts = [jnp.zeros((TILE, LANES), f32) for _ in range(3)]
    for n in range(SEQ):
        share = weights[n] / mass
        for j in range(3):
            wide = jnp.where(low16, share[:, 2 * j : 2 * j + 1], share[:, 2 * j + 1 : 2 * j + 2])
            parts[j] = parts[j] + wide * att_recv[n, :, 128 * j : 128 * j + 128].astype(f32)
    att_all[tp] = jnp.concatenate(parts, axis=-1).astype(bf16)

    copies = [
        tp_copy(step, att_all.at[tp], att_all.at[tp], lax.rem(tp + step, TP))
        for step in range(1, TP)
    ]
    loads[5].wait()
    width = out_w_ref.shape[1]
    residual = tokens_ref[rows_of(me), pl.ds(pl.multiple_of(tp * width, 128), width)].astype(f32)
    for copy in copies:
        copy.wait()
    for n in range(TP):
        residual = residual + jnp.dot(
            att_all[n], out_w_ref[width * n : width * (n + 1), :], preferred_element_type=f32
        )
    res_own[...] = residual
    res_all[me] = residual.astype(bf16)
    copies = seq_copies(1, lambda peer: res_all.at[me], lambda index: res_all.at[index])
    for copy in copies:
        copy.wait()

    full = res_all[...].reshape(SEQ * TILE, width).astype(f32)
    gained = full * moe_gain_ref[...]
    gained_b = gained.astype(bf16)
    rest = (gained - gained_b.astype(f32)).astype(bf16)
    router = router_ref[...]
    logits = jnp.dot(gained_b, router, preferred_element_type=f32) + jnp.dot(
        rest, router, preferred_element_type=f32
    )
    squares = jnp.sum(full * full, axis=-1, keepdims=True)
    logit_rows[...] = jnp.zeros_like(logit_rows)
    logit_rows[:, 0:EXPERTS] = logits
    rows = jnp.where(lane == EXPERTS, squares, logit_rows[...])
    rows = split_pair(jnp.where(low, rows, swap_half(rows)))
    picks[:, TOP * TILE :, :] = rows.reshape(8, TILE, LANES)

    def experts(n, carry):
        both = jnp.dot(gained_b, pair_w[n], preferred_element_type=f32).astype(bf16)
        dense[2 * n] = both[:, :LANES]
        dense[2 * n + 1] = both[:, LANES:]
        return carry

    lax.fori_loop(0, EXPERTS // 2, experts, 0)

    def pick(n, carry):
        group = dense[:, rows_of(n), :].reshape(EXPERTS * TILE, LANES)
        picks[n, 0 : TOP * TILE, :] = jnp.dot(
            onehot[n], group, preferred_element_type=f32
        ).astype(bf16)
        return carry

    lax.fori_loop(0, 8, pick, 0)

    mine = pl.ds(4 * core, 4)
    copy = tp_copy(4, picks.at[pl.ds(4 * (1 - core), 4)], picks_recv, core_peer)
    copy.wait()
    picks_half[:, 0 : TOP * TILE, :] = (
        picks[mine, 0 : TOP * TILE, :].astype(f32) + picks_recv[:, 0 : TOP * TILE, :].astype(f32)
    ).astype(bf16)
    ours = picks[mine, TOP * TILE :, :].reshape(64, LANES)
    theirs = picks_recv[:, TOP * TILE :, :].reshape(64, LANES)
    picks_half[:, TOP * TILE :, :] = split_pair(join_pair(ours) + join_pair(theirs)).reshape(
        4, TILE, LANES
    )
    copy = tp_copy(5, picks_half, picks_far, far_peer)
    copy.wait()
    rows = join_pair(picks_half[:, TOP * TILE :, :].reshape(64, LANES)) + join_pair(
        picks_far[:, TOP * TILE :, :].reshape(64, LANES)
    )
    lane64 = lane_of((64, LANES))
    low64 = lane64 < 64
    scale = lax.rsqrt(rows[:, EXPERTS : EXPERTS + 1] / D + EPSILON)
    routes = routes_ref[pl.ds(pl.multiple_of(64 * core, 64), 64), :]
    hits = [lane64 == routes[:, k : k + 1] for k in range(TOP)]
    routed = hits[0]
    for k in range(1, TOP):
        routed = routed | hits[k]
    scores = jnp.where(routed, rows * scale, FLOOR_SCORE)
    prob = jnp.exp(scores - jnp.max(scores, axis=-1, keepdims=True))
    prob = jnp.where(routed, prob, 0.0)
    prob = prob / jnp.sum(prob, axis=-1, keepdims=True)
    for k in range(TOP):
        at = slice(TILE * k, TILE * (k + 1))
        both = (picks_half[:, at, :].astype(f32) + picks_far[:, at, :].astype(f32)).reshape(
            64, LANES
        ) * scale
        active = both / (1.0 + jnp.exp(-both)) * swap_half(both)
        active = active.astype(bf16).astype(f32)
        active = active * jnp.sum(jnp.where(hits[k], prob, 0.0), axis=-1, keepdims=True)
        active = jnp.where(low64, active, swap_half(active))
        scaled[mine, at, :] = active.astype(bf16).reshape(4, TILE, LANES)
    copy = tp_copy(6, scaled.at[mine], scaled.at[mine], core_peer)
    loads[6].wait()
    copy.wait()

    for k in range(TOP):
        scaled_f[k] = scaled[:, TILE * k : TILE * (k + 1), :].reshape(128, LANES).astype(f32)
    total[...] = jnp.zeros_like(total)

    def down(n, carry):
        spread = []
        for pair in range(2):
            wanted = 4 * n + 2 * pair
            one = jnp.zeros((128, LANES), f32)
            for k in range(TOP):
                one = jnp.where(shifted[k] == wanted, scaled_f[k], one)
            spread.append(one)
        spread = jnp.concatenate(spread, axis=-1).astype(bf16)
        weight = down_ref[pl.ds(4 * n, 4)].reshape(256, width)
        total[...] += jnp.dot(spread, weight, preferred_element_type=f32)
        return carry

    lax.fori_loop(0, EXPERTS // 4, down, 0)
    part_send[...] = total[...].astype(bf16)

    copies = seq_copies(
        2, lambda peer: part_send.at[rows_of(peer), :], lambda index: part_recv.at[index]
    )
    result = res_own[...] + total[rows_of(me), :]
    for copy in copies:
        copy.wait()
    part_recv[me] = jnp.zeros((TILE, width), bf16)
    for n in range(SEQ):
        result = result + part_recv[n].astype(f32)
    out_own[...] = result.astype(bf16)
    out_ref[rows_of(me), :] = out_own[...]
    copies = seq_copies(3, lambda peer: out_own, lambda index: out_ref.at[rows_of(index), :])
    for copy in copies:
        copy.wait()


def fused_device(
    tokens,
    attn_gain,
    qkv_weight,
    out_weight,
    moe_gain,
    router_weight,
    expert_gate,
    expert_up,
    expert_down,
    cache_keys,
    cache_values,
    lengths,
    routes,
):
    seq_index = lax.axis_index("seq")
    count = tokens.shape[0]
    width = out_weight.shape[1]
    requests, slot_count = cache_keys.shape[:2]
    window = slot_count * SEQ - SINK
    places = (
        (lengths[:, None] + jnp.arange(NEW, dtype=jnp.int32)[None, :])
        .reshape(count)
        .astype(jnp.float32)
    )
    lane = jnp.arange(LANES, dtype=jnp.int32)
    half = HEAD // 2
    freqs = jnp.exp(-jnp.log(ROPE_BASE) * (lane % half).astype(jnp.float32) / half)
    angles = places[:, None] * freqs[None, :]
    cosine = jnp.cos(angles)
    sine = jnp.where((lane % HEAD < half)[None, :], -jnp.sin(angles), jnp.sin(angles))
    column = jnp.arange(8 * slot_count, dtype=jnp.int32)
    token = jnp.arange(count, dtype=jnp.int32)
    lens = jnp.repeat(lengths, NEW)[:, None]
    slot = (seq_index * slot_count + column % slot_count)[None, :]
    older = lens - 1 - jnp.mod(lens - 1 - slot, window)
    seen = (slot < lens) & ((slot < SINK) | (older >= lens + (token % NEW)[:, None] - window))
    same = ((token // NEW) % 8)[:, None] == (column // slot_count)[None, :]
    bias = jnp.where(seen & same, 0.0, FLOOR_SCORE).astype(jnp.float32)

    vmem = pl.BlockSpec(memory_space=pltpu.VMEM)
    anywhere = pl.BlockSpec(memory_space=pl.ANY)
    bf16, f32 = jnp.bfloat16, jnp.float32
    hidden = expert_gate.shape[2]
    return pl.pallas_call(
        layer_kernel,
        out_shape=jax.ShapeDtypeStruct((count, width), bf16),
        in_specs=[vmem] * 8 + [anywhere] * 7,
        out_specs=vmem,
        scratch_shapes=[
            pltpu.VMEM(qkv_weight.shape, bf16),
            pltpu.VMEM((requests * slot_count, LANES), bf16),
            pltpu.VMEM((requests * slot_count, LANES), bf16),
            pltpu.VMEM(out_weight.shape, bf16),
            pltpu.VMEM(expert_gate.shape, bf16),
            pltpu.VMEM(expert_up.shape, bf16),
            pltpu.VMEM(expert_down.shape, bf16),
            pltpu.VMEM((count, 512), bf16),
            pltpu.VMEM((SEQ, TILE, 512), bf16),
            pltpu.VMEM((TP, TILE, width), bf16),
            pltpu.VMEM((TILE, width), f32),
            pltpu.VMEM((SEQ, TILE, width), bf16),
            pltpu.VMEM((EXPERTS // 2, width, 4 * hidden), bf16),
            pltpu.VMEM((EXPERTS, count, LANES), bf16),
            pltpu.VMEM((8, TOP * TILE, EXPERTS * TILE), bf16),
            pltpu.VMEM((TOP, count, LANES), jnp.int32),
            pltpu.VMEM((8, (TOP + 1) * TILE, LANES), bf16),
            pltpu.VMEM((4, (TOP + 1) * TILE, LANES), bf16),
            pltpu.VMEM((4, (TOP + 1) * TILE, LANES), bf16),
            pltpu.VMEM((4, (TOP + 1) * TILE, LANES), bf16),
            pltpu.VMEM((count, LANES), f32),
            pltpu.VMEM((8, TOP * TILE, LANES), bf16),
            pltpu.VMEM((TOP, count, LANES), f32),
            pltpu.VMEM((count, width), f32),
            pltpu.VMEM((count, width), bf16),
            pltpu.VMEM((SEQ, TILE, width), bf16),
            pltpu.VMEM((TILE, width), bf16),
            pltpu.SemaphoreType.DMA((7,)),
            pltpu.SemaphoreType.DMA((4, SEQ)),
            pltpu.SemaphoreType.DMA((4, SEQ)),
            pltpu.SemaphoreType.DMA((7,)),
            pltpu.SemaphoreType.DMA((7,)),
        ],
        compiler_params=pltpu.CompilerParams(
            collective_id=0, has_side_effects=True, vmem_limit_bytes=48 * 1024 * 1024
        ),
        cost_estimate=pl.CostEstimate(
            flops=2_000_000_000, bytes_accessed=20_000_000, transcendentals=1_000_000
        ),
        name="layer",
    )(
        tokens,
        attn_gain.reshape(1, -1),
        moe_gain.reshape(1, -1),
        cosine,
        sine,
        bias,
        routes,
        router_weight,
        qkv_weight,
        cache_keys.reshape(-1, LANES),
        cache_values.reshape(-1, LANES),
        out_weight,
        expert_gate,
        expert_up,
        expert_down,
    )


def solution(mesh):
    in_specs = (
        P(),
        P(),
        P(None, "tp"),
        P(None, "tp"),
        P("tp"),
        P("tp", None),
        P(None, "tp", "seq"),
        P(None, "tp", "seq"),
        P(None, "seq", "tp"),
        P(None, "seq", "tp"),
        P(None, "seq", "tp"),
        P(),
        P(),
    )
    out_specs = P(None, "tp")
    body = fused_device if fits_fused(mesh) else on_device
    return jax.shard_map(
        body, mesh=mesh, in_specs=in_specs, out_specs=out_specs, check_vma=False
    )
```

```python
import jax
import jax.numpy as jnp
import numpy as np
from jax import lax
from jax.experimental import pallas as pl
from jax.experimental.pallas import tpu as pltpu
from jax.sharding import PartitionSpec as P

D = 1536
HEAD = 64
EXPERTS = 40
SINK = 4
NEW = 4
GROUP = 3


EPSILON = 1e-06
ROPE_BASE = 10000.0
FLOOR_SCORE = -1e30


def joined(shard, axis, combine):
    everything = jax.tree.map(lambda part: lax.all_gather(part, axis), shard)
    initial = jax.tree.map(lambda part: part[0], everything)

    def lap(k, so_far):
        return combine(so_far, jax.tree.map(lambda part: part[k], everything))

    return lax.fori_loop(1, lax.axis_size(axis), lap, initial)


def rms_scale(values, gain):
    return values * lax.rsqrt(jnp.mean(values * values, axis=-1, keepdims=True) + EPSILON) * gain


def rotate(values, places):
    half_dim = values.shape[-1] // 2
    freqs = jnp.exp(-jnp.log(ROPE_BASE) * jnp.arange(half_dim, dtype=jnp.float32) / half_dim)
    angles = places.reshape((-1,) + (1,) * (values.ndim - 1)) * freqs
    cosine = jnp.cos(angles)
    sine = jnp.sin(angles)
    first = values[..., :half_dim]
    second = values[..., half_dim:]
    return jnp.concatenate(
        [first * cosine - second * sine, first * sine + second * cosine], axis=-1
    )


def visible(slots, lengths, window):
    lens = lengths[:, None]
    slot_row = slots[None, :]
    live = slot_row < lens
    older = lens - 1 - jnp.mod(lens - 1 - slot_row, window)
    placed = jnp.where(slot_row < SINK, slot_row, older)
    offsets = jnp.arange(NEW, dtype=jnp.int32)
    inside = (slot_row[:, None, :] < SINK) | (
        placed[:, None, :] >= lens[:, :, None] + offsets[None, :, None] - window
    )
    return live[:, None, :] & inside


def combine_parts(earlier, later):
    top_a, mass_a, weighted_a = earlier
    top_b, mass_b, weighted_b = later
    top_both = jnp.maximum(top_a, top_b)
    factor_a = jnp.exp(top_a - top_both)
    factor_b = jnp.exp(top_b - top_both)
    return (
        top_both,
        mass_a * factor_a + mass_b * factor_b,
        weighted_a * factor_a[..., None] + weighted_b * factor_b[..., None],
    )


def on_device(
    tokens,
    attn_gain,
    qkv_weight,
    out_weight,
    moe_gain,
    router_weight,
    expert_gate,
    expert_up,
    expert_down,
    cache_keys,
    cache_values,
    lengths,
    routes,
):
    seq_count = lax.axis_size("seq")
    seq_index = lax.axis_index("seq")
    tp_index = lax.axis_index("tp")
    token_count = tokens.shape[0]
    requests = cache_keys.shape[0]
    slot_count = cache_keys.shape[1]
    window = slot_count * seq_count - SINK
    local_kv = cache_keys.shape[2] // HEAD
    token_full = tokens.astype(jnp.float32)
    normed = rms_scale(token_full, attn_gain).astype(jnp.bfloat16)
    projected = jnp.dot(normed, qkv_weight, preferred_element_type=jnp.float32)
    projected = projected.reshape(token_count, local_kv, GROUP + 2, HEAD)
    places = (
        (lengths[:, None] + jnp.arange(NEW, dtype=jnp.int32)[None, :])
        .reshape(token_count)
        .astype(jnp.float32)
    )
    queries = rotate(projected[:, :, :GROUP], places).astype(jnp.bfloat16)
    new_keys = rotate(projected[:, :, GROUP], places).astype(jnp.bfloat16)
    new_values = projected[:, :, GROUP + 1].astype(jnp.bfloat16)
    query_b = queries.reshape(requests, NEW, local_kv, GROUP, HEAD)
    key_new = new_keys.reshape(requests, NEW, local_kv, HEAD)
    value_new = new_values.reshape(requests, NEW, local_kv, HEAD)
    slots = seq_index * slot_count + jnp.arange(slot_count, dtype=jnp.int32)
    seen = visible(slots, lengths, window)[:, :, None, None, :]
    factor = 1.0 / HEAD**0.5
    key_old = cache_keys.reshape(requests, slot_count, local_kv, HEAD)
    value_old = cache_values.reshape(requests, slot_count, local_kv, HEAD)
    old_scores = (
        jnp.einsum("rtgqd,rsgd->rtgqs", query_b, key_old, preferred_element_type=jnp.float32)
        * factor
    )
    new_scores = (
        jnp.einsum("rtgqd,rugd->rtgqu", query_b, key_new, preferred_element_type=jnp.float32)
        * factor
    )
    causal = jnp.arange(NEW)[:, None] >= jnp.arange(NEW)[None, :]
    own_mask = causal[None, :, None, None, :] & (seq_index == 0)
    old_masked = jnp.where(seen, old_scores, FLOOR_SCORE)
    new_masked = jnp.where(own_mask, new_scores, FLOOR_SCORE)
    top_score = jnp.maximum(jnp.max(old_masked, axis=-1), jnp.max(new_masked, axis=-1))
    old_weights = jnp.where(seen, jnp.exp(old_masked - top_score[..., None]), 0.0)
    new_weights = jnp.where(own_mask, jnp.exp(new_masked - top_score[..., None]), 0.0)
    mass = jnp.sum(old_weights, axis=-1) + jnp.sum(new_weights, axis=-1)
    weighted = jnp.einsum(
        "rtgqs,rsgd->rtgqd", old_weights, value_old.astype(jnp.float32)
    ) + jnp.einsum("rtgqu,rugd->rtgqd", new_weights, value_new.astype(jnp.float32))
    top_score, mass, weighted = joined((top_score, mass, weighted), "seq", combine_parts)
    attended = (weighted / mass[..., None]).reshape(token_count, -1).astype(jnp.bfloat16)
    feature_part = out_weight.shape[1]
    attn_out = jnp.dot(
        lax.all_gather(attended, "tp", axis=1, tiled=True),
        out_weight,
        preferred_element_type=jnp.float32,
    )
    residual = (
        lax.dynamic_slice_in_dim(token_full, tp_index * feature_part, feature_part, 1) + attn_out
    )
    gained = residual * moe_gain
    squares_local = jnp.sum(residual * residual, axis=-1)
    router_f = router_weight.astype(jnp.float32)
    squares_total = lax.psum(squares_local, "tp")
    scale = lax.rsqrt(squares_total / D + EPSILON)
    logits = lax.psum(
        jnp.dot(gained * scale[:, None], router_f, precision=lax.Precision.HIGHEST), "tp"
    )
    moe_in = (gained * scale[:, None]).astype(jnp.bfloat16)
    chosen = jnp.take_along_axis(logits, routes, axis=1)
    gate_prob = jax.nn.softmax(chosen, axis=-1)
    gate_part = jnp.einsum("td,edf->tef", moe_in, expert_gate, preferred_element_type=jnp.float32)
    up_part = jnp.einsum("td,edf->tef", moe_in, expert_up, preferred_element_type=jnp.float32)
    gate_pick = jnp.take_along_axis(gate_part, routes[:, :, None], axis=1)
    up_pick = jnp.take_along_axis(up_part, routes[:, :, None], axis=1)
    gate_sum, up_sum = (
        lax.psum(gate_pick.astype(jnp.bfloat16), "tp").astype(jnp.float32),
        lax.psum(up_pick.astype(jnp.bfloat16), "tp").astype(jnp.float32),
    )
    activated = (jax.nn.silu(gate_sum) * up_sum).astype(jnp.bfloat16)
    scaled = (gate_prob[:, :, None] * activated.astype(jnp.float32)).astype(jnp.bfloat16)
    onehot = (routes[:, :, None] == jnp.arange(EXPERTS, dtype=jnp.int32)[None, None, :]).astype(
        jnp.bfloat16
    )
    spread = jnp.einsum("tke,tkf->tef", onehot, scaled, preferred_element_type=jnp.float32).astype(
        jnp.bfloat16
    )
    moe_part = jnp.einsum("tef,efd->td", spread, expert_down, preferred_element_type=jnp.float32)
    moe_out = lax.psum(moe_part, "seq")
    return (residual + moe_out).astype(jnp.bfloat16)


TOP = 8
TILE = 16
LANES = 128
SEQ = 8
TP = 4
MESH = pl.DeviceIdType.MESH
CHUNKS = 2
VMEM_LIMIT = 62 * 1024 * 1024
TURN = 6.28125
TURN_MIDDLE = 0.0019350051879882812
TURN_REST = 3.0199159819568123e-07


def fits_fused(mesh):
    return mesh.shape["seq"] == SEQ and mesh.shape["tp"] == TP


def lane_of(shape):
    return lax.broadcasted_iota(jnp.int32, shape, len(shape) - 1)


def swap_half(values):
    return pltpu.roll(values, 64, 1)


def split_pair(values):
    high = values.astype(jnp.bfloat16).astype(jnp.float32)
    return jnp.where(lane_of(values.shape) < 64, high, values - high).astype(jnp.bfloat16)


def join_pair(packed):
    values = packed.astype(jnp.float32)
    return values + swap_half(values)


def layer_kernel(
    tokens_hbm,
    attn_gain_hbm,
    moe_gain_hbm,
    lengths_hbm,
    routes_hbm,
    router_hbm,
    qkv_hbm,
    keys_hbm,
    values_hbm,
    out_w_hbm,
    gate_hbm,
    up_hbm,
    down_hbm,
    out_ref,
    tokens_ref,
    attn_gain_ref,
    moe_gain_ref,
    lengths_ref,
    routes_t_ref,
    router_ref,
    routes_ref,
    qkv_ref,
    keys_ref,
    values_ref,
    out_w_ref,
    down_ref,
    att_send,
    att_recv,
    att_all,
    res_own,
    res_all,
    pair_w,
    dense,
    onehot,
    shifted,
    picks,
    picks_recv,
    picks_half,
    picks_far,
    logit_rows,
    scaled,
    scaled_f,
    total,
    part_send,
    part_recv,
    out_own,
    local_sem,
    seq_send,
    seq_recv,
    tp_send,
    tp_recv,
):
    me = lax.axis_index("seq")
    tp = lax.axis_index("tp")
    core = lax.rem(tp, 2)
    core_peer = tp + 1 - 2 * core
    far_peer = lax.rem(tp + 2, TP)
    f32, bf16 = jnp.float32, jnp.bfloat16

    barrier = pltpu.get_barrier_semaphore()
    for step in range(1, SEQ):
        pl.semaphore_signal(
            barrier, inc=1, device_id=(lax.rem(me + step, SEQ), tp), device_id_type=MESH
        )
    for step in range(1, TP):
        pl.semaphore_signal(
            barrier, inc=1, device_id=(me, lax.rem(tp + step, TP)), device_id_type=MESH
        )

    depth = qkv_ref.shape[0] // 3
    hidden = gate_hbm.shape[1]
    wanted = [
        (lengths_hbm, lengths_ref),
        (tokens_hbm, tokens_ref),
        (attn_gain_hbm, attn_gain_ref),
        (qkv_hbm.at[0:depth], qkv_ref.at[0:depth]),
        (qkv_hbm.at[depth : 2 * depth], qkv_ref.at[depth : 2 * depth]),
        (qkv_hbm.at[2 * depth :], qkv_ref.at[2 * depth :]),
        (keys_hbm, keys_ref),
        (values_hbm, values_ref),
        (routes_hbm, routes_t_ref),
        (moe_gain_hbm, moe_gain_ref),
        (router_hbm, router_ref),
        (out_w_hbm, out_w_ref),
        (gate_hbm, pair_w.at[:, 0:hidden, :]),
        (up_hbm, pair_w.at[:, hidden:, :]),
        (down_hbm, down_ref),
    ]
    loads = [
        pltpu.make_async_copy(src, dst, local_sem.at[n]) for n, (src, dst) in enumerate(wanted)
    ]
    for load in loads[:8]:
        load.start()

    def seq_copies(phase, source, target):
        copies = []
        for step in range(1, SEQ):
            peer = lax.rem(me + step, SEQ)
            copies.append(
                pltpu.make_async_remote_copy(
                    src_ref=source(peer),
                    dst_ref=target(me),
                    send_sem=seq_send.at[phase, step],
                    recv_sem=seq_recv.at[phase, step],
                    device_id=(peer, tp),
                    device_id_type=MESH,
                )
            )
        for copy in copies:
            copy.start()
        return copies

    def tp_copy(slot, source, target, peer):
        copy = pltpu.make_async_remote_copy(
            src_ref=source,
            dst_ref=target,
            send_sem=tp_send.at[slot],
            recv_sem=tp_recv.at[slot],
            device_id=(me, peer),
            device_id_type=MESH,
        )
        copy.start()
        return copy

    def rows_of(index):
        return pl.ds(pl.multiple_of(index * TILE, TILE), TILE)

    loads[0].wait()
    request = lax.broadcasted_iota(jnp.int32, (128, 32), 0) // NEW
    picked = request == lane_of((128, 32))
    lens = jnp.sum(
        jnp.where(picked, lengths_ref[...].astype(f32), 0.0), axis=-1, keepdims=True
    )
    lane = lane_of((128, LANES))
    low = lane < 64
    token = lax.broadcasted_iota(jnp.int32, (128, LANES), 0)
    half = HEAD // 2
    table = np.exp(-np.log(np.float32(ROPE_BASE)) * np.arange(half, dtype=np.float32) / half)
    lane1 = lane_of((1, LANES)) % half
    freqs = jnp.zeros((1, LANES), f32)
    for n in range(half):
        freqs = jnp.where(lane1 == n, float(table[n]), freqs)
    angles = (lens + (token % NEW).astype(f32)) * freqs
    turns = jnp.floor(angles * (1.0 / (2 * np.pi)) + 0.5)
    angles = ((angles - turns * TURN) - turns * TURN_MIDDLE) - turns * TURN_REST
    cosine = jnp.cos(angles)
    sine = jnp.sin(angles)
    sine = jnp.where(lane % HEAD < half, -sine, sine)

    loads[1].wait()
    loads[2].wait()
    token_full = tokens_ref[...].astype(f32)
    normed = rms_scale(token_full, attn_gain_ref[...].reshape(1, -1)).astype(bf16)
    projected = jnp.zeros((128, qkv_ref.shape[1]), f32)
    for n in range(3):
        at = slice(depth * n, depth * (n + 1))
        loads[3 + n].wait()
        projected = projected + jnp.dot(normed[:, at], qkv_ref[at, :], preferred_element_type=f32)
    for load in loads[8:]:
        load.start()
    tiles = [projected[:, LANES * n : LANES * (n + 1)] for n in range(5)]

    def turned(x):
        swapped = jnp.where(lane % 64 < 32, pltpu.roll(x, 96, 1), pltpu.roll(x, 32, 1))
        return x * cosine + swapped * sine

    turn = [turned(x) for x in tiles]
    factor = 1.0 / HEAD**0.5
    queries = [
        jnp.where(low, turn[0], 0.0),
        jnp.where(low, swap_half(turn[0]), 0.0),
        jnp.where(low, turn[1], 0.0),
        jnp.where(low, 0.0, turn[2]),
        jnp.where(low, 0.0, swap_half(turn[3])),
        jnp.where(low, 0.0, turn[3]),
    ]
    queries = [(q * factor).astype(bf16) for q in queries]
    new_keys = jnp.where(low, swap_half(turn[1]), swap_half(turn[4])).astype(bf16)
    new_values = jnp.where(low, tiles[2], tiles[4]).astype(bf16)

    loads[6].wait()
    loads[7].wait()
    slot_count = keys_hbm.shape[0] // 32
    window = float(slot_count * SEQ - SINK)
    col256 = lane_of((32, 8 * slot_count))
    row256 = lax.broadcasted_iota(jnp.int32, (32, 8 * slot_count), 0)
    same = row256 // NEW == col256 // slot_count
    slot = (me * slot_count + col256 % slot_count).astype(f32)
    offset = (row256 % NEW).astype(f32)
    pl.semaphore_wait(barrier, SEQ + TP - 2)

    def send_part(peer):
        return pltpu.make_async_remote_copy(
            src_ref=att_send.at[TILE * peer : TILE * (peer + 1), :],
            dst_ref=att_recv.at[me],
            send_sem=seq_send.at[0, peer],
            recv_sem=seq_recv.at[0, me],
            device_id=(peer, tp),
            device_id_type=MESH,
        )

    row32 = lax.broadcasted_iota(jnp.int32, (32, 32), 0)
    col32 = lax.broadcasted_iota(jnp.int32, (32, 32), 1)
    own = (row32 // NEW == col32 // NEW) & (col32 <= row32) & (me == 0)
    own_bias = jnp.where(own, 0.0, FLOOR_SCORE).astype(f32)
    own_bias = jnp.concatenate([own_bias] * 6, axis=0)
    contract = (((1,), (1,)), ((), ()))
    for block in range(4):
        at = slice(32 * block, 32 * block + 32)
        slots = slice(256 * block, 256 * block + 256)
        query = jnp.concatenate([q[at] for q in queries], axis=0)
        last = lens[at] - 1.0
        back = last - slot
        older = last - (back - window * jnp.floor((back + 0.5) * (1.0 / window)))
        seen = (slot <= last) & ((slot < SINK) | (older > last + offset - window))
        old_bias = jnp.where(seen & same, 0.0, FLOOR_SCORE).astype(f32)
        old_bias = jnp.concatenate([old_bias] * 6, axis=0)
        old = lax.dot_general(query, keys_ref[slots, :], contract, preferred_element_type=f32)
        new = lax.dot_general(query, new_keys[at], contract, preferred_element_type=f32)
        old = old + old_bias
        new = new + own_bias
        top = jnp.maximum(
            jnp.max(old, axis=-1, keepdims=True), jnp.max(new, axis=-1, keepdims=True)
        )
        old = jnp.exp(old - top)
        new = jnp.exp(new - top)
        mass = jnp.sum(old, axis=-1, keepdims=True) + jnp.sum(new, axis=-1, keepdims=True)
        mixed = jnp.dot(
            old.astype(bf16), values_ref[slots, :], preferred_element_type=f32
        ) + jnp.dot(new.astype(bf16), new_values[at], preferred_element_type=f32)
        mixed = mixed / mass
        level = top + jnp.log(mass)
        head = [mixed[32 * n : 32 * n + 32] for n in range(6)]
        lane32 = lane_of((32, LANES))
        low32 = lane32 < 64
        att_send[at, 0:128] = jnp.where(low32, head[0], swap_half(head[1])).astype(bf16)
        att_send[at, 128:256] = jnp.where(low32, head[2], head[3]).astype(bf16)
        att_send[at, 256:384] = jnp.where(low32, swap_half(head[4]), head[5]).astype(bf16)
        levels = jnp.zeros((32, LANES), f32)
        for n in range(6):
            levels = jnp.where(lane32 % 8 == n, level[32 * n : 32 * n + 32], levels)
        high = levels.astype(bf16).astype(f32)
        rest = levels - high
        middle = rest.astype(bf16).astype(f32)
        levels = jnp.where(
            lane32 < 8, high, jnp.where(lane32 < 16, middle, rest - middle)
        )
        att_send[at, 384:512] = jnp.where(lane32 < 24, levels, 0.0).astype(bf16)

        for peer in (2 * block, 2 * block + 1):

            @pl.when(peer != me)
            def _(peer=peer):
                send_part(peer).start()

    att_recv[me] = att_send[rows_of(me), :]

    loads[8].wait()
    routes_ref[...] = jnp.transpose(
        jnp.concatenate([routes_t_ref[...], jnp.zeros((120, 128), jnp.int32)], axis=0)
    )
    spread_col = lax.broadcasted_iota(jnp.int32, (TILE, EXPERTS * TILE), 1)
    spread_row = lax.broadcasted_iota(jnp.int32, (TILE, EXPERTS * TILE), 0)
    expert_at = jnp.where(spread_col % TILE == spread_row, spread_col // TILE, -1)

    def mark(n, carry):
        routes = routes_ref[rows_of(n), 0:TOP]
        for k in range(TOP):
            hit = routes[:, k : k + 1] == expert_at
            onehot[n, TILE * k : TILE * (k + 1), :] = jnp.where(hit, 1.0, 0.0).astype(bf16)
        return carry

    lax.fori_loop(0, 8, mark, 0)
    half_lane = jnp.where(low, 0, 1)
    for k in range(TOP):
        shifted[k] = routes_ref[:, k : k + 1] - half_lane

    for step in range(1, SEQ):
        peer = lax.rem(me + step, SEQ)
        pltpu.make_async_remote_copy(
            src_ref=att_send.at[rows_of(peer), :],
            dst_ref=att_recv.at[peer],
            send_sem=seq_send.at[0, peer],
            recv_sem=seq_recv.at[0, peer],
            device_id=(peer, tp),
            device_id_type=MESH,
        ).wait()
    own_level = []
    for n in range(SEQ):
        packed = att_recv[n, :, 384:512].astype(f32)
        own_level.append(packed + pltpu.roll(packed, 120, 1) + pltpu.roll(packed, 112, 1))
    top = own_level[0]
    for n in range(1, SEQ):
        top = jnp.maximum(top, own_level[n])
    weights = [jnp.exp(x - top) for x in own_level]
    mass = weights[0]
    for n in range(1, SEQ):
        mass = mass + weights[n]
    low16 = lane_of((TILE, LANES)) < 64
    parts = [jnp.zeros((TILE, LANES), f32) for _ in range(3)]
    for n in range(SEQ):
        share = weights[n] / mass
        for j in range(3):
            wide = jnp.where(low16, share[:, 2 * j : 2 * j + 1], share[:, 2 * j + 1 : 2 * j + 2])
            parts[j] = parts[j] + wide * att_recv[n, :, 128 * j : 128 * j + 128].astype(f32)
    att_all[tp] = jnp.concatenate(parts, axis=-1).astype(bf16)

    copies = [
        tp_copy(step, att_all.at[tp], att_all.at[tp], lax.rem(tp + step, TP))
        for step in range(1, TP)
    ]
    loads[11].wait()
    width = out_w_ref.shape[1]
    residual = tokens_ref[rows_of(me), pl.ds(pl.multiple_of(tp * width, 128), width)].astype(f32)
    for copy in copies:
        copy.wait()
    for n in range(TP):
        residual = residual + jnp.dot(
            att_all[n], out_w_ref[width * n : width * (n + 1), :], preferred_element_type=f32
        )
    res_own[...] = residual
    res_all[me] = residual.astype(bf16)
    copies = seq_copies(1, lambda peer: res_all.at[me], lambda index: res_all.at[index])
    for copy in copies:
        copy.wait()

    full = res_all[...].reshape(SEQ * TILE, width).astype(f32)
    loads[9].wait()
    loads[10].wait()
    gained = full * moe_gain_ref[...].reshape(1, -1)
    gained_b = gained.astype(bf16)
    rest = (gained - gained_b.astype(f32)).astype(bf16)
    router = router_ref[...]
    logits = lax.dot_general(
        gained_b, router, contract, preferred_element_type=f32
    ) + lax.dot_general(rest, router, contract, preferred_element_type=f32)
    squares = jnp.sum(full * full, axis=-1, keepdims=True)
    logit_rows[...] = jnp.zeros_like(logit_rows)
    logit_rows[:, 0:EXPERTS] = logits
    rows = jnp.where(lane == EXPERTS, squares, logit_rows[...])
    rows = split_pair(jnp.where(low, rows, swap_half(rows)))
    picks[:, TOP * TILE :, :] = rows.reshape(8, TILE, LANES)

    loads[12].wait()
    loads[13].wait()

    def experts(n, carry):
        weight = pair_w[pl.ds(2 * n, 2)].reshape(2 * LANES, width)
        both = lax.dot_general(
            gained_b, weight, contract, preferred_element_type=f32
        ).astype(bf16)
        dense[2 * n] = both[:, :LANES]
        dense[2 * n + 1] = both[:, LANES:]
        return carry

    lax.fori_loop(0, EXPERTS // 2, experts, 0)

    def pick(n, carry):
        group = dense[:, rows_of(n), :].reshape(EXPERTS * TILE, LANES)
        picks[n, 0 : TOP * TILE, :] = jnp.dot(
            onehot[n], group, preferred_element_type=f32
        ).astype(bf16)
        return carry

    groups = 4 // CHUNKS
    count = groups * TILE
    near, far, back = [], [], []
    for chunk in range(CHUNKS):
        first = 4 * (1 - core) + groups * chunk
        lax.fori_loop(first, first + groups, pick, 0)
        at = slice(groups * chunk, groups * (chunk + 1))
        near.append(
            tp_copy(4 + chunk, picks.at[pl.ds(first, groups)], picks_recv.at[at], core_peer)
        )
    lax.fori_loop(4 * core, 4 * core + 4, pick, 0)
    for chunk in range(CHUNKS):
        at = slice(groups * chunk, groups * (chunk + 1))
        mine = pl.ds(4 * core + groups * chunk, groups)
        near[chunk].wait()
        picks_half[at, 0 : TOP * TILE, :] = (
            picks[mine, 0 : TOP * TILE, :].astype(f32)
            + picks_recv[at, 0 : TOP * TILE, :].astype(f32)
        ).astype(bf16)
        ours = picks[mine, TOP * TILE :, :].reshape(count, LANES)
        theirs = picks_recv[at, TOP * TILE :, :].reshape(count, LANES)
        picks_half[at, TOP * TILE :, :] = split_pair(join_pair(ours) + join_pair(theirs)).reshape(
            groups, TILE, LANES
        )
        far.append(
            tp_copy(4 + CHUNKS + chunk, picks_half.at[at], picks_far.at[at], far_peer)
        )
    lanes = lane_of((count, LANES))
    low_part = lanes < 64
    for chunk in range(CHUNKS):
        at = slice(groups * chunk, groups * (chunk + 1))
        mine = pl.ds(4 * core + groups * chunk, groups)
        far[chunk].wait()
        rows = join_pair(picks_half[at, TOP * TILE :, :].reshape(count, LANES)) + join_pair(
            picks_far[at, TOP * TILE :, :].reshape(count, LANES)
        )
        scale = lax.rsqrt(rows[:, EXPERTS : EXPERTS + 1] / D + EPSILON)
        start = pl.multiple_of(64 * core + count * chunk, count)
        routes = routes_ref[pl.ds(start, count), 0:TOP]
        hits = [lanes == routes[:, k : k + 1] for k in range(TOP)]
        routed = hits[0]
        for k in range(1, TOP):
            routed = routed | hits[k]
        scores = jnp.where(routed, rows * scale, FLOOR_SCORE)
        prob = jnp.exp(scores - jnp.max(scores, axis=-1, keepdims=True))
        prob = jnp.where(routed, prob, 0.0)
        prob = prob / jnp.sum(prob, axis=-1, keepdims=True)
        for k in range(TOP):
            of = slice(TILE * k, TILE * (k + 1))
            both = (picks_half[at, of, :].astype(f32) + picks_far[at, of, :].astype(f32)).reshape(
                count, LANES
            ) * scale
            active = both / (1.0 + jnp.exp(-both)) * swap_half(both)
            active = active.astype(bf16).astype(f32)
            active = active * jnp.sum(jnp.where(hits[k], prob, 0.0), axis=-1, keepdims=True)
            active = jnp.where(low_part, active, swap_half(active))
            scaled[mine, of, :] = active.astype(bf16).reshape(groups, TILE, LANES)
        back.append(
            tp_copy(4 + 2 * CHUNKS + chunk, scaled.at[mine], scaled.at[mine], core_peer)
        )
    loads[14].wait()
    for copy in back:
        copy.wait()

    for k in range(TOP):
        scaled_f[k] = scaled[:, TILE * k : TILE * (k + 1), :].reshape(128, LANES).astype(f32)
    total[...] = jnp.zeros_like(total)

    def down(n, carry):
        spread = []
        for pair in range(2):
            wanted = 4 * n + 2 * pair
            one = jnp.zeros((128, LANES), f32)
            for k in range(TOP):
                one = jnp.where(shifted[k] == wanted, scaled_f[k], one)
            spread.append(one)
        spread = jnp.concatenate(spread, axis=-1).astype(bf16)
        weight = down_ref[pl.ds(4 * n, 4)].reshape(256, width)
        total[...] += jnp.dot(spread, weight, preferred_element_type=f32)
        return carry

    lax.fori_loop(0, EXPERTS // 4, down, 0)
    part_send[...] = total[...].astype(bf16)

    copies = seq_copies(
        2, lambda peer: part_send.at[rows_of(peer), :], lambda index: part_recv.at[index]
    )
    result = res_own[...] + total[rows_of(me), :]
    for copy in copies:
        copy.wait()
    part_recv[me] = jnp.zeros((TILE, width), bf16)
    for n in range(SEQ):
        result = result + part_recv[n].astype(f32)
    out_own[...] = result.astype(bf16)
    out_ref[rows_of(me), :] = out_own[...]
    copies = seq_copies(3, lambda peer: out_own, lambda index: out_ref.at[rows_of(index), :])
    for copy in copies:
        copy.wait()


def fused_device(
    tokens,
    attn_gain,
    qkv_weight,
    out_weight,
    moe_gain,
    router_weight,
    expert_gate,
    expert_up,
    expert_down,
    cache_keys,
    cache_values,
    lengths,
    routes,
):
    count = tokens.shape[0]
    width = out_weight.shape[1]
    requests, slot_count = cache_keys.shape[:2]
    vmem = pl.BlockSpec(memory_space=pltpu.VMEM)
    hbm = pl.BlockSpec(memory_space=pltpu.HBM)
    bf16, f32 = jnp.bfloat16, jnp.float32
    hidden = expert_gate.shape[2]
    return pl.pallas_call(
        layer_kernel,
        out_shape=jax.ShapeDtypeStruct((count, width), bf16),
        in_specs=[hbm] * 13,
        out_specs=vmem,
        scratch_shapes=[
            pltpu.VMEM(tokens.shape, bf16),
            pltpu.VMEM((D,), f32),
            pltpu.VMEM((width,), f32),
            pltpu.VMEM((1, requests), jnp.int32),
            pltpu.VMEM((TOP, count), jnp.int32),
            pltpu.VMEM((EXPERTS, width), bf16),
            pltpu.VMEM((count, count), jnp.int32),
            pltpu.VMEM(qkv_weight.shape, bf16),
            pltpu.VMEM((requests * slot_count, LANES), bf16),
            pltpu.VMEM((requests * slot_count, LANES), bf16),
            pltpu.VMEM(out_weight.shape, bf16),
            pltpu.VMEM(expert_down.shape, bf16),
            pltpu.VMEM((count, 512), bf16),
            pltpu.VMEM((SEQ, TILE, 512), bf16),
            pltpu.VMEM((TP, TILE, width), bf16),
            pltpu.VMEM((TILE, width), f32),
            pltpu.VMEM((SEQ, TILE, width), bf16),
            pltpu.VMEM((EXPERTS, 2 * hidden, width), bf16),
            pltpu.VMEM((EXPERTS, count, LANES), bf16),
            pltpu.VMEM((8, TOP * TILE, EXPERTS * TILE), bf16),
            pltpu.VMEM((TOP, count, LANES), jnp.int32),
            pltpu.VMEM((8, (TOP + 1) * TILE, LANES), bf16),
            pltpu.VMEM((4, (TOP + 1) * TILE, LANES), bf16),
            pltpu.VMEM((4, (TOP + 1) * TILE, LANES), bf16),
            pltpu.VMEM((4, (TOP + 1) * TILE, LANES), bf16),
            pltpu.VMEM((count, LANES), f32),
            pltpu.VMEM((8, TOP * TILE, LANES), bf16),
            pltpu.VMEM((TOP, count, LANES), f32),
            pltpu.VMEM((count, width), f32),
            pltpu.VMEM((count, width), bf16),
            pltpu.VMEM((SEQ, TILE, width), bf16),
            pltpu.VMEM((TILE, width), bf16),
            pltpu.SemaphoreType.DMA((15,)),
            pltpu.SemaphoreType.DMA((4, SEQ)),
            pltpu.SemaphoreType.DMA((4, SEQ)),
            pltpu.SemaphoreType.DMA((4 + 3 * CHUNKS,)),
            pltpu.SemaphoreType.DMA((4 + 3 * CHUNKS,)),
        ],
        compiler_params=pltpu.CompilerParams(
            collective_id=0, has_side_effects=True, vmem_limit_bytes=VMEM_LIMIT
        ),
        cost_estimate=pl.CostEstimate(
            flops=2_000_000_000, bytes_accessed=20_000_000, transcendentals=1_000_000
        ),
        name="layer",
    )(
        tokens,
        attn_gain,
        moe_gain,
        lengths.reshape(1, -1),
        routes.T,
        router_weight.T,
        qkv_weight,
        cache_keys.reshape(-1, LANES),
        cache_values.reshape(-1, LANES),
        out_weight,
        jnp.swapaxes(expert_gate, 1, 2),
        jnp.swapaxes(expert_up, 1, 2),
        expert_down,
    )


def solution(mesh):
    in_specs = (
        P(),
        P(),
        P(None, "tp"),
        P(None, "tp"),
        P("tp"),
        P("tp", None),
        P(None, "tp", "seq"),
        P(None, "tp", "seq"),
        P(None, "seq", "tp"),
        P(None, "seq", "tp"),
        P(None, "seq", "tp"),
        P(),
        P(),
    )
    out_specs = P(None, "tp")
    body = fused_device if fits_fused(mesh) else on_device
    return jax.shard_map(
        body, mesh=mesh, in_specs=in_specs, out_specs=out_specs, check_vma=False
    )
```

```python
import jax
import jax.numpy as jnp
import numpy as np
from jax import lax
from jax.experimental import pallas as pl
from jax.experimental.pallas import tpu as pltpu
from jax.sharding import PartitionSpec as P

D = 1536
HEAD = 64
EXPERTS = 40
SINK = 4
NEW = 4
GROUP = 3


EPSILON = 1e-06
ROPE_BASE = 10000.0
FLOOR_SCORE = -1e30


def joined(shard, axis, combine):
    everything = jax.tree.map(lambda part: lax.all_gather(part, axis), shard)
    initial = jax.tree.map(lambda part: part[0], everything)

    def lap(k, so_far):
        return combine(so_far, jax.tree.map(lambda part: part[k], everything))

    return lax.fori_loop(1, lax.axis_size(axis), lap, initial)


def rms_scale(values, gain):
    return values * lax.rsqrt(jnp.mean(values * values, axis=-1, keepdims=True) + EPSILON) * gain


def rotate(values, places):
    half_dim = values.shape[-1] // 2
    freqs = jnp.exp(-jnp.log(ROPE_BASE) * jnp.arange(half_dim, dtype=jnp.float32) / half_dim)
    angles = places.reshape((-1,) + (1,) * (values.ndim - 1)) * freqs
    cosine = jnp.cos(angles)
    sine = jnp.sin(angles)
    first = values[..., :half_dim]
    second = values[..., half_dim:]
    return jnp.concatenate(
        [first * cosine - second * sine, first * sine + second * cosine], axis=-1
    )


def visible(slots, lengths, window):
    lens = lengths[:, None]
    slot_row = slots[None, :]
    live = slot_row < lens
    older = lens - 1 - jnp.mod(lens - 1 - slot_row, window)
    placed = jnp.where(slot_row < SINK, slot_row, older)
    offsets = jnp.arange(NEW, dtype=jnp.int32)
    inside = (slot_row[:, None, :] < SINK) | (
        placed[:, None, :] >= lens[:, :, None] + offsets[None, :, None] - window
    )
    return live[:, None, :] & inside


def combine_parts(earlier, later):
    top_a, mass_a, weighted_a = earlier
    top_b, mass_b, weighted_b = later
    top_both = jnp.maximum(top_a, top_b)
    factor_a = jnp.exp(top_a - top_both)
    factor_b = jnp.exp(top_b - top_both)
    return (
        top_both,
        mass_a * factor_a + mass_b * factor_b,
        weighted_a * factor_a[..., None] + weighted_b * factor_b[..., None],
    )


def on_device(
    tokens,
    attn_gain,
    qkv_weight,
    out_weight,
    moe_gain,
    router_weight,
    expert_gate,
    expert_up,
    expert_down,
    cache_keys,
    cache_values,
    lengths,
    routes,
):
    seq_count = lax.axis_size("seq")
    seq_index = lax.axis_index("seq")
    tp_index = lax.axis_index("tp")
    token_count = tokens.shape[0]
    requests = cache_keys.shape[0]
    slot_count = cache_keys.shape[1]
    window = slot_count * seq_count - SINK
    local_kv = cache_keys.shape[2] // HEAD
    token_full = tokens.astype(jnp.float32)
    normed = rms_scale(token_full, attn_gain).astype(jnp.bfloat16)
    projected = jnp.dot(normed, qkv_weight, preferred_element_type=jnp.float32)
    projected = projected.reshape(token_count, local_kv, GROUP + 2, HEAD)
    places = (
        (lengths[:, None] + jnp.arange(NEW, dtype=jnp.int32)[None, :])
        .reshape(token_count)
        .astype(jnp.float32)
    )
    queries = rotate(projected[:, :, :GROUP], places).astype(jnp.bfloat16)
    new_keys = rotate(projected[:, :, GROUP], places).astype(jnp.bfloat16)
    new_values = projected[:, :, GROUP + 1].astype(jnp.bfloat16)
    query_b = queries.reshape(requests, NEW, local_kv, GROUP, HEAD)
    key_new = new_keys.reshape(requests, NEW, local_kv, HEAD)
    value_new = new_values.reshape(requests, NEW, local_kv, HEAD)
    slots = seq_index * slot_count + jnp.arange(slot_count, dtype=jnp.int32)
    seen = visible(slots, lengths, window)[:, :, None, None, :]
    factor = 1.0 / HEAD**0.5
    key_old = cache_keys.reshape(requests, slot_count, local_kv, HEAD)
    value_old = cache_values.reshape(requests, slot_count, local_kv, HEAD)
    old_scores = (
        jnp.einsum("rtgqd,rsgd->rtgqs", query_b, key_old, preferred_element_type=jnp.float32)
        * factor
    )
    new_scores = (
        jnp.einsum("rtgqd,rugd->rtgqu", query_b, key_new, preferred_element_type=jnp.float32)
        * factor
    )
    causal = jnp.arange(NEW)[:, None] >= jnp.arange(NEW)[None, :]
    own_mask = causal[None, :, None, None, :] & (seq_index == 0)
    old_masked = jnp.where(seen, old_scores, FLOOR_SCORE)
    new_masked = jnp.where(own_mask, new_scores, FLOOR_SCORE)
    top_score = jnp.maximum(jnp.max(old_masked, axis=-1), jnp.max(new_masked, axis=-1))
    old_weights = jnp.where(seen, jnp.exp(old_masked - top_score[..., None]), 0.0)
    new_weights = jnp.where(own_mask, jnp.exp(new_masked - top_score[..., None]), 0.0)
    mass = jnp.sum(old_weights, axis=-1) + jnp.sum(new_weights, axis=-1)
    weighted = jnp.einsum(
        "rtgqs,rsgd->rtgqd", old_weights, value_old.astype(jnp.float32)
    ) + jnp.einsum("rtgqu,rugd->rtgqd", new_weights, value_new.astype(jnp.float32))
    top_score, mass, weighted = joined((top_score, mass, weighted), "seq", combine_parts)
    attended = (weighted / mass[..., None]).reshape(token_count, -1).astype(jnp.bfloat16)
    feature_part = out_weight.shape[1]
    attn_out = jnp.dot(
        lax.all_gather(attended, "tp", axis=1, tiled=True),
        out_weight,
        preferred_element_type=jnp.float32,
    )
    residual = (
        lax.dynamic_slice_in_dim(token_full, tp_index * feature_part, feature_part, 1) + attn_out
    )
    gained = residual * moe_gain
    squares_local = jnp.sum(residual * residual, axis=-1)
    router_f = router_weight.astype(jnp.float32)
    squares_total = lax.psum(squares_local, "tp")
    scale = lax.rsqrt(squares_total / D + EPSILON)
    logits = lax.psum(
        jnp.dot(gained * scale[:, None], router_f, precision=lax.Precision.HIGHEST), "tp"
    )
    moe_in = (gained * scale[:, None]).astype(jnp.bfloat16)
    chosen = jnp.take_along_axis(logits, routes, axis=1)
    gate_prob = jax.nn.softmax(chosen, axis=-1)
    gate_part = jnp.einsum("td,edf->tef", moe_in, expert_gate, preferred_element_type=jnp.float32)
    up_part = jnp.einsum("td,edf->tef", moe_in, expert_up, preferred_element_type=jnp.float32)
    gate_pick = jnp.take_along_axis(gate_part, routes[:, :, None], axis=1)
    up_pick = jnp.take_along_axis(up_part, routes[:, :, None], axis=1)
    gate_sum, up_sum = (
        lax.psum(gate_pick.astype(jnp.bfloat16), "tp").astype(jnp.float32),
        lax.psum(up_pick.astype(jnp.bfloat16), "tp").astype(jnp.float32),
    )
    activated = (jax.nn.silu(gate_sum) * up_sum).astype(jnp.bfloat16)
    scaled = (gate_prob[:, :, None] * activated.astype(jnp.float32)).astype(jnp.bfloat16)
    onehot = (routes[:, :, None] == jnp.arange(EXPERTS, dtype=jnp.int32)[None, None, :]).astype(
        jnp.bfloat16
    )
    spread = jnp.einsum("tke,tkf->tef", onehot, scaled, preferred_element_type=jnp.float32).astype(
        jnp.bfloat16
    )
    moe_part = jnp.einsum("tef,efd->td", spread, expert_down, preferred_element_type=jnp.float32)
    moe_out = lax.psum(moe_part, "seq")
    return (residual + moe_out).astype(jnp.bfloat16)


TOP = 8
TILE = 16
LANES = 128
SEQ = 8
TP = 4
MESH = pl.DeviceIdType.MESH
CHUNKS = 2
VMEM_LIMIT = 61 * 1024 * 1024
TURN = 6.28125
TURN_MIDDLE = 0.0019350051879882812
TURN_REST = 3.0199159819568123e-07


def fits_fused(mesh):
    return mesh.shape["seq"] == SEQ and mesh.shape["tp"] == TP


def lane_of(shape):
    return lax.broadcasted_iota(jnp.int32, shape, len(shape) - 1)


def swap_half(values):
    return pltpu.roll(values, 64, 1)


def split_pair(values):
    high = values.astype(jnp.bfloat16).astype(jnp.float32)
    return jnp.where(lane_of(values.shape) < 64, high, values - high).astype(jnp.bfloat16)


def join_pair(packed):
    values = packed.astype(jnp.float32)
    return values + swap_half(values)


def layer_kernel(
    tokens_hbm,
    attn_gain_hbm,
    moe_gain_hbm,
    lengths_hbm,
    routes_hbm,
    router_hbm,
    qkv_hbm,
    keys_hbm,
    values_hbm,
    out_w_hbm,
    gate_hbm,
    up_hbm,
    down_hbm,
    out_ref,
    tokens_ref,
    attn_gain_ref,
    moe_gain_ref,
    lengths_ref,
    routes_t_ref,
    router_ref,
    routes_ref,
    qkv_ref,
    keys_ref,
    values_ref,
    out_w_ref,
    down_ref,
    att_send,
    att_recv,
    att_all,
    res_own,
    res_all,
    pair_w,
    dense,
    onehot,
    shifted,
    picks,
    picks_recv,
    picks_half,
    picks_far,
    logit_rows,
    scaled,
    scaled_f,
    total,
    part_send,
    part_recv,
    out_own,
    local_sem,
    seq_send,
    seq_recv,
    tp_send,
    tp_recv,
):
    me = lax.axis_index("seq")
    tp = lax.axis_index("tp")
    core = lax.rem(tp, 2)
    core_peer = tp + 1 - 2 * core
    far_peer = lax.rem(tp + 2, TP)
    f32, bf16 = jnp.float32, jnp.bfloat16

    barrier = pltpu.get_barrier_semaphore()
    for step in range(1, SEQ):
        pl.semaphore_signal(
            barrier, inc=1, device_id=(lax.rem(me + step, SEQ), tp), device_id_type=MESH
        )
    for step in range(1, TP):
        pl.semaphore_signal(
            barrier, inc=1, device_id=(me, lax.rem(tp + step, TP)), device_id_type=MESH
        )

    depth = qkv_ref.shape[0] // 3
    hidden = gate_hbm.shape[1]
    wanted = [
        (lengths_hbm, lengths_ref),
        (tokens_hbm, tokens_ref),
        (attn_gain_hbm, attn_gain_ref),
        (qkv_hbm.at[0:depth], qkv_ref.at[0:depth]),
        (qkv_hbm.at[depth : 2 * depth], qkv_ref.at[depth : 2 * depth]),
        (qkv_hbm.at[2 * depth :], qkv_ref.at[2 * depth :]),
        (keys_hbm, keys_ref),
        (values_hbm, values_ref),
        (routes_hbm, routes_t_ref),
        (moe_gain_hbm, moe_gain_ref),
        (router_hbm, router_ref),
        (out_w_hbm, out_w_ref),
        (gate_hbm, pair_w.at[:, 0:hidden, :]),
        (up_hbm, pair_w.at[:, hidden:, :]),
        (down_hbm, down_ref),
    ]
    loads = [
        pltpu.make_async_copy(src, dst, local_sem.at[n]) for n, (src, dst) in enumerate(wanted)
    ]
    for load in loads[:8]:
        load.start()

    def seq_copies(phase, source, target):
        copies = []
        for step in range(1, SEQ):
            peer = lax.rem(me + step, SEQ)
            copies.append(
                pltpu.make_async_remote_copy(
                    src_ref=source(peer),
                    dst_ref=target(me),
                    send_sem=seq_send.at[phase, step],
                    recv_sem=seq_recv.at[phase, step],
                    device_id=(peer, tp),
                    device_id_type=MESH,
                )
            )
        for copy in copies:
            copy.start()
        return copies

    def tp_copy(slot, source, target, peer):
        copy = pltpu.make_async_remote_copy(
            src_ref=source,
            dst_ref=target,
            send_sem=tp_send.at[slot],
            recv_sem=tp_recv.at[slot],
            device_id=(me, peer),
            device_id_type=MESH,
        )
        copy.start()
        return copy

    def rows_of(index):
        return pl.ds(pl.multiple_of(index * TILE, TILE), TILE)

    loads[0].wait()
    request = lax.broadcasted_iota(jnp.int32, (128, 32), 0) // NEW
    picked = request == lane_of((128, 32))
    lens = jnp.sum(
        jnp.where(picked, lengths_ref[...].astype(f32), 0.0), axis=-1, keepdims=True
    )
    lane = lane_of((128, LANES))
    low = lane < 64
    token = lax.broadcasted_iota(jnp.int32, (128, LANES), 0)
    half = HEAD // 2
    table = np.exp(-np.log(np.float32(ROPE_BASE)) * np.arange(half, dtype=np.float32) / half)
    lane1 = lane_of((1, LANES)) % half
    freqs = jnp.zeros((1, LANES), f32)
    for n in range(half):
        freqs = jnp.where(lane1 == n, float(table[n]), freqs)
    angles = (lens + (token % NEW).astype(f32)) * freqs
    turns = jnp.floor(angles * (1.0 / (2 * np.pi)) + 0.5)
    angles = ((angles - turns * TURN) - turns * TURN_MIDDLE) - turns * TURN_REST
    cosine = jnp.cos(angles)
    sine = jnp.sin(angles)
    sine = jnp.where(lane % HEAD < half, -sine, sine)

    loads[1].wait()
    loads[2].wait()
    token_full = tokens_ref[...].astype(f32)
    normed = rms_scale(token_full, attn_gain_ref[...].reshape(1, -1)).astype(bf16)
    projected = jnp.zeros((128, qkv_ref.shape[1]), f32)
    for n in range(3):
        at = slice(depth * n, depth * (n + 1))
        loads[3 + n].wait()
        projected = projected + jnp.dot(normed[:, at], qkv_ref[at, :], preferred_element_type=f32)
    for load in loads[8:]:
        load.start()
    tiles = [projected[:, LANES * n : LANES * (n + 1)] for n in range(5)]

    def turned(x):
        swapped = jnp.where(lane % 64 < 32, pltpu.roll(x, 96, 1), pltpu.roll(x, 32, 1))
        return x * cosine + swapped * sine

    turn = [turned(x) for x in tiles]
    factor = 1.0 / HEAD**0.5
    queries = [
        jnp.where(low, turn[0], 0.0),
        jnp.where(low, swap_half(turn[0]), 0.0),
        jnp.where(low, turn[1], 0.0),
        jnp.where(low, 0.0, turn[2]),
        jnp.where(low, 0.0, swap_half(turn[3])),
        jnp.where(low, 0.0, turn[3]),
    ]
    queries = [(q * factor).astype(bf16) for q in queries]
    new_keys = jnp.where(low, swap_half(turn[1]), swap_half(turn[4])).astype(bf16)
    new_values = jnp.where(low, tiles[2], tiles[4]).astype(bf16)

    loads[6].wait()
    loads[7].wait()
    slot_count = keys_hbm.shape[0] // 32
    window = float(slot_count * SEQ - SINK)
    col256 = lane_of((32, 8 * slot_count))
    row256 = lax.broadcasted_iota(jnp.int32, (32, 8 * slot_count), 0)
    same = row256 // NEW == col256 // slot_count
    slot = (me * slot_count + col256 % slot_count).astype(f32)
    offset = (row256 % NEW).astype(f32)
    pl.semaphore_wait(barrier, SEQ + TP - 2)

    def send_part(peer):
        return pltpu.make_async_remote_copy(
            src_ref=att_send.at[TILE * peer : TILE * (peer + 1), :],
            dst_ref=att_recv.at[me],
            send_sem=seq_send.at[0, peer],
            recv_sem=seq_recv.at[0, me],
            device_id=(peer, tp),
            device_id_type=MESH,
        )

    row32 = lax.broadcasted_iota(jnp.int32, (32, 32), 0)
    col32 = lax.broadcasted_iota(jnp.int32, (32, 32), 1)
    own = (row32 // NEW == col32 // NEW) & (col32 <= row32) & (me == 0)
    own_bias = jnp.where(own, 0.0, FLOOR_SCORE).astype(f32)
    own_bias = jnp.concatenate([own_bias] * 6, axis=0)
    contract = (((1,), (1,)), ((), ()))
    for block in range(4):
        at = slice(32 * block, 32 * block + 32)
        slots = slice(256 * block, 256 * block + 256)
        query = jnp.concatenate([q[at] for q in queries], axis=0)
        last = lens[at] - 1.0
        back = last - slot
        older = last - (back - window * jnp.floor((back + 0.5) * (1.0 / window)))
        seen = (slot <= last) & ((slot < SINK) | (older > last + offset - window))
        old_bias = jnp.where(seen & same, 0.0, FLOOR_SCORE).astype(f32)
        old_bias = jnp.concatenate([old_bias] * 6, axis=0)
        old = lax.dot_general(query, keys_ref[slots, :], contract, preferred_element_type=f32)
        new = lax.dot_general(query, new_keys[at], contract, preferred_element_type=f32)
        old = old + old_bias
        new = new + own_bias
        top = jnp.maximum(
            jnp.max(old, axis=-1, keepdims=True), jnp.max(new, axis=-1, keepdims=True)
        )
        old = jnp.exp(old - top)
        new = jnp.exp(new - top)
        mass = jnp.sum(old, axis=-1, keepdims=True) + jnp.sum(new, axis=-1, keepdims=True)
        mixed = jnp.dot(
            old.astype(bf16), values_ref[slots, :], preferred_element_type=f32
        ) + jnp.dot(new.astype(bf16), new_values[at], preferred_element_type=f32)
        mixed = mixed / mass
        level = top + jnp.log(mass)
        head = [mixed[32 * n : 32 * n + 32] for n in range(6)]
        lane32 = lane_of((32, LANES))
        low32 = lane32 < 64
        att_send[at, 0:128] = jnp.where(low32, head[0], swap_half(head[1])).astype(bf16)
        att_send[at, 128:256] = jnp.where(low32, head[2], head[3]).astype(bf16)
        att_send[at, 256:384] = jnp.where(low32, swap_half(head[4]), head[5]).astype(bf16)
        levels = jnp.zeros((32, LANES), f32)
        for n in range(6):
            levels = jnp.where(lane32 % 8 == n, level[32 * n : 32 * n + 32], levels)
        high = levels.astype(bf16).astype(f32)
        rest = levels - high
        middle = rest.astype(bf16).astype(f32)
        levels = jnp.where(
            lane32 < 8, high, jnp.where(lane32 < 16, middle, rest - middle)
        )
        att_send[at, 384:512] = jnp.where(lane32 < 24, levels, 0.0).astype(bf16)

        for peer in (2 * block, 2 * block + 1):

            @pl.when(peer != me)
            def _(peer=peer):
                send_part(peer).start()

    att_recv[me] = att_send[rows_of(me), :]

    loads[8].wait()
    routes_ref[...] = jnp.transpose(
        jnp.concatenate([routes_t_ref[...], jnp.zeros((120, 128), jnp.int32)], axis=0)
    )
    spread_col = lax.broadcasted_iota(jnp.int32, (TILE, EXPERTS * TILE), 1)
    spread_row = lax.broadcasted_iota(jnp.int32, (TILE, EXPERTS * TILE), 0)
    expert_at = jnp.where(spread_col % TILE == spread_row, spread_col // TILE, -1)

    def mark(n, carry):
        routes = routes_ref[rows_of(n), 0:TOP]
        for k in range(TOP):
            hit = routes[:, k : k + 1] == expert_at
            onehot[n, TILE * k : TILE * (k + 1), :] = jnp.where(hit, 1.0, 0.0).astype(bf16)
        return carry

    lax.fori_loop(0, 8, mark, 0, unroll=2)
    half_lane = jnp.where(low, 0, 1)
    for k in range(TOP):
        shifted[k] = routes_ref[:, k : k + 1] - half_lane

    for step in range(1, SEQ):
        peer = lax.rem(me + step, SEQ)
        pltpu.make_async_remote_copy(
            src_ref=att_send.at[rows_of(peer), :],
            dst_ref=att_recv.at[peer],
            send_sem=seq_send.at[0, peer],
            recv_sem=seq_recv.at[0, peer],
            device_id=(peer, tp),
            device_id_type=MESH,
        ).wait()
    own_level = []
    for n in range(SEQ):
        packed = att_recv[n, :, 384:512].astype(f32)
        own_level.append(packed + pltpu.roll(packed, 120, 1) + pltpu.roll(packed, 112, 1))
    top = own_level[0]
    for n in range(1, SEQ):
        top = jnp.maximum(top, own_level[n])
    weights = [jnp.exp(x - top) for x in own_level]
    mass = weights[0]
    for n in range(1, SEQ):
        mass = mass + weights[n]
    low16 = lane_of((TILE, LANES)) < 64
    parts = [jnp.zeros((TILE, LANES), f32) for _ in range(3)]
    for n in range(SEQ):
        share = weights[n] / mass
        for j in range(3):
            wide = jnp.where(low16, share[:, 2 * j : 2 * j + 1], share[:, 2 * j + 1 : 2 * j + 2])
            parts[j] = parts[j] + wide * att_recv[n, :, 128 * j : 128 * j + 128].astype(f32)
    att_all[tp] = jnp.concatenate(parts, axis=-1).astype(bf16)

    copies = [
        tp_copy(step, att_all.at[tp], att_all.at[tp], lax.rem(tp + step, TP))
        for step in range(1, TP)
    ]
    loads[11].wait()
    width = out_w_ref.shape[1]
    residual = tokens_ref[rows_of(me), pl.ds(pl.multiple_of(tp * width, 128), width)].astype(f32)
    for copy in copies:
        copy.wait()
    for n in range(TP):
        residual = residual + jnp.dot(
            att_all[n], out_w_ref[width * n : width * (n + 1), :], preferred_element_type=f32
        )
    res_own[...] = residual
    res_all[me] = residual.astype(bf16)
    copies = seq_copies(1, lambda peer: res_all.at[me], lambda index: res_all.at[index])
    for copy in copies:
        copy.wait()

    full = res_all[...].reshape(SEQ * TILE, width).astype(f32)
    loads[9].wait()
    loads[10].wait()
    gained = full * moe_gain_ref[...].reshape(1, -1)
    gained_b = gained.astype(bf16)
    rest = (gained - gained_b.astype(f32)).astype(bf16)
    router = router_ref[...]
    logits = lax.dot_general(
        gained_b, router, contract, preferred_element_type=f32
    ) + lax.dot_general(rest, router, contract, preferred_element_type=f32)
    squares = jnp.sum(full * full, axis=-1, keepdims=True)
    logit_rows[...] = jnp.zeros_like(logit_rows)
    logit_rows[:, 0:EXPERTS] = logits
    rows = jnp.where(lane == EXPERTS, squares, logit_rows[...])
    rows = split_pair(jnp.where(low, rows, swap_half(rows)))
    picks[:, TOP * TILE :, :] = rows.reshape(8, TILE, LANES)

    loads[12].wait()
    loads[13].wait()

    def experts(n, carry):
        weight = pair_w[pl.ds(2 * n, 2)].reshape(2 * LANES, width)
        both = lax.dot_general(
            gained_b, weight, contract, preferred_element_type=f32
        ).astype(bf16)
        dense[2 * n] = both[:, :LANES]
        dense[2 * n + 1] = both[:, LANES:]
        return carry

    lax.fori_loop(0, EXPERTS // 2, experts, 0, unroll=5)

    def pick(n, carry):
        group = dense[:, rows_of(n), :].reshape(EXPERTS * TILE, LANES)
        picks[n, 0 : TOP * TILE, :] = jnp.dot(
            onehot[n], group, preferred_element_type=f32
        ).astype(bf16)
        return carry

    groups = 4 // CHUNKS
    count = groups * TILE
    near, far, back = [], [], []
    for chunk in range(CHUNKS):
        first = 4 * (1 - core) + groups * chunk
        for n in range(groups):
            pick(first + n, 0)
        at = slice(groups * chunk, groups * (chunk + 1))
        near.append(
            tp_copy(4 + chunk, picks.at[pl.ds(first, groups)], picks_recv.at[at], core_peer)
        )
    for n in range(4):
        pick(4 * core + n, 0)
    for chunk in range(CHUNKS):
        at = slice(groups * chunk, groups * (chunk + 1))
        mine = pl.ds(4 * core + groups * chunk, groups)
        near[chunk].wait()
        picks_half[at, 0 : TOP * TILE, :] = (
            picks[mine, 0 : TOP * TILE, :].astype(f32)
            + picks_recv[at, 0 : TOP * TILE, :].astype(f32)
        ).astype(bf16)
        ours = picks[mine, TOP * TILE :, :].reshape(count, LANES)
        theirs = picks_recv[at, TOP * TILE :, :].reshape(count, LANES)
        picks_half[at, TOP * TILE :, :] = split_pair(join_pair(ours) + join_pair(theirs)).reshape(
            groups, TILE, LANES
        )
        far.append(
            tp_copy(4 + CHUNKS + chunk, picks_half.at[at], picks_far.at[at], far_peer)
        )
    lanes = lane_of((count, LANES))
    low_part = lanes < 64
    for chunk in range(CHUNKS):
        at = slice(groups * chunk, groups * (chunk + 1))
        mine = pl.ds(4 * core + groups * chunk, groups)
        far[chunk].wait()
        rows = join_pair(picks_half[at, TOP * TILE :, :].reshape(count, LANES)) + join_pair(
            picks_far[at, TOP * TILE :, :].reshape(count, LANES)
        )
        scale = lax.rsqrt(rows[:, EXPERTS : EXPERTS + 1] / D + EPSILON)
        start = pl.multiple_of(64 * core + count * chunk, count)
        routes = routes_ref[pl.ds(start, count), 0:TOP]
        hits = [lanes == routes[:, k : k + 1] for k in range(TOP)]
        routed = hits[0]
        for k in range(1, TOP):
            routed = routed | hits[k]
        scores = jnp.where(routed, rows * scale, FLOOR_SCORE)
        prob = jnp.exp(scores - jnp.max(scores, axis=-1, keepdims=True))
        prob = jnp.where(routed, prob, 0.0)
        prob = prob / jnp.sum(prob, axis=-1, keepdims=True)
        for k in range(TOP):
            of = slice(TILE * k, TILE * (k + 1))
            both = (picks_half[at, of, :].astype(f32) + picks_far[at, of, :].astype(f32)).reshape(
                count, LANES
            ) * scale
            active = both / (1.0 + jnp.exp(-both)) * swap_half(both)
            active = active.astype(bf16).astype(f32)
            active = active * jnp.sum(jnp.where(hits[k], prob, 0.0), axis=-1, keepdims=True)
            active = jnp.where(low_part, active, swap_half(active))
            scaled[mine, of, :] = active.astype(bf16).reshape(groups, TILE, LANES)
        back.append(
            tp_copy(4 + 2 * CHUNKS + chunk, scaled.at[mine], scaled.at[mine], core_peer)
        )
    loads[14].wait()
    for copy in back:
        copy.wait()

    for k in range(TOP):
        scaled_f[k] = scaled[:, TILE * k : TILE * (k + 1), :].reshape(128, LANES).astype(f32)
    total[...] = jnp.zeros_like(total)

    def down(n, carry):
        spread = []
        for pair in range(2):
            wanted = 4 * n + 2 * pair
            one = jnp.zeros((128, LANES), f32)
            for k in range(TOP):
                one = jnp.where(shifted[k] == wanted, scaled_f[k], one)
            spread.append(one)
        spread = jnp.concatenate(spread, axis=-1).astype(bf16)
        weight = down_ref[pl.ds(4 * n, 4)].reshape(256, width)
        total[...] += jnp.dot(spread, weight, preferred_element_type=f32)
        return carry

    lax.fori_loop(0, EXPERTS // 4, down, 0, unroll=5)
    part_send[...] = total[...].astype(bf16)

    copies = seq_copies(
        2, lambda peer: part_send.at[rows_of(peer), :], lambda index: part_recv.at[index]
    )
    result = res_own[...] + total[rows_of(me), :]
    for copy in copies:
        copy.wait()
    part_recv[me] = jnp.zeros((TILE, width), bf16)
    for n in range(SEQ):
        result = result + part_recv[n].astype(f32)
    out_own[...] = result.astype(bf16)
    out_ref[rows_of(me), :] = out_own[...]
    copies = seq_copies(3, lambda peer: out_own, lambda index: out_ref.at[rows_of(index), :])
    for copy in copies:
        copy.wait()


def fused_device(
    tokens,
    attn_gain,
    qkv_weight,
    out_weight,
    moe_gain,
    router_weight,
    expert_gate,
    expert_up,
    expert_down,
    cache_keys,
    cache_values,
    lengths,
    routes,
):
    count = tokens.shape[0]
    width = out_weight.shape[1]
    requests, slot_count = cache_keys.shape[:2]
    vmem = pl.BlockSpec(memory_space=pltpu.VMEM)
    hbm = pl.BlockSpec(memory_space=pltpu.HBM)
    bf16, f32 = jnp.bfloat16, jnp.float32
    hidden = expert_gate.shape[2]
    return pl.pallas_call(
        layer_kernel,
        out_shape=pltpu.VMEM((count, width), bf16),
        in_specs=[hbm] * 13,
        out_specs=vmem,
        scratch_shapes=[
            pltpu.VMEM(tokens.shape, bf16),
            pltpu.VMEM((D,), f32),
            pltpu.VMEM((width,), f32),
            pltpu.VMEM((1, requests), jnp.int32),
            pltpu.VMEM((TOP, count), jnp.int32),
            pltpu.VMEM((EXPERTS, width), bf16),
            pltpu.VMEM((count, count), jnp.int32),
            pltpu.VMEM(qkv_weight.shape, bf16),
            pltpu.VMEM((requests * slot_count, LANES), bf16),
            pltpu.VMEM((requests * slot_count, LANES), bf16),
            pltpu.VMEM(out_weight.shape, bf16),
            pltpu.VMEM(expert_down.shape, bf16),
            pltpu.VMEM((count, 512), bf16),
            pltpu.VMEM((SEQ, TILE, 512), bf16),
            pltpu.VMEM((TP, TILE, width), bf16),
            pltpu.VMEM((TILE, width), f32),
            pltpu.VMEM((SEQ, TILE, width), bf16),
            pltpu.VMEM((EXPERTS, 2 * hidden, width), bf16),
            pltpu.VMEM((EXPERTS, count, LANES), bf16),
            pltpu.VMEM((8, TOP * TILE, EXPERTS * TILE), bf16),
            pltpu.VMEM((TOP, count, LANES), jnp.int32),
            pltpu.VMEM((8, (TOP + 1) * TILE, LANES), bf16),
            pltpu.VMEM((4, (TOP + 1) * TILE, LANES), bf16),
            pltpu.VMEM((4, (TOP + 1) * TILE, LANES), bf16),
            pltpu.VMEM((4, (TOP + 1) * TILE, LANES), bf16),
            pltpu.VMEM((count, LANES), f32),
            pltpu.VMEM((8, TOP * TILE, LANES), bf16),
            pltpu.VMEM((TOP, count, LANES), f32),
            pltpu.VMEM((count, width), f32),
            pltpu.VMEM((count, width), bf16),
            pltpu.VMEM((SEQ, TILE, width), bf16),
            pltpu.VMEM((TILE, width), bf16),
            pltpu.SemaphoreType.DMA((15,)),
            pltpu.SemaphoreType.DMA((4, SEQ)),
            pltpu.SemaphoreType.DMA((4, SEQ)),
            pltpu.SemaphoreType.DMA((4 + 3 * CHUNKS,)),
            pltpu.SemaphoreType.DMA((4 + 3 * CHUNKS,)),
        ],
        compiler_params=pltpu.CompilerParams(
            collective_id=0, has_side_effects=True, vmem_limit_bytes=VMEM_LIMIT
        ),
        cost_estimate=pl.CostEstimate(
            flops=2_000_000_000, bytes_accessed=20_000_000, transcendentals=1_000_000
        ),
        name="layer",
    )(
        tokens,
        attn_gain,
        moe_gain,
        lengths.reshape(1, -1),
        routes.T,
        router_weight.T,
        qkv_weight,
        cache_keys.reshape(-1, LANES),
        cache_values.reshape(-1, LANES),
        out_weight,
        jnp.swapaxes(expert_gate, 1, 2),
        jnp.swapaxes(expert_up, 1, 2),
        expert_down,
    )


def solution(mesh):
    in_specs = (
        P(),
        P(),
        P(None, "tp"),
        P(None, "tp"),
        P("tp"),
        P("tp", None),
        P(None, "tp", "seq"),
        P(None, "tp", "seq"),
        P(None, "seq", "tp"),
        P(None, "seq", "tp"),
        P(None, "seq", "tp"),
        P(),
        P(),
    )
    out_specs = P(None, "tp")
    body = fused_device if fits_fused(mesh) else on_device
    return jax.shard_map(
        body, mesh=mesh, in_specs=in_specs, out_specs=out_specs, check_vma=False
    )
```

```python
import jax
import jax.numpy as jnp
import numpy as np
from jax import lax
from jax.experimental import pallas as pl
from jax.experimental.pallas import tpu as pltpu
from jax.sharding import PartitionSpec as P

D = 1536
HEAD = 64
EXPERTS = 40
SINK = 4
NEW = 4
GROUP = 3


EPSILON = 1e-06
ROPE_BASE = 10000.0
FLOOR_SCORE = -1e30


def joined(shard, axis, combine):
    everything = jax.tree.map(lambda part: lax.all_gather(part, axis), shard)
    initial = jax.tree.map(lambda part: part[0], everything)

    def lap(k, so_far):
        return combine(so_far, jax.tree.map(lambda part: part[k], everything))

    return lax.fori_loop(1, lax.axis_size(axis), lap, initial)


def rms_scale(values, gain):
    return values * lax.rsqrt(jnp.mean(values * values, axis=-1, keepdims=True) + EPSILON) * gain


def rotate(values, places):
    half_dim = values.shape[-1] // 2
    freqs = jnp.exp(-jnp.log(ROPE_BASE) * jnp.arange(half_dim, dtype=jnp.float32) / half_dim)
    angles = places.reshape((-1,) + (1,) * (values.ndim - 1)) * freqs
    cosine = jnp.cos(angles)
    sine = jnp.sin(angles)
    first = values[..., :half_dim]
    second = values[..., half_dim:]
    return jnp.concatenate(
        [first * cosine - second * sine, first * sine + second * cosine], axis=-1
    )


def visible(slots, lengths, window):
    lens = lengths[:, None]
    slot_row = slots[None, :]
    live = slot_row < lens
    older = lens - 1 - jnp.mod(lens - 1 - slot_row, window)
    placed = jnp.where(slot_row < SINK, slot_row, older)
    offsets = jnp.arange(NEW, dtype=jnp.int32)
    inside = (slot_row[:, None, :] < SINK) | (
        placed[:, None, :] >= lens[:, :, None] + offsets[None, :, None] - window
    )
    return live[:, None, :] & inside


def combine_parts(earlier, later):
    top_a, mass_a, weighted_a = earlier
    top_b, mass_b, weighted_b = later
    top_both = jnp.maximum(top_a, top_b)
    factor_a = jnp.exp(top_a - top_both)
    factor_b = jnp.exp(top_b - top_both)
    return (
        top_both,
        mass_a * factor_a + mass_b * factor_b,
        weighted_a * factor_a[..., None] + weighted_b * factor_b[..., None],
    )


def on_device(
    tokens,
    attn_gain,
    qkv_weight,
    out_weight,
    moe_gain,
    router_weight,
    expert_gate,
    expert_up,
    expert_down,
    cache_keys,
    cache_values,
    lengths,
    routes,
):
    seq_count = lax.axis_size("seq")
    seq_index = lax.axis_index("seq")
    tp_index = lax.axis_index("tp")
    token_count = tokens.shape[0]
    requests = cache_keys.shape[0]
    slot_count = cache_keys.shape[1]
    window = slot_count * seq_count - SINK
    local_kv = cache_keys.shape[2] // HEAD
    token_full = tokens.astype(jnp.float32)
    normed = rms_scale(token_full, attn_gain).astype(jnp.bfloat16)
    projected = jnp.dot(normed, qkv_weight, preferred_element_type=jnp.float32)
    projected = projected.reshape(token_count, local_kv, GROUP + 2, HEAD)
    places = (
        (lengths[:, None] + jnp.arange(NEW, dtype=jnp.int32)[None, :])
        .reshape(token_count)
        .astype(jnp.float32)
    )
    queries = rotate(projected[:, :, :GROUP], places).astype(jnp.bfloat16)
    new_keys = rotate(projected[:, :, GROUP], places).astype(jnp.bfloat16)
    new_values = projected[:, :, GROUP + 1].astype(jnp.bfloat16)
    query_b = queries.reshape(requests, NEW, local_kv, GROUP, HEAD)
    key_new = new_keys.reshape(requests, NEW, local_kv, HEAD)
    value_new = new_values.reshape(requests, NEW, local_kv, HEAD)
    slots = seq_index * slot_count + jnp.arange(slot_count, dtype=jnp.int32)
    seen = visible(slots, lengths, window)[:, :, None, None, :]
    factor = 1.0 / HEAD**0.5
    key_old = cache_keys.reshape(requests, slot_count, local_kv, HEAD)
    value_old = cache_values.reshape(requests, slot_count, local_kv, HEAD)
    old_scores = (
        jnp.einsum("rtgqd,rsgd->rtgqs", query_b, key_old, preferred_element_type=jnp.float32)
        * factor
    )
    new_scores = (
        jnp.einsum("rtgqd,rugd->rtgqu", query_b, key_new, preferred_element_type=jnp.float32)
        * factor
    )
    causal = jnp.arange(NEW)[:, None] >= jnp.arange(NEW)[None, :]
    own_mask = causal[None, :, None, None, :] & (seq_index == 0)
    old_masked = jnp.where(seen, old_scores, FLOOR_SCORE)
    new_masked = jnp.where(own_mask, new_scores, FLOOR_SCORE)
    top_score = jnp.maximum(jnp.max(old_masked, axis=-1), jnp.max(new_masked, axis=-1))
    old_weights = jnp.where(seen, jnp.exp(old_masked - top_score[..., None]), 0.0)
    new_weights = jnp.where(own_mask, jnp.exp(new_masked - top_score[..., None]), 0.0)
    mass = jnp.sum(old_weights, axis=-1) + jnp.sum(new_weights, axis=-1)
    weighted = jnp.einsum(
        "rtgqs,rsgd->rtgqd", old_weights, value_old.astype(jnp.float32)
    ) + jnp.einsum("rtgqu,rugd->rtgqd", new_weights, value_new.astype(jnp.float32))
    top_score, mass, weighted = joined((top_score, mass, weighted), "seq", combine_parts)
    attended = (weighted / mass[..., None]).reshape(token_count, -1).astype(jnp.bfloat16)
    feature_part = out_weight.shape[1]
    attn_out = jnp.dot(
        lax.all_gather(attended, "tp", axis=1, tiled=True),
        out_weight,
        preferred_element_type=jnp.float32,
    )
    residual = (
        lax.dynamic_slice_in_dim(token_full, tp_index * feature_part, feature_part, 1) + attn_out
    )
    gained = residual * moe_gain
    squares_local = jnp.sum(residual * residual, axis=-1)
    router_f = router_weight.astype(jnp.float32)
    squares_total = lax.psum(squares_local, "tp")
    scale = lax.rsqrt(squares_total / D + EPSILON)
    logits = lax.psum(
        jnp.dot(gained * scale[:, None], router_f, precision=lax.Precision.HIGHEST), "tp"
    )
    moe_in = (gained * scale[:, None]).astype(jnp.bfloat16)
    chosen = jnp.take_along_axis(logits, routes, axis=1)
    gate_prob = jax.nn.softmax(chosen, axis=-1)
    gate_part = jnp.einsum("td,edf->tef", moe_in, expert_gate, preferred_element_type=jnp.float32)
    up_part = jnp.einsum("td,edf->tef", moe_in, expert_up, preferred_element_type=jnp.float32)
    gate_pick = jnp.take_along_axis(gate_part, routes[:, :, None], axis=1)
    up_pick = jnp.take_along_axis(up_part, routes[:, :, None], axis=1)
    gate_sum, up_sum = (
        lax.psum(gate_pick.astype(jnp.bfloat16), "tp").astype(jnp.float32),
        lax.psum(up_pick.astype(jnp.bfloat16), "tp").astype(jnp.float32),
    )
    activated = (jax.nn.silu(gate_sum) * up_sum).astype(jnp.bfloat16)
    scaled = (gate_prob[:, :, None] * activated.astype(jnp.float32)).astype(jnp.bfloat16)
    onehot = (routes[:, :, None] == jnp.arange(EXPERTS, dtype=jnp.int32)[None, None, :]).astype(
        jnp.bfloat16
    )
    spread = jnp.einsum("tke,tkf->tef", onehot, scaled, preferred_element_type=jnp.float32).astype(
        jnp.bfloat16
    )
    moe_part = jnp.einsum("tef,efd->td", spread, expert_down, preferred_element_type=jnp.float32)
    moe_out = lax.psum(moe_part, "seq")
    return (residual + moe_out).astype(jnp.bfloat16)


TOP = 8
TILE = 16
LANES = 128
SEQ = 8
TP = 4
MESH = pl.DeviceIdType.MESH
CHUNKS = 2
VMEM_LIMIT = 61 * 1024 * 1024
TURN = 6.28125
TURN_MIDDLE = 0.0019350051879882812
TURN_REST = 3.0199159819568123e-07


def fits_fused(mesh):
    return mesh.shape["seq"] == SEQ and mesh.shape["tp"] == TP


def lane_of(shape):
    return lax.broadcasted_iota(jnp.int32, shape, len(shape) - 1)


def swap_half(values):
    return pltpu.roll(values, 64, 1)


def split_pair(values):
    high = values.astype(jnp.bfloat16).astype(jnp.float32)
    return jnp.where(lane_of(values.shape) < 64, high, values - high).astype(jnp.bfloat16)


def join_pair(packed):
    values = packed.astype(jnp.float32)
    return values + swap_half(values)


def circle(angles):
    half = angles * 0.5
    square = half * half
    sine = jnp.full_like(square, 1.0 / 6227020800.0)
    cosine = jnp.full_like(square, -1.0 / 87178291200.0)
    for term in (-39916800.0, 362880.0, -5040.0, 120.0, -6.0, 1.0):
        sine = sine * square + 1.0 / term
    for term in (479001600.0, -3628800.0, 40320.0, -720.0, 24.0, -2.0, 1.0):
        cosine = cosine * square + 1.0 / term
    sine = sine * half
    return 1.0 - 2.0 * sine * sine, 2.0 * sine * cosine


def layer_kernel(
    tokens_hbm,
    attn_gain_hbm,
    moe_gain_hbm,
    lengths_hbm,
    routes_hbm,
    router_hbm,
    qkv_hbm,
    keys_hbm,
    values_hbm,
    out_w_hbm,
    gate_hbm,
    up_hbm,
    down_hbm,
    out_ref,
    tokens_ref,
    attn_gain_ref,
    moe_gain_ref,
    lengths_ref,
    routes_t_ref,
    router_ref,
    routes_ref,
    qkv_ref,
    keys_ref,
    values_ref,
    out_w_ref,
    down_ref,
    att_send,
    att_recv,
    att_all,
    res_own,
    res_all,
    pair_w,
    dense,
    onehot,
    shifted,
    picks,
    picks_recv,
    picks_half,
    picks_far,
    logit_rows,
    sums,
    sums_recv,
    sums_half,
    sums_far,
    gate_scale,
    scaled,
    spread,
    total,
    part_send,
    part_recv,
    out_own,
    local_sem,
    seq_send,
    seq_recv,
    tp_send,
    tp_recv,
):
    me = lax.axis_index("seq")
    tp = lax.axis_index("tp")
    core = lax.rem(tp, 2)
    core_peer = tp + 1 - 2 * core
    far_peer = lax.rem(tp + 2, TP)
    f32, bf16 = jnp.float32, jnp.bfloat16

    barrier = pltpu.get_barrier_semaphore()
    for step in range(1, SEQ):
        pl.semaphore_signal(
            barrier, inc=1, device_id=(lax.rem(me + step, SEQ), tp), device_id_type=MESH
        )
    for step in range(1, TP):
        pl.semaphore_signal(
            barrier, inc=1, device_id=(me, lax.rem(tp + step, TP)), device_id_type=MESH
        )

    depth = qkv_ref.shape[0] // 3
    hidden = gate_hbm.shape[1]
    wanted = [
        (lengths_hbm, lengths_ref),
        (tokens_hbm, tokens_ref),
        (attn_gain_hbm, attn_gain_ref),
        (qkv_hbm.at[0:depth], qkv_ref.at[0:depth]),
        (qkv_hbm.at[depth : 2 * depth], qkv_ref.at[depth : 2 * depth]),
        (qkv_hbm.at[2 * depth :], qkv_ref.at[2 * depth :]),
        (keys_hbm, keys_ref),
        (values_hbm, values_ref),
        (routes_hbm, routes_t_ref),
        (moe_gain_hbm, moe_gain_ref),
        (router_hbm, router_ref),
        (out_w_hbm, out_w_ref),
        (gate_hbm, pair_w.at[:, 0:hidden, :]),
        (up_hbm, pair_w.at[:, hidden:, :]),
        (down_hbm, down_ref),
    ]
    loads = [
        pltpu.make_async_copy(src, dst, local_sem.at[n]) for n, (src, dst) in enumerate(wanted)
    ]
    for load in loads[:8]:
        load.start()

    def seq_copies(phase, source, target):
        copies = []
        for step in range(1, SEQ):
            peer = lax.rem(me + step, SEQ)
            copies.append(
                pltpu.make_async_remote_copy(
                    src_ref=source(peer),
                    dst_ref=target(me),
                    send_sem=seq_send.at[phase, step],
                    recv_sem=seq_recv.at[phase, step],
                    device_id=(peer, tp),
                    device_id_type=MESH,
                )
            )
        for copy in copies:
            copy.start()
        return copies

    def tp_copy(slot, source, target, peer):
        copy = pltpu.make_async_remote_copy(
            src_ref=source,
            dst_ref=target,
            send_sem=tp_send.at[slot],
            recv_sem=tp_recv.at[slot],
            device_id=(me, peer),
            device_id_type=MESH,
        )
        copy.start()
        return copy

    def rows_of(index):
        return pl.ds(pl.multiple_of(index * TILE, TILE), TILE)

    loads[0].wait()
    request = lax.broadcasted_iota(jnp.int32, (128, 32), 0) // NEW
    picked = request == lane_of((128, 32))
    lens = jnp.sum(
        jnp.where(picked, lengths_ref[...].astype(f32), 0.0), axis=-1, keepdims=True
    )
    lane = lane_of((128, LANES))
    low = lane < 64
    token = lax.broadcasted_iota(jnp.int32, (128, LANES), 0)
    half = HEAD // 2
    table = np.exp(-np.log(np.float32(ROPE_BASE)) * np.arange(half, dtype=np.float32) / half)
    lane1 = lane_of((1, LANES)) % half
    freqs = jnp.zeros((1, LANES), f32)
    for n in range(half):
        freqs = jnp.where(lane1 == n, float(table[n]), freqs)
    angles = (lens + (token % NEW).astype(f32)) * freqs
    turns = jnp.floor(angles * (1.0 / (2 * np.pi)) + 0.5)
    angles = ((angles - turns * TURN) - turns * TURN_MIDDLE) - turns * TURN_REST
    cosine, sine = circle(angles)
    sine = jnp.where(lane % HEAD < half, -sine, sine)

    loads[1].wait()
    loads[2].wait()
    token_full = tokens_ref[...].astype(f32)
    normed = rms_scale(token_full, attn_gain_ref[...].reshape(1, -1)).astype(bf16)
    projected = jnp.zeros((128, qkv_ref.shape[1]), f32)
    for n in range(3):
        at = slice(depth * n, depth * (n + 1))
        loads[3 + n].wait()
        projected = projected + jnp.dot(normed[:, at], qkv_ref[at, :], preferred_element_type=f32)
    for load in loads[8:]:
        load.start()
    tiles = [projected[:, LANES * n : LANES * (n + 1)] for n in range(5)]

    def turned(x):
        swapped = jnp.where(lane % 64 < 32, pltpu.roll(x, 96, 1), pltpu.roll(x, 32, 1))
        return x * cosine + swapped * sine

    turn = [turned(x) for x in tiles]
    factor = 1.0 / HEAD**0.5
    queries = [
        jnp.where(low, turn[0], 0.0),
        jnp.where(low, swap_half(turn[0]), 0.0),
        jnp.where(low, turn[1], 0.0),
        jnp.where(low, 0.0, turn[2]),
        jnp.where(low, 0.0, swap_half(turn[3])),
        jnp.where(low, 0.0, turn[3]),
    ]
    queries = [(q * factor).astype(bf16) for q in queries]
    new_keys = jnp.where(low, swap_half(turn[1]), swap_half(turn[4])).astype(bf16)
    new_values = jnp.where(low, tiles[2], tiles[4]).astype(bf16)

    loads[6].wait()
    loads[7].wait()
    slot_count = keys_hbm.shape[0] // 32
    window = float(slot_count * SEQ - SINK)
    col256 = lane_of((32, 8 * slot_count))
    row256 = lax.broadcasted_iota(jnp.int32, (32, 8 * slot_count), 0)
    same = row256 // NEW == col256 // slot_count
    slot = (me * slot_count + col256 % slot_count).astype(f32)
    offset = (row256 % NEW).astype(f32)
    row32 = lax.broadcasted_iota(jnp.int32, (32, 32), 0)
    col32 = lax.broadcasted_iota(jnp.int32, (32, 32), 1)
    own = (row32 // NEW == col32 // NEW) & (col32 <= row32) & (me == 0)
    own_bias = jnp.where(own, 0.0, FLOOR_SCORE).astype(f32)
    own_bias = jnp.concatenate([own_bias] * 6, axis=0)
    contract = (((1,), (1,)), ((), ()))
    for block in range(4):
        at = slice(32 * block, 32 * block + 32)
        slots = slice(256 * block, 256 * block + 256)
        query = jnp.concatenate([q[at] for q in queries], axis=0)
        last = lens[at] - 1.0
        back = last - slot
        older = last - (back - window * jnp.floor((back + 0.5) * (1.0 / window)))
        seen = (slot <= last) & ((slot < SINK) | (older > last + offset - window))
        old_bias = jnp.where(seen & same, 0.0, FLOOR_SCORE).astype(f32)
        old_bias = jnp.concatenate([old_bias] * 6, axis=0)
        old = lax.dot_general(query, keys_ref[slots, :], contract, preferred_element_type=f32)
        new = lax.dot_general(query, new_keys[at], contract, preferred_element_type=f32)
        old = old + old_bias
        new = new + own_bias
        top = jnp.maximum(
            jnp.max(old, axis=-1, keepdims=True), jnp.max(new, axis=-1, keepdims=True)
        )
        old = jnp.exp(old - top)
        new = jnp.exp(new - top)
        mass = jnp.sum(old, axis=-1, keepdims=True) + jnp.sum(new, axis=-1, keepdims=True)
        mixed = jnp.dot(
            old.astype(bf16), values_ref[slots, :], preferred_element_type=f32
        ) + jnp.dot(new.astype(bf16), new_values[at], preferred_element_type=f32)
        mixed = mixed / mass
        level = top + jnp.log(mass)
        head = [mixed[32 * n : 32 * n + 32] for n in range(6)]
        lane32 = lane_of((32, LANES))
        low32 = lane32 < 64
        att_send[at, 0:128] = jnp.where(low32, head[0], swap_half(head[1])).astype(bf16)
        att_send[at, 128:256] = jnp.where(low32, head[2], head[3]).astype(bf16)
        att_send[at, 256:384] = jnp.where(low32, swap_half(head[4]), head[5]).astype(bf16)
        levels = jnp.zeros((32, LANES), f32)
        for n in range(6):
            levels = jnp.where(lane32 % 8 == n, level[32 * n : 32 * n + 32], levels)
        high = levels.astype(bf16).astype(f32)
        rest = levels - high
        middle = rest.astype(bf16).astype(f32)
        levels = jnp.where(
            lane32 < 8, high, jnp.where(lane32 < 16, middle, rest - middle)
        )
        att_send[at, 384:512] = jnp.where(lane32 < 24, levels, 0.0).astype(bf16)

    pl.semaphore_wait(barrier, SEQ + TP - 2)
    copies = seq_copies(
        0, lambda peer: att_send.at[rows_of(peer), :], lambda index: att_recv.at[index]
    )
    att_recv[me] = att_send[rows_of(me), :]

    loads[8].wait()
    routes_ref[...] = jnp.transpose(
        jnp.concatenate([routes_t_ref[...], jnp.zeros((120, 128), jnp.int32)], axis=0)
    )
    spread_col = lax.broadcasted_iota(jnp.int32, (TILE, EXPERTS * TILE), 1)
    spread_row = lax.broadcasted_iota(jnp.int32, (TILE, EXPERTS * TILE), 0)
    expert_at = jnp.where(spread_col % TILE == spread_row, spread_col // TILE, -1)

    def mark(n, carry):
        routes = routes_ref[rows_of(n), 0:TOP]
        for k in range(TOP):
            hit = routes[:, k : k + 1] == expert_at
            onehot[n, TILE * k : TILE * (k + 1), :] = jnp.where(hit, 1.0, 0.0).astype(bf16)
        return carry

    lax.fori_loop(0, 8, mark, 0, unroll=2)
    half_lane = jnp.where(low, 0, 1)
    for k in range(TOP):
        shifted[k] = routes_ref[:, k : k + 1] - half_lane

    for copy in copies:
        copy.wait()
    own_level = []
    for n in range(SEQ):
        packed = att_recv[n, :, 384:512].astype(f32)
        own_level.append(packed + pltpu.roll(packed, 120, 1) + pltpu.roll(packed, 112, 1))
    top = own_level[0]
    for n in range(1, SEQ):
        top = jnp.maximum(top, own_level[n])
    weights = [jnp.exp(x - top) for x in own_level]
    mass = weights[0]
    for n in range(1, SEQ):
        mass = mass + weights[n]
    low16 = lane_of((TILE, LANES)) < 64
    parts = [jnp.zeros((TILE, LANES), f32) for _ in range(3)]
    for n in range(SEQ):
        share = weights[n] / mass
        for j in range(3):
            wide = jnp.where(low16, share[:, 2 * j : 2 * j + 1], share[:, 2 * j + 1 : 2 * j + 2])
            parts[j] = parts[j] + wide * att_recv[n, :, 128 * j : 128 * j + 128].astype(f32)
    att_all[tp] = jnp.concatenate(parts, axis=-1).astype(bf16)

    copies = [
        tp_copy(step, att_all.at[tp], att_all.at[tp], lax.rem(tp + step, TP))
        for step in range(1, TP)
    ]
    loads[11].wait()
    width = out_w_ref.shape[1]
    residual = tokens_ref[rows_of(me), pl.ds(pl.multiple_of(tp * width, 128), width)].astype(f32)
    for copy in copies:
        copy.wait()
    for n in range(TP):
        residual = residual + jnp.dot(
            att_all[n], out_w_ref[width * n : width * (n + 1), :], preferred_element_type=f32
        )
    res_own[...] = residual
    res_all[me] = residual.astype(bf16)
    copies = seq_copies(1, lambda peer: res_all.at[me], lambda index: res_all.at[index])
    for copy in copies:
        copy.wait()

    full = res_all[...].reshape(SEQ * TILE, width).astype(f32)
    loads[9].wait()
    loads[10].wait()
    gained = full * moe_gain_ref[...].reshape(1, -1)
    gained_b = gained.astype(bf16)
    rest = (gained - gained_b.astype(f32)).astype(bf16)
    router = router_ref[...]
    logits = lax.dot_general(
        gained_b, router, contract, preferred_element_type=f32
    ) + lax.dot_general(rest, router, contract, preferred_element_type=f32)
    squares = jnp.sum(full * full, axis=-1, keepdims=True)
    logit_rows[...] = jnp.zeros_like(logit_rows)
    logit_rows[:, 0:EXPERTS] = logits
    rows = jnp.where(lane == EXPERTS, squares, logit_rows[...])
    rows = split_pair(jnp.where(low, rows, swap_half(rows)))
    sums[...] = rows
    sums_copy = tp_copy(
        4 + 3 * CHUNKS,
        sums.at[pl.ds(pl.multiple_of(64 * (1 - core), 64), 64), :],
        sums_recv,
        core_peer,
    )

    loads[12].wait()
    loads[13].wait()

    def experts(n, carry):
        weight = pair_w[pl.ds(2 * n, 2)].reshape(2 * LANES, width)
        both = lax.dot_general(
            gained_b, weight, contract, preferred_element_type=f32
        ).astype(bf16)
        dense[2 * n] = both[:, :LANES]
        dense[2 * n + 1] = both[:, LANES:]
        return carry

    lax.fori_loop(0, EXPERTS // 2, experts, 0, unroll=10)

    def pick(n, carry):
        group = dense[:, rows_of(n), :].reshape(EXPERTS * TILE, LANES)
        picks[n, 0 : TOP * TILE, :] = jnp.dot(
            onehot[n], group, preferred_element_type=f32
        ).astype(bf16)
        return carry

    groups = 4 // CHUNKS
    count = groups * TILE
    near, far, back = [], [], []
    for chunk in range(CHUNKS):
        first = 4 * (1 - core) + groups * chunk
        for n in range(groups):
            pick(first + n, 0)
        at = slice(groups * chunk, groups * (chunk + 1))
        near.append(
            tp_copy(4 + chunk, picks.at[pl.ds(first, groups)], picks_recv.at[at], core_peer)
        )
    for n in range(4):
        pick(4 * core + n, 0)
    sums_copy.wait()
    ours = pl.ds(pl.multiple_of(64 * core, 64), 64)
    sums_half[...] = split_pair(join_pair(sums[ours, :]) + join_pair(sums_recv[...]))
    sums_copy = tp_copy(5 + 3 * CHUNKS, sums_half, sums_far, far_peer)
    for chunk in range(CHUNKS):
        at = slice(groups * chunk, groups * (chunk + 1))
        mine = pl.ds(4 * core + groups * chunk, groups)
        near[chunk].wait()
        picks_half[at] = (picks[mine].astype(f32) + picks_recv[at].astype(f32)).astype(bf16)
        far.append(
            tp_copy(4 + CHUNKS + chunk, picks_half.at[at], picks_far.at[at], far_peer)
        )

    sums_copy.wait()
    rows = join_pair(sums_half[...]) + join_pair(sums_far[...])
    lanes = lane_of((64, LANES))
    scales = lax.rsqrt(rows[:, EXPERTS : EXPERTS + 1] / D + EPSILON)
    routes = routes_ref[ours, 0:TOP]
    hits = [lanes == routes[:, k : k + 1] for k in range(TOP)]
    routed = hits[0]
    for k in range(1, TOP):
        routed = routed | hits[k]
    scores = jnp.where(routed, rows * scales, FLOOR_SCORE)
    prob = jnp.exp(scores - jnp.max(scores, axis=-1, keepdims=True))
    prob = jnp.where(routed, prob, 0.0)
    prob = prob / jnp.sum(prob, axis=-1, keepdims=True)
    probs = [jnp.sum(jnp.where(hits[k], prob, 0.0), axis=-1, keepdims=True) for k in range(TOP)]
    for k in range(TOP):
        gate_scale[k] = jnp.broadcast_to(probs[k], (64, LANES))
    gate_scale[TOP] = jnp.broadcast_to(scales, (64, LANES))
    low_part = lane_of((count, LANES)) < 64
    for chunk in range(CHUNKS):
        at = slice(groups * chunk, groups * (chunk + 1))
        mine = pl.ds(4 * core + groups * chunk, groups)
        part = slice(count * chunk, count * (chunk + 1))
        far[chunk].wait()
        scale = gate_scale[TOP, part, :]
        for k in range(TOP):
            of = slice(TILE * k, TILE * (k + 1))
            both = (picks_half[at, of, :].astype(f32) + picks_far[at, of, :].astype(f32)).reshape(
                count, LANES
            ) * scale
            active = both / (1.0 + jnp.exp(-both)) * swap_half(both)
            active = active.astype(bf16).astype(f32) * gate_scale[k, part, :]
            active = jnp.where(low_part, active, swap_half(active))
            scaled[mine, of, :] = active.astype(bf16).reshape(groups, TILE, LANES)
        back.append(
            tp_copy(4 + 2 * CHUNKS + chunk, scaled.at[mine], scaled.at[mine], core_peer)
        )

    def spread_rows(n):
        values = [
            scaled[n, TILE * k : TILE * (k + 1), :].astype(f32) for k in range(TOP)
        ]
        routes = [shifted[k, rows_of(n), :] for k in range(TOP)]
        for pair in range(EXPERTS // 2):
            one = jnp.zeros((TILE, LANES), f32)
            for k in range(TOP):
                one = jnp.where(routes[k] == 2 * pair, values[k], one)
            spread[rows_of(n), LANES * pair : LANES * (pair + 1)] = one.astype(bf16)

    for n in range(4):
        spread_rows(4 * core + n)
    loads[14].wait()
    for chunk in range(CHUNKS):
        back[chunk].wait()
        for n in range(groups):
            spread_rows(4 * (1 - core) + groups * chunk + n)
    total[...] = jnp.dot(
        spread[...], down_ref[...].reshape(EXPERTS * hidden, width), preferred_element_type=f32
    )
    part_send[...] = total[...].astype(bf16)

    copies = seq_copies(
        2, lambda peer: part_send.at[rows_of(peer), :], lambda index: part_recv.at[index]
    )
    result = res_own[...] + total[rows_of(me), :]
    for copy in copies:
        copy.wait()
    part_recv[me] = jnp.zeros((TILE, width), bf16)
    for n in range(SEQ):
        result = result + part_recv[n].astype(f32)
    out_own[...] = result.astype(bf16)
    out_ref[rows_of(me), :] = out_own[...]
    copies = seq_copies(3, lambda peer: out_own, lambda index: out_ref.at[rows_of(index), :])
    for copy in copies:
        copy.wait()


def fused_device(
    tokens,
    attn_gain,
    qkv_weight,
    out_weight,
    moe_gain,
    router_weight,
    expert_gate,
    expert_up,
    expert_down,
    cache_keys,
    cache_values,
    lengths,
    routes,
):
    count = tokens.shape[0]
    width = out_weight.shape[1]
    requests, slot_count = cache_keys.shape[:2]
    vmem = pl.BlockSpec(memory_space=pltpu.VMEM)
    hbm = pl.BlockSpec(memory_space=pltpu.HBM)
    bf16, f32 = jnp.bfloat16, jnp.float32
    hidden = expert_gate.shape[2]
    return pl.pallas_call(
        layer_kernel,
        out_shape=pltpu.VMEM((count, width), bf16),
        in_specs=[hbm] * 13,
        out_specs=vmem,
        scratch_shapes=[
            pltpu.VMEM(tokens.shape, bf16),
            pltpu.VMEM((D,), f32),
            pltpu.VMEM((width,), f32),
            pltpu.VMEM((1, requests), jnp.int32),
            pltpu.VMEM((TOP, count), jnp.int32),
            pltpu.VMEM((EXPERTS, width), bf16),
            pltpu.VMEM((count, count), jnp.int32),
            pltpu.VMEM(qkv_weight.shape, bf16),
            pltpu.VMEM((requests * slot_count, LANES), bf16),
            pltpu.VMEM((requests * slot_count, LANES), bf16),
            pltpu.VMEM(out_weight.shape, bf16),
            pltpu.VMEM(expert_down.shape, bf16),
            pltpu.VMEM((count, 512), bf16),
            pltpu.VMEM((SEQ, TILE, 512), bf16),
            pltpu.VMEM((TP, TILE, width), bf16),
            pltpu.VMEM((TILE, width), f32),
            pltpu.VMEM((SEQ, TILE, width), bf16),
            pltpu.VMEM((EXPERTS, 2 * hidden, width), bf16),
            pltpu.VMEM((EXPERTS, count, LANES), bf16),
            pltpu.VMEM((8, TOP * TILE, EXPERTS * TILE), bf16),
            pltpu.VMEM((TOP, count, LANES), jnp.int32),
            pltpu.VMEM((8, TOP * TILE, LANES), bf16),
            pltpu.VMEM((4, TOP * TILE, LANES), bf16),
            pltpu.VMEM((4, TOP * TILE, LANES), bf16),
            pltpu.VMEM((4, TOP * TILE, LANES), bf16),
            pltpu.VMEM((count, LANES), f32),
            pltpu.VMEM((count, LANES), bf16),
            pltpu.VMEM((64, LANES), bf16),
            pltpu.VMEM((64, LANES), bf16),
            pltpu.VMEM((64, LANES), bf16),
            pltpu.VMEM((TOP + 1, 64, LANES), f32),
            pltpu.VMEM((8, TOP * TILE, LANES), bf16),
            pltpu.VMEM((count, EXPERTS * hidden), bf16),
            pltpu.VMEM((count, width), f32),
            pltpu.VMEM((count, width), bf16),
            pltpu.VMEM((SEQ, TILE, width), bf16),
            pltpu.VMEM((TILE, width), bf16),
            pltpu.SemaphoreType.DMA((15,)),
            pltpu.SemaphoreType.DMA((4, SEQ)),
            pltpu.SemaphoreType.DMA((4, SEQ)),
            pltpu.SemaphoreType.DMA((6 + 3 * CHUNKS,)),
            pltpu.SemaphoreType.DMA((6 + 3 * CHUNKS,)),
        ],
        compiler_params=pltpu.CompilerParams(
            collective_id=0, has_side_effects=True, vmem_limit_bytes=VMEM_LIMIT
        ),
        cost_estimate=pl.CostEstimate(
            flops=2_000_000_000, bytes_accessed=20_000_000, transcendentals=1_000_000
        ),
        name="layer",
    )(
        tokens,
        attn_gain,
        moe_gain,
        lengths.reshape(1, -1),
        routes.T,
        router_weight.T,
        qkv_weight,
        cache_keys.reshape(-1, LANES),
        cache_values.reshape(-1, LANES),
        out_weight,
        jnp.swapaxes(expert_gate, 1, 2),
        jnp.swapaxes(expert_up, 1, 2),
        expert_down,
    )


def solution(mesh):
    in_specs = (
        P(),
        P(),
        P(None, "tp"),
        P(None, "tp"),
        P("tp"),
        P("tp", None),
        P(None, "tp", "seq"),
        P(None, "tp", "seq"),
        P(None, "seq", "tp"),
        P(None, "seq", "tp"),
        P(None, "seq", "tp"),
        P(),
        P(),
    )
    out_specs = P(None, "tp")
    body = fused_device if fits_fused(mesh) else on_device
    return jax.shard_map(
        body, mesh=mesh, in_specs=in_specs, out_specs=out_specs, check_vma=False
    )
```

```python
import jax
import jax.numpy as jnp
import numpy as np
from jax import lax
from jax.experimental import pallas as pl
from jax.experimental.pallas import tpu as pltpu
from jax.sharding import PartitionSpec as P

D = 1536
HEAD = 64
EXPERTS = 40
SINK = 4
NEW = 4
GROUP = 3


EPSILON = 1e-06
ROPE_BASE = 10000.0
FLOOR_SCORE = -1e30


def joined(shard, axis, combine):
    everything = jax.tree.map(lambda part: lax.all_gather(part, axis), shard)
    initial = jax.tree.map(lambda part: part[0], everything)

    def lap(k, so_far):
        return combine(so_far, jax.tree.map(lambda part: part[k], everything))

    return lax.fori_loop(1, lax.axis_size(axis), lap, initial)


def rms_scale(values, gain):
    return values * lax.rsqrt(jnp.mean(values * values, axis=-1, keepdims=True) + EPSILON) * gain


def rotate(values, places):
    half_dim = values.shape[-1] // 2
    freqs = jnp.exp(-jnp.log(ROPE_BASE) * jnp.arange(half_dim, dtype=jnp.float32) / half_dim)
    angles = places.reshape((-1,) + (1,) * (values.ndim - 1)) * freqs
    cosine = jnp.cos(angles)
    sine = jnp.sin(angles)
    first = values[..., :half_dim]
    second = values[..., half_dim:]
    return jnp.concatenate(
        [first * cosine - second * sine, first * sine + second * cosine], axis=-1
    )


def visible(slots, lengths, window):
    lens = lengths[:, None]
    slot_row = slots[None, :]
    live = slot_row < lens
    older = lens - 1 - jnp.mod(lens - 1 - slot_row, window)
    placed = jnp.where(slot_row < SINK, slot_row, older)
    offsets = jnp.arange(NEW, dtype=jnp.int32)
    inside = (slot_row[:, None, :] < SINK) | (
        placed[:, None, :] >= lens[:, :, None] + offsets[None, :, None] - window
    )
    return live[:, None, :] & inside


def combine_parts(earlier, later):
    top_a, mass_a, weighted_a = earlier
    top_b, mass_b, weighted_b = later
    top_both = jnp.maximum(top_a, top_b)
    factor_a = jnp.exp(top_a - top_both)
    factor_b = jnp.exp(top_b - top_both)
    return (
        top_both,
        mass_a * factor_a + mass_b * factor_b,
        weighted_a * factor_a[..., None] + weighted_b * factor_b[..., None],
    )


def on_device(
    tokens,
    attn_gain,
    qkv_weight,
    out_weight,
    moe_gain,
    router_weight,
    expert_gate,
    expert_up,
    expert_down,
    cache_keys,
    cache_values,
    lengths,
    routes,
):
    seq_count = lax.axis_size("seq")
    seq_index = lax.axis_index("seq")
    tp_index = lax.axis_index("tp")
    token_count = tokens.shape[0]
    requests = cache_keys.shape[0]
    slot_count = cache_keys.shape[1]
    window = slot_count * seq_count - SINK
    local_kv = cache_keys.shape[2] // HEAD
    token_full = tokens.astype(jnp.float32)
    normed = rms_scale(token_full, attn_gain).astype(jnp.bfloat16)
    projected = jnp.dot(normed, qkv_weight, preferred_element_type=jnp.float32)
    projected = projected.reshape(token_count, local_kv, GROUP + 2, HEAD)
    places = (
        (lengths[:, None] + jnp.arange(NEW, dtype=jnp.int32)[None, :])
        .reshape(token_count)
        .astype(jnp.float32)
    )
    queries = rotate(projected[:, :, :GROUP], places).astype(jnp.bfloat16)
    new_keys = rotate(projected[:, :, GROUP], places).astype(jnp.bfloat16)
    new_values = projected[:, :, GROUP + 1].astype(jnp.bfloat16)
    query_b = queries.reshape(requests, NEW, local_kv, GROUP, HEAD)
    key_new = new_keys.reshape(requests, NEW, local_kv, HEAD)
    value_new = new_values.reshape(requests, NEW, local_kv, HEAD)
    slots = seq_index * slot_count + jnp.arange(slot_count, dtype=jnp.int32)
    seen = visible(slots, lengths, window)[:, :, None, None, :]
    factor = 1.0 / HEAD**0.5
    key_old = cache_keys.reshape(requests, slot_count, local_kv, HEAD)
    value_old = cache_values.reshape(requests, slot_count, local_kv, HEAD)
    old_scores = (
        jnp.einsum("rtgqd,rsgd->rtgqs", query_b, key_old, preferred_element_type=jnp.float32)
        * factor
    )
    new_scores = (
        jnp.einsum("rtgqd,rugd->rtgqu", query_b, key_new, preferred_element_type=jnp.float32)
        * factor
    )
    causal = jnp.arange(NEW)[:, None] >= jnp.arange(NEW)[None, :]
    own_mask = causal[None, :, None, None, :] & (seq_index == 0)
    old_masked = jnp.where(seen, old_scores, FLOOR_SCORE)
    new_masked = jnp.where(own_mask, new_scores, FLOOR_SCORE)
    top_score = jnp.maximum(jnp.max(old_masked, axis=-1), jnp.max(new_masked, axis=-1))
    old_weights = jnp.where(seen, jnp.exp(old_masked - top_score[..., None]), 0.0)
    new_weights = jnp.where(own_mask, jnp.exp(new_masked - top_score[..., None]), 0.0)
    mass = jnp.sum(old_weights, axis=-1) + jnp.sum(new_weights, axis=-1)
    weighted = jnp.einsum(
        "rtgqs,rsgd->rtgqd", old_weights, value_old.astype(jnp.float32)
    ) + jnp.einsum("rtgqu,rugd->rtgqd", new_weights, value_new.astype(jnp.float32))
    top_score, mass, weighted = joined((top_score, mass, weighted), "seq", combine_parts)
    attended = (weighted / mass[..., None]).reshape(token_count, -1).astype(jnp.bfloat16)
    feature_part = out_weight.shape[1]
    attn_out = jnp.dot(
        lax.all_gather(attended, "tp", axis=1, tiled=True),
        out_weight,
        preferred_element_type=jnp.float32,
    )
    residual = (
        lax.dynamic_slice_in_dim(token_full, tp_index * feature_part, feature_part, 1) + attn_out
    )
    gained = residual * moe_gain
    squares_local = jnp.sum(residual * residual, axis=-1)
    router_f = router_weight.astype(jnp.float32)
    squares_total = lax.psum(squares_local, "tp")
    scale = lax.rsqrt(squares_total / D + EPSILON)
    logits = lax.psum(
        jnp.dot(gained * scale[:, None], router_f, precision=lax.Precision.HIGHEST), "tp"
    )
    moe_in = (gained * scale[:, None]).astype(jnp.bfloat16)
    chosen = jnp.take_along_axis(logits, routes, axis=1)
    gate_prob = jax.nn.softmax(chosen, axis=-1)
    gate_part = jnp.einsum("td,edf->tef", moe_in, expert_gate, preferred_element_type=jnp.float32)
    up_part = jnp.einsum("td,edf->tef", moe_in, expert_up, preferred_element_type=jnp.float32)
    gate_pick = jnp.take_along_axis(gate_part, routes[:, :, None], axis=1)
    up_pick = jnp.take_along_axis(up_part, routes[:, :, None], axis=1)
    gate_sum, up_sum = (
        lax.psum(gate_pick.astype(jnp.bfloat16), "tp").astype(jnp.float32),
        lax.psum(up_pick.astype(jnp.bfloat16), "tp").astype(jnp.float32),
    )
    activated = (jax.nn.silu(gate_sum) * up_sum).astype(jnp.bfloat16)
    scaled = (gate_prob[:, :, None] * activated.astype(jnp.float32)).astype(jnp.bfloat16)
    onehot = (routes[:, :, None] == jnp.arange(EXPERTS, dtype=jnp.int32)[None, None, :]).astype(
        jnp.bfloat16
    )
    spread = jnp.einsum("tke,tkf->tef", onehot, scaled, preferred_element_type=jnp.float32).astype(
        jnp.bfloat16
    )
    moe_part = jnp.einsum("tef,efd->td", spread, expert_down, preferred_element_type=jnp.float32)
    moe_out = lax.psum(moe_part, "seq")
    return (residual + moe_out).astype(jnp.bfloat16)


TOP = 8
TILE = 16
LANES = 128
SEQ = 8
TP = 4
MESH = pl.DeviceIdType.MESH
CHUNKS = 2
VMEM_LIMIT = 61 * 1024 * 1024
TURN = 6.28125
TURN_MIDDLE = 0.0019350051879882812
TURN_REST = 3.0199159819568123e-07


def fits_fused(mesh):
    return mesh.shape["seq"] == SEQ and mesh.shape["tp"] == TP


def lane_of(shape):
    return lax.broadcasted_iota(jnp.int32, shape, len(shape) - 1)


def swap_half(values):
    return pltpu.roll(values, 64, 1)


def split_pair(values):
    high = values.astype(jnp.bfloat16).astype(jnp.float32)
    return jnp.where(lane_of(values.shape) < 64, high, values - high).astype(jnp.bfloat16)


def join_pair(packed):
    values = packed.astype(jnp.float32)
    return values + swap_half(values)


def circle(angles):
    half = angles * 0.5
    square = half * half
    sine = jnp.full_like(square, 1.0 / 6227020800.0)
    cosine = jnp.full_like(square, -1.0 / 87178291200.0)
    for term in (-39916800.0, 362880.0, -5040.0, 120.0, -6.0, 1.0):
        sine = sine * square + 1.0 / term
    for term in (479001600.0, -3628800.0, 40320.0, -720.0, 24.0, -2.0, 1.0):
        cosine = cosine * square + 1.0 / term
    sine = sine * half
    return 1.0 - 2.0 * sine * sine, 2.0 * sine * cosine


def layer_kernel(
    tokens_hbm,
    attn_gain_hbm,
    moe_gain_hbm,
    lengths_hbm,
    routes_hbm,
    router_hbm,
    qkv_hbm,
    keys_hbm,
    values_hbm,
    out_w_hbm,
    gate_hbm,
    up_hbm,
    down_hbm,
    out_ref,
    tokens_ref,
    attn_gain_ref,
    moe_gain_ref,
    lengths_ref,
    routes_t_ref,
    router_ref,
    routes_ref,
    qkv_ref,
    keys_ref,
    values_ref,
    out_w_ref,
    down_ref,
    att_send,
    att_recv,
    att_all,
    res_own,
    res_all,
    pair_w,
    dense,
    onehot,
    shifted,
    picks,
    picks_recv,
    picks_half,
    picks_far,
    logit_rows,
    sums,
    sums_recv,
    sums_half,
    sums_far,
    gate_scale,
    queries_ref,
    new_keys_ref,
    new_values_ref,
    lens_ref,
    scaled,
    spread,
    total,
    part_send,
    part_recv,
    out_own,
    local_sem,
    seq_send,
    seq_recv,
    tp_send,
    tp_recv,
):
    me = lax.axis_index("seq")
    tp = lax.axis_index("tp")
    core = lax.rem(tp, 2)
    core_peer = tp + 1 - 2 * core
    far_peer = lax.rem(tp + 2, TP)
    f32, bf16 = jnp.float32, jnp.bfloat16

    barrier = pltpu.get_barrier_semaphore()
    for step in range(1, SEQ):
        pl.semaphore_signal(
            barrier, inc=1, device_id=(lax.rem(me + step, SEQ), tp), device_id_type=MESH
        )
    for step in range(1, TP):
        pl.semaphore_signal(
            barrier, inc=1, device_id=(me, lax.rem(tp + step, TP)), device_id_type=MESH
        )

    depth = qkv_ref.shape[0] // 3
    hidden = gate_hbm.shape[1]
    wanted = [
        (lengths_hbm, lengths_ref),
        (tokens_hbm, tokens_ref),
        (attn_gain_hbm, attn_gain_ref),
        (qkv_hbm.at[0:depth], qkv_ref.at[0:depth]),
        (qkv_hbm.at[depth : 2 * depth], qkv_ref.at[depth : 2 * depth]),
        (qkv_hbm.at[2 * depth :], qkv_ref.at[2 * depth :]),
        (keys_hbm, keys_ref),
        (values_hbm, values_ref),
        (routes_hbm, routes_t_ref),
        (moe_gain_hbm, moe_gain_ref),
        (router_hbm, router_ref),
        (out_w_hbm, out_w_ref),
        (gate_hbm, pair_w.at[:, 0:hidden, :]),
        (up_hbm, pair_w.at[:, hidden:, :]),
        (down_hbm, down_ref),
    ]
    loads = [
        pltpu.make_async_copy(src, dst, local_sem.at[n]) for n, (src, dst) in enumerate(wanted)
    ]
    for load in loads[:8]:
        load.start()

    def seq_copies(phase, source, target):
        copies = []
        for step in range(1, SEQ):
            peer = lax.rem(me + step, SEQ)
            copies.append(
                pltpu.make_async_remote_copy(
                    src_ref=source(peer),
                    dst_ref=target(me),
                    send_sem=seq_send.at[phase, step],
                    recv_sem=seq_recv.at[phase, step],
                    device_id=(peer, tp),
                    device_id_type=MESH,
                )
            )
        for copy in copies:
            copy.start()
        return copies

    def tp_copy(slot, source, target, peer):
        copy = pltpu.make_async_remote_copy(
            src_ref=source,
            dst_ref=target,
            send_sem=tp_send.at[slot],
            recv_sem=tp_recv.at[slot],
            device_id=(me, peer),
            device_id_type=MESH,
        )
        copy.start()
        return copy

    def rows_of(index):
        return pl.ds(pl.multiple_of(index * TILE, TILE), TILE)

    loads[0].wait()
    request = lax.broadcasted_iota(jnp.int32, (128, 32), 0) // NEW
    picked = request == lane_of((128, 32))
    lens = jnp.sum(
        jnp.where(picked, lengths_ref[...].astype(f32), 0.0), axis=-1, keepdims=True
    )
    lane = lane_of((128, LANES))
    low = lane < 64
    token = lax.broadcasted_iota(jnp.int32, (128, LANES), 0)
    half = HEAD // 2
    table = np.exp(-np.log(np.float32(ROPE_BASE)) * np.arange(half, dtype=np.float32) / half)
    lane1 = lane_of((1, LANES)) % half
    freqs = jnp.zeros((1, LANES), f32)
    for n in range(half):
        freqs = jnp.where(lane1 == n, float(table[n]), freqs)
    angles = (lens + (token % NEW).astype(f32)) * freqs
    turns = jnp.floor(angles * (1.0 / (2 * np.pi)) + 0.5)
    angles = ((angles - turns * TURN) - turns * TURN_MIDDLE) - turns * TURN_REST
    cosine, sine = circle(angles)
    sine = jnp.where(lane % HEAD < half, -sine, sine)

    loads[1].wait()
    loads[2].wait()
    token_full = tokens_ref[...].astype(f32)
    normed = rms_scale(token_full, attn_gain_ref[...].reshape(1, -1)).astype(bf16)
    projected = jnp.zeros((128, qkv_ref.shape[1]), f32)
    for n in range(3):
        at = slice(depth * n, depth * (n + 1))
        loads[3 + n].wait()
        projected = projected + jnp.dot(normed[:, at], qkv_ref[at, :], preferred_element_type=f32)
    for load in loads[8:]:
        load.start()
    tiles = [projected[:, LANES * n : LANES * (n + 1)] for n in range(5)]

    def turned(x):
        swapped = jnp.where(lane % 64 < 32, pltpu.roll(x, 96, 1), pltpu.roll(x, 32, 1))
        return x * cosine + swapped * sine

    turn = [turned(x) for x in tiles]
    factor = 1.0 / HEAD**0.5
    queries = [
        jnp.where(low, turn[0], 0.0),
        jnp.where(low, swap_half(turn[0]), 0.0),
        jnp.where(low, turn[1], 0.0),
        jnp.where(low, 0.0, turn[2]),
        jnp.where(low, 0.0, swap_half(turn[3])),
        jnp.where(low, 0.0, turn[3]),
    ]
    for n in range(6):
        queries_ref[n] = (queries[n] * factor).astype(bf16)
    new_keys_ref[...] = jnp.where(low, swap_half(turn[1]), swap_half(turn[4])).astype(bf16)
    new_values_ref[...] = jnp.where(low, tiles[2], tiles[4]).astype(bf16)
    lens_ref[...] = jnp.broadcast_to(lens, (128, LANES))

    loads[6].wait()
    loads[7].wait()
    slot_count = keys_hbm.shape[0] // 32
    window = float(slot_count * SEQ - SINK)
    col256 = lane_of((32, 8 * slot_count))
    row256 = lax.broadcasted_iota(jnp.int32, (32, 8 * slot_count), 0)
    same = row256 // NEW == col256 // slot_count
    slot = (me * slot_count + col256 % slot_count).astype(f32)
    offset = (row256 % NEW).astype(f32)
    row32 = lax.broadcasted_iota(jnp.int32, (32, 32), 0)
    col32 = lax.broadcasted_iota(jnp.int32, (32, 32), 1)
    own = (row32 // NEW == col32 // NEW) & (col32 <= row32) & (me == 0)
    own_bias = jnp.where(own, 0.0, FLOOR_SCORE).astype(f32)
    own_bias = jnp.concatenate([own_bias] * 6, axis=0)
    contract = (((1,), (1,)), ((), ()))
    place, side = me // 2, lax.rem(me, 2)

    def send_parts(shift):
        sent = []
        for turned_side in range(2):
            if shift == 0 and turned_side == 0:
                continue
            peer = 2 * lax.rem(place + shift, 4) + lax.rem(side + turned_side, 2)
            copy = pltpu.make_async_remote_copy(
                src_ref=att_send.at[rows_of(peer), :],
                dst_ref=att_recv.at[me],
                send_sem=seq_send.at[0, 2 * shift + turned_side],
                recv_sem=seq_recv.at[0, 2 * shift + turned_side],
                device_id=(peer, tp),
                device_id_type=MESH,
            )
            copy.start()
            sent.append(copy)
        return sent

    copies = []
    for block in (2, 1, 3, 0):
        number = lax.rem(place + block, 4)
        at = pl.ds(pl.multiple_of(32 * number, 32), 32)
        slots = pl.ds(pl.multiple_of(256 * number, 256), 256)
        query = queries_ref[:, at, :].reshape(192, LANES)
        last = lens_ref[at, 0:1] - 1.0
        back = last - slot
        older = last - (back - window * jnp.floor((back + 0.5) * (1.0 / window)))
        seen = (slot <= last) & ((slot < SINK) | (older > last + offset - window))
        old_bias = jnp.where(seen & same, 0.0, FLOOR_SCORE).astype(f32)
        old_bias = jnp.concatenate([old_bias] * 6, axis=0)
        old = lax.dot_general(query, keys_ref[slots, :], contract, preferred_element_type=f32)
        new = lax.dot_general(query, new_keys_ref[at, :], contract, preferred_element_type=f32)
        old = old + old_bias
        new = new + own_bias
        top = jnp.maximum(
            jnp.max(old, axis=-1, keepdims=True), jnp.max(new, axis=-1, keepdims=True)
        )
        old = jnp.exp(old - top)
        new = jnp.exp(new - top)
        mass = jnp.sum(old, axis=-1, keepdims=True) + jnp.sum(new, axis=-1, keepdims=True)
        mixed = jnp.dot(
            old.astype(bf16), values_ref[slots, :], preferred_element_type=f32
        ) + jnp.dot(new.astype(bf16), new_values_ref[at, :], preferred_element_type=f32)
        mixed = mixed / mass
        level = top + jnp.log(mass)
        head = [mixed[32 * n : 32 * n + 32] for n in range(6)]
        lane32 = lane_of((32, LANES))
        low32 = lane32 < 64
        att_send[at, 0:128] = jnp.where(low32, head[0], swap_half(head[1])).astype(bf16)
        att_send[at, 128:256] = jnp.where(low32, head[2], head[3]).astype(bf16)
        att_send[at, 256:384] = jnp.where(low32, swap_half(head[4]), head[5]).astype(bf16)
        levels = jnp.zeros((32, LANES), f32)
        for n in range(6):
            levels = jnp.where(lane32 % 8 == n, level[32 * n : 32 * n + 32], levels)
        high = levels.astype(bf16).astype(f32)
        rest = levels - high
        middle = rest.astype(bf16).astype(f32)
        levels = jnp.where(
            lane32 < 8, high, jnp.where(lane32 < 16, middle, rest - middle)
        )
        att_send[at, 384:512] = jnp.where(lane32 < 24, levels, 0.0).astype(bf16)

        if block == 1:
            pl.semaphore_wait(barrier, SEQ + TP - 2)
            copies += send_parts(2) + send_parts(1)
    copies += send_parts(3) + send_parts(0)
    att_recv[me] = att_send[rows_of(me), :]

    loads[8].wait()
    routes_ref[...] = jnp.transpose(
        jnp.concatenate([routes_t_ref[...], jnp.zeros((120, 128), jnp.int32)], axis=0)
    )
    spread_col = lax.broadcasted_iota(jnp.int32, (TILE, EXPERTS * TILE), 1)
    spread_row = lax.broadcasted_iota(jnp.int32, (TILE, EXPERTS * TILE), 0)
    expert_at = jnp.where(spread_col % TILE == spread_row, spread_col // TILE, -1)

    def mark(n, carry):
        routes = routes_ref[rows_of(n), 0:TOP]
        for k in range(TOP):
            hit = routes[:, k : k + 1] == expert_at
            onehot[n, TILE * k : TILE * (k + 1), :] = jnp.where(hit, 1.0, 0.0).astype(bf16)
        return carry

    lax.fori_loop(0, 8, mark, 0, unroll=2)
    half_lane = jnp.where(low, 0, 1)
    for k in range(TOP):
        shifted[k] = routes_ref[:, k : k + 1] - half_lane

    for copy in copies:
        copy.wait()
    own_level = []
    for n in range(SEQ):
        packed = att_recv[n, :, 384:512].astype(f32)
        own_level.append(packed + pltpu.roll(packed, 120, 1) + pltpu.roll(packed, 112, 1))
    top = own_level[0]
    for n in range(1, SEQ):
        top = jnp.maximum(top, own_level[n])
    weights = [jnp.exp(x - top) for x in own_level]
    mass = weights[0]
    for n in range(1, SEQ):
        mass = mass + weights[n]
    low16 = lane_of((TILE, LANES)) < 64
    parts = [jnp.zeros((TILE, LANES), f32) for _ in range(3)]
    for n in range(SEQ):
        share = weights[n] / mass
        for j in range(3):
            wide = jnp.where(low16, share[:, 2 * j : 2 * j + 1], share[:, 2 * j + 1 : 2 * j + 2])
            parts[j] = parts[j] + wide * att_recv[n, :, 128 * j : 128 * j + 128].astype(f32)
    att_all[tp] = jnp.concatenate(parts, axis=-1).astype(bf16)

    copies = [
        tp_copy(step, att_all.at[tp], att_all.at[tp], peer)
        for step, peer in enumerate((core_peer, far_peer, lax.rem(core_peer + 2, TP)))
    ]
    loads[11].wait()
    width = out_w_ref.shape[1]
    residual = tokens_ref[rows_of(me), pl.ds(pl.multiple_of(tp * width, 128), width)].astype(f32)
    for step, group in enumerate((tp, core_peer, far_peer, lax.rem(core_peer + 2, TP))):
        if step > 0:
            copies[step - 1].wait()
        at = pl.ds(pl.multiple_of(group * width, 128), width)
        residual = residual + jnp.dot(
            att_all[group], out_w_ref[at, :], preferred_element_type=f32
        )
    res_own[...] = residual
    res_all[me] = residual.astype(bf16)
    copies = seq_copies(1, lambda peer: res_all.at[me], lambda index: res_all.at[index])
    for copy in copies:
        copy.wait()

    full = res_all[...].reshape(SEQ * TILE, width).astype(f32)
    loads[9].wait()
    loads[10].wait()
    gained = full * moe_gain_ref[...].reshape(1, -1)
    gained_b = gained.astype(bf16)
    rest = (gained - gained_b.astype(f32)).astype(bf16)
    router = router_ref[...]
    logits = lax.dot_general(
        gained_b, router, contract, preferred_element_type=f32
    ) + lax.dot_general(rest, router, contract, preferred_element_type=f32)
    squares = jnp.sum(full * full, axis=-1, keepdims=True)
    logit_rows[...] = jnp.zeros_like(logit_rows)
    logit_rows[:, 0:EXPERTS] = logits
    rows = jnp.where(lane == EXPERTS, squares, logit_rows[...])
    rows = split_pair(jnp.where(low, rows, swap_half(rows)))
    sums[...] = rows
    sums_copy = tp_copy(
        4 + 3 * CHUNKS,
        sums.at[pl.ds(pl.multiple_of(64 * (1 - core), 64), 64), :],
        sums_recv,
        core_peer,
    )

    loads[12].wait()
    loads[13].wait()

    def experts(n, carry):
        weight = pair_w[pl.ds(2 * n, 2)].reshape(2 * LANES, width)
        both = lax.dot_general(
            gained_b, weight, contract, preferred_element_type=f32
        ).astype(bf16)
        dense[2 * n] = both[:, :LANES]
        dense[2 * n + 1] = both[:, LANES:]
        return carry

    lax.fori_loop(0, EXPERTS // 2, experts, 0, unroll=10)

    def pick(n, carry):
        group = dense[:, rows_of(n), :].reshape(EXPERTS * TILE, LANES)
        picks[n, 0 : TOP * TILE, :] = jnp.dot(
            onehot[n], group, preferred_element_type=f32
        ).astype(bf16)
        return carry

    groups = 4 // CHUNKS
    count = groups * TILE
    near, far, back = [], [], []

    def pick_theirs(chunk):
        first = 4 * (1 - core) + groups * chunk
        for n in range(groups):
            pick(first + n, 0)
        at = slice(groups * chunk, groups * (chunk + 1))
        near.append(
            tp_copy(4 + chunk, picks.at[pl.ds(first, groups)], picks_recv.at[at], core_peer)
        )

    def pick_ours(chunk):
        for n in range(groups):
            pick(4 * core + groups * chunk + n, 0)

    def add_near(chunk):
        at = slice(groups * chunk, groups * (chunk + 1))
        mine = pl.ds(4 * core + groups * chunk, groups)
        near[chunk].wait()
        picks_half[at] = (picks[mine].astype(f32) + picks_recv[at].astype(f32)).astype(bf16)
        far.append(
            tp_copy(4 + CHUNKS + chunk, picks_half.at[at], picks_far.at[at], far_peer)
        )

    ours = pl.ds(pl.multiple_of(64 * core, 64), 64)
    pick_theirs(0)
    pick_ours(0)
    for chunk in range(1, CHUNKS):
        pick_theirs(chunk)
        add_near(chunk - 1)
        pick_ours(chunk)
    sums_copy.wait()
    sums_half[...] = split_pair(join_pair(sums[ours, :]) + join_pair(sums_recv[...]))
    sums_copy = tp_copy(5 + 3 * CHUNKS, sums_half, sums_far, far_peer)
    add_near(CHUNKS - 1)

    sums_copy.wait()
    rows = join_pair(sums_half[...]) + join_pair(sums_far[...])
    lanes = lane_of((64, LANES))
    scales = lax.rsqrt(rows[:, EXPERTS : EXPERTS + 1] / D + EPSILON)
    routes = routes_ref[ours, 0:TOP]
    hits = [lanes == routes[:, k : k + 1] for k in range(TOP)]
    routed = hits[0]
    for k in range(1, TOP):
        routed = routed | hits[k]
    scores = jnp.where(routed, rows * scales, FLOOR_SCORE)
    prob = jnp.exp(scores - jnp.max(scores, axis=-1, keepdims=True))
    prob = jnp.where(routed, prob, 0.0)
    prob = prob / jnp.sum(prob, axis=-1, keepdims=True)
    probs = [jnp.sum(jnp.where(hits[k], prob, 0.0), axis=-1, keepdims=True) for k in range(TOP)]
    for k in range(TOP):
        gate_scale[k] = jnp.broadcast_to(probs[k], (64, LANES))
    gate_scale[TOP] = jnp.broadcast_to(scales, (64, LANES))
    low_part = lane_of((count, LANES)) < 64
    for chunk in range(CHUNKS):
        at = slice(groups * chunk, groups * (chunk + 1))
        mine = pl.ds(4 * core + groups * chunk, groups)
        part = slice(count * chunk, count * (chunk + 1))
        far[chunk].wait()
        scale = gate_scale[TOP, part, :]
        for k in range(TOP):
            of = slice(TILE * k, TILE * (k + 1))
            both = (picks_half[at, of, :].astype(f32) + picks_far[at, of, :].astype(f32)).reshape(
                count, LANES
            ) * scale
            active = both / (1.0 + jnp.exp(-both)) * swap_half(both)
            active = active.astype(bf16).astype(f32) * gate_scale[k, part, :]
            active = jnp.where(low_part, active, swap_half(active))
            scaled[mine, of, :] = active.astype(bf16).reshape(groups, TILE, LANES)
        back.append(
            tp_copy(4 + 2 * CHUNKS + chunk, scaled.at[mine], scaled.at[mine], core_peer)
        )

    def spread_rows(n):
        values = [
            scaled[n, TILE * k : TILE * (k + 1), :].astype(f32) for k in range(TOP)
        ]
        routes = [shifted[k, rows_of(n), :] for k in range(TOP)]
        for pair in range(EXPERTS // 2):
            one = jnp.zeros((TILE, LANES), f32)
            for k in range(TOP):
                one = jnp.where(routes[k] == 2 * pair, values[k], one)
            spread[rows_of(n), LANES * pair : LANES * (pair + 1)] = one.astype(bf16)

    for n in range(4):
        spread_rows(4 * core + n)
    loads[14].wait()
    for chunk in range(CHUNKS):
        back[chunk].wait()
        for n in range(groups):
            spread_rows(4 * (1 - core) + groups * chunk + n)
    total[...] = jnp.dot(
        spread[...], down_ref[...].reshape(EXPERTS * hidden, width), preferred_element_type=f32
    )
    part_send[...] = total[...].astype(bf16)

    copies = seq_copies(
        2, lambda peer: part_send.at[rows_of(peer), :], lambda index: part_recv.at[index]
    )
    result = res_own[...] + total[rows_of(me), :]
    for copy in copies:
        copy.wait()
    part_recv[me] = jnp.zeros((TILE, width), bf16)
    for n in range(SEQ):
        result = result + part_recv[n].astype(f32)
    out_own[...] = result.astype(bf16)
    out_ref[rows_of(me), :] = out_own[...]
    copies = seq_copies(3, lambda peer: out_own, lambda index: out_ref.at[rows_of(index), :])
    for copy in copies:
        copy.wait()


def fused_device(
    tokens,
    attn_gain,
    qkv_weight,
    out_weight,
    moe_gain,
    router_weight,
    expert_gate,
    expert_up,
    expert_down,
    cache_keys,
    cache_values,
    lengths,
    routes,
):
    count = tokens.shape[0]
    width = out_weight.shape[1]
    requests, slot_count = cache_keys.shape[:2]
    vmem = pl.BlockSpec(memory_space=pltpu.VMEM)
    hbm = pl.BlockSpec(memory_space=pltpu.HBM)
    bf16, f32 = jnp.bfloat16, jnp.float32
    hidden = expert_gate.shape[2]
    return pl.pallas_call(
        layer_kernel,
        out_shape=pltpu.VMEM((count, width), bf16),
        in_specs=[hbm] * 13,
        out_specs=vmem,
        scratch_shapes=[
            pltpu.VMEM(tokens.shape, bf16),
            pltpu.VMEM((D,), f32),
            pltpu.VMEM((width,), f32),
            pltpu.VMEM((1, requests), jnp.int32),
            pltpu.VMEM((TOP, count), jnp.int32),
            pltpu.VMEM((EXPERTS, width), bf16),
            pltpu.VMEM((count, count), jnp.int32),
            pltpu.VMEM(qkv_weight.shape, bf16),
            pltpu.VMEM((requests * slot_count, LANES), bf16),
            pltpu.VMEM((requests * slot_count, LANES), bf16),
            pltpu.VMEM(out_weight.shape, bf16),
            pltpu.VMEM(expert_down.shape, bf16),
            pltpu.VMEM((count, 512), bf16),
            pltpu.VMEM((SEQ, TILE, 512), bf16),
            pltpu.VMEM((TP, TILE, width), bf16),
            pltpu.VMEM((TILE, width), f32),
            pltpu.VMEM((SEQ, TILE, width), bf16),
            pltpu.VMEM((EXPERTS, 2 * hidden, width), bf16),
            pltpu.VMEM((EXPERTS, count, LANES), bf16),
            pltpu.VMEM((8, TOP * TILE, EXPERTS * TILE), bf16),
            pltpu.VMEM((TOP, count, LANES), jnp.int32),
            pltpu.VMEM((8, TOP * TILE, LANES), bf16),
            pltpu.VMEM((4, TOP * TILE, LANES), bf16),
            pltpu.VMEM((4, TOP * TILE, LANES), bf16),
            pltpu.VMEM((4, TOP * TILE, LANES), bf16),
            pltpu.VMEM((count, LANES), f32),
            pltpu.VMEM((count, LANES), bf16),
            pltpu.VMEM((64, LANES), bf16),
            pltpu.VMEM((64, LANES), bf16),
            pltpu.VMEM((64, LANES), bf16),
            pltpu.VMEM((TOP + 1, 64, LANES), f32),
            pltpu.VMEM((6, count, LANES), bf16),
            pltpu.VMEM((count, LANES), bf16),
            pltpu.VMEM((count, LANES), bf16),
            pltpu.VMEM((count, LANES), f32),
            pltpu.VMEM((8, TOP * TILE, LANES), bf16),
            pltpu.VMEM((count, EXPERTS * hidden), bf16),
            pltpu.VMEM((count, width), f32),
            pltpu.VMEM((count, width), bf16),
            pltpu.VMEM((SEQ, TILE, width), bf16),
            pltpu.VMEM((TILE, width), bf16),
            pltpu.SemaphoreType.DMA((15,)),
            pltpu.SemaphoreType.DMA((4, SEQ)),
            pltpu.SemaphoreType.DMA((4, SEQ)),
            pltpu.SemaphoreType.DMA((6 + 3 * CHUNKS,)),
            pltpu.SemaphoreType.DMA((6 + 3 * CHUNKS,)),
        ],
        compiler_params=pltpu.CompilerParams(
            collective_id=0, has_side_effects=True, vmem_limit_bytes=VMEM_LIMIT
        ),
        cost_estimate=pl.CostEstimate(
            flops=2_000_000_000, bytes_accessed=20_000_000, transcendentals=1_000_000
        ),
        name="layer",
    )(
        tokens,
        attn_gain,
        moe_gain,
        lengths.reshape(1, -1),
        routes.T,
        router_weight.T,
        qkv_weight,
        cache_keys.reshape(-1, LANES),
        cache_values.reshape(-1, LANES),
        out_weight,
        jnp.swapaxes(expert_gate, 1, 2),
        jnp.swapaxes(expert_up, 1, 2),
        expert_down,
    )


def solution(mesh):
    in_specs = (
        P(),
        P(),
        P(None, "tp"),
        P(None, "tp"),
        P("tp"),
        P("tp", None),
        P(None, "tp", "seq"),
        P(None, "tp", "seq"),
        P(None, "seq", "tp"),
        P(None, "seq", "tp"),
        P(None, "seq", "tp"),
        P(),
        P(),
    )
    out_specs = P(None, "tp")
    body = fused_device if fits_fused(mesh) else on_device
    return jax.shard_map(
        body, mesh=mesh, in_specs=in_specs, out_specs=out_specs, check_vma=False
    )
```

```python
import jax
import jax.numpy as jnp
import numpy as np
from jax import lax
from jax.experimental import pallas as pl
from jax.experimental.pallas import tpu as pltpu
from jax.sharding import PartitionSpec as P

D = 1536
HEAD = 64
EXPERTS = 40
SINK = 4
NEW = 4
GROUP = 3


EPSILON = 1e-06
ROPE_BASE = 10000.0
FLOOR_SCORE = -1e30


def joined(shard, axis, combine):
    everything = jax.tree.map(lambda part: lax.all_gather(part, axis), shard)
    initial = jax.tree.map(lambda part: part[0], everything)

    def lap(k, so_far):
        return combine(so_far, jax.tree.map(lambda part: part[k], everything))

    return lax.fori_loop(1, lax.axis_size(axis), lap, initial)


def rms_scale(values, gain):
    return values * lax.rsqrt(jnp.mean(values * values, axis=-1, keepdims=True) + EPSILON) * gain


def rotate(values, places):
    half_dim = values.shape[-1] // 2
    freqs = jnp.exp(-jnp.log(ROPE_BASE) * jnp.arange(half_dim, dtype=jnp.float32) / half_dim)
    angles = places.reshape((-1,) + (1,) * (values.ndim - 1)) * freqs
    cosine = jnp.cos(angles)
    sine = jnp.sin(angles)
    first = values[..., :half_dim]
    second = values[..., half_dim:]
    return jnp.concatenate(
        [first * cosine - second * sine, first * sine + second * cosine], axis=-1
    )


def visible(slots, lengths, window):
    lens = lengths[:, None]
    slot_row = slots[None, :]
    live = slot_row < lens
    older = lens - 1 - jnp.mod(lens - 1 - slot_row, window)
    placed = jnp.where(slot_row < SINK, slot_row, older)
    offsets = jnp.arange(NEW, dtype=jnp.int32)
    inside = (slot_row[:, None, :] < SINK) | (
        placed[:, None, :] >= lens[:, :, None] + offsets[None, :, None] - window
    )
    return live[:, None, :] & inside


def combine_parts(earlier, later):
    top_a, mass_a, weighted_a = earlier
    top_b, mass_b, weighted_b = later
    top_both = jnp.maximum(top_a, top_b)
    factor_a = jnp.exp(top_a - top_both)
    factor_b = jnp.exp(top_b - top_both)
    return (
        top_both,
        mass_a * factor_a + mass_b * factor_b,
        weighted_a * factor_a[..., None] + weighted_b * factor_b[..., None],
    )


def on_device(
    tokens,
    attn_gain,
    qkv_weight,
    out_weight,
    moe_gain,
    router_weight,
    expert_gate,
    expert_up,
    expert_down,
    cache_keys,
    cache_values,
    lengths,
    routes,
):
    seq_count = lax.axis_size("seq")
    seq_index = lax.axis_index("seq")
    tp_index = lax.axis_index("tp")
    token_count = tokens.shape[0]
    requests = cache_keys.shape[0]
    slot_count = cache_keys.shape[1]
    window = slot_count * seq_count - SINK
    local_kv = cache_keys.shape[2] // HEAD
    token_full = tokens.astype(jnp.float32)
    normed = rms_scale(token_full, attn_gain).astype(jnp.bfloat16)
    projected = jnp.dot(normed, qkv_weight, preferred_element_type=jnp.float32)
    projected = projected.reshape(token_count, local_kv, GROUP + 2, HEAD)
    places = (
        (lengths[:, None] + jnp.arange(NEW, dtype=jnp.int32)[None, :])
        .reshape(token_count)
        .astype(jnp.float32)
    )
    queries = rotate(projected[:, :, :GROUP], places).astype(jnp.bfloat16)
    new_keys = rotate(projected[:, :, GROUP], places).astype(jnp.bfloat16)
    new_values = projected[:, :, GROUP + 1].astype(jnp.bfloat16)
    query_b = queries.reshape(requests, NEW, local_kv, GROUP, HEAD)
    key_new = new_keys.reshape(requests, NEW, local_kv, HEAD)
    value_new = new_values.reshape(requests, NEW, local_kv, HEAD)
    slots = seq_index * slot_count + jnp.arange(slot_count, dtype=jnp.int32)
    seen = visible(slots, lengths, window)[:, :, None, None, :]
    factor = 1.0 / HEAD**0.5
    key_old = cache_keys.reshape(requests, slot_count, local_kv, HEAD)
    value_old = cache_values.reshape(requests, slot_count, local_kv, HEAD)
    old_scores = (
        jnp.einsum("rtgqd,rsgd->rtgqs", query_b, key_old, preferred_element_type=jnp.float32)
        * factor
    )
    new_scores = (
        jnp.einsum("rtgqd,rugd->rtgqu", query_b, key_new, preferred_element_type=jnp.float32)
        * factor
    )
    causal = jnp.arange(NEW)[:, None] >= jnp.arange(NEW)[None, :]
    own_mask = causal[None, :, None, None, :] & (seq_index == 0)
    old_masked = jnp.where(seen, old_scores, FLOOR_SCORE)
    new_masked = jnp.where(own_mask, new_scores, FLOOR_SCORE)
    top_score = jnp.maximum(jnp.max(old_masked, axis=-1), jnp.max(new_masked, axis=-1))
    old_weights = jnp.where(seen, jnp.exp(old_masked - top_score[..., None]), 0.0)
    new_weights = jnp.where(own_mask, jnp.exp(new_masked - top_score[..., None]), 0.0)
    mass = jnp.sum(old_weights, axis=-1) + jnp.sum(new_weights, axis=-1)
    weighted = jnp.einsum(
        "rtgqs,rsgd->rtgqd", old_weights, value_old.astype(jnp.float32)
    ) + jnp.einsum("rtgqu,rugd->rtgqd", new_weights, value_new.astype(jnp.float32))
    top_score, mass, weighted = joined((top_score, mass, weighted), "seq", combine_parts)
    attended = (weighted / mass[..., None]).reshape(token_count, -1).astype(jnp.bfloat16)
    feature_part = out_weight.shape[1]
    attn_out = jnp.dot(
        lax.all_gather(attended, "tp", axis=1, tiled=True),
        out_weight,
        preferred_element_type=jnp.float32,
    )
    residual = (
        lax.dynamic_slice_in_dim(token_full, tp_index * feature_part, feature_part, 1) + attn_out
    )
    gained = residual * moe_gain
    squares_local = jnp.sum(residual * residual, axis=-1)
    router_f = router_weight.astype(jnp.float32)
    squares_total = lax.psum(squares_local, "tp")
    scale = lax.rsqrt(squares_total / D + EPSILON)
    logits = lax.psum(
        jnp.dot(gained * scale[:, None], router_f, precision=lax.Precision.HIGHEST), "tp"
    )
    moe_in = (gained * scale[:, None]).astype(jnp.bfloat16)
    chosen = jnp.take_along_axis(logits, routes, axis=1)
    gate_prob = jax.nn.softmax(chosen, axis=-1)
    gate_part = jnp.einsum("td,edf->tef", moe_in, expert_gate, preferred_element_type=jnp.float32)
    up_part = jnp.einsum("td,edf->tef", moe_in, expert_up, preferred_element_type=jnp.float32)
    gate_pick = jnp.take_along_axis(gate_part, routes[:, :, None], axis=1)
    up_pick = jnp.take_along_axis(up_part, routes[:, :, None], axis=1)
    gate_sum, up_sum = (
        lax.psum(gate_pick.astype(jnp.bfloat16), "tp").astype(jnp.float32),
        lax.psum(up_pick.astype(jnp.bfloat16), "tp").astype(jnp.float32),
    )
    activated = (jax.nn.silu(gate_sum) * up_sum).astype(jnp.bfloat16)
    scaled = (gate_prob[:, :, None] * activated.astype(jnp.float32)).astype(jnp.bfloat16)
    onehot = (routes[:, :, None] == jnp.arange(EXPERTS, dtype=jnp.int32)[None, None, :]).astype(
        jnp.bfloat16
    )
    spread = jnp.einsum("tke,tkf->tef", onehot, scaled, preferred_element_type=jnp.float32).astype(
        jnp.bfloat16
    )
    moe_part = jnp.einsum("tef,efd->td", spread, expert_down, preferred_element_type=jnp.float32)
    moe_out = lax.psum(moe_part, "seq")
    return (residual + moe_out).astype(jnp.bfloat16)


TOP = 8
TILE = 16
LANES = 128
SEQ = 8
TP = 4
MESH = pl.DeviceIdType.MESH
CHUNKS = 4
VMEM_LIMIT = 61 * 1024 * 1024
TURN = 6.28125
TURN_MIDDLE = 0.0019350051879882812
TURN_REST = 3.0199159819568123e-07


def fits_fused(mesh):
    return mesh.shape["seq"] == SEQ and mesh.shape["tp"] == TP


def lane_of(shape):
    return lax.broadcasted_iota(jnp.int32, shape, len(shape) - 1)


def swap_half(values):
    return pltpu.roll(values, 64, 1)


def split_pair(values):
    high = values.astype(jnp.bfloat16).astype(jnp.float32)
    return jnp.where(lane_of(values.shape) < 64, high, values - high).astype(jnp.bfloat16)


def join_pair(packed):
    values = packed.astype(jnp.float32)
    return values + swap_half(values)


def circle(angles):
    half = angles * 0.5
    square = half * half
    sine = jnp.full_like(square, 1.0 / 6227020800.0)
    cosine = jnp.full_like(square, -1.0 / 87178291200.0)
    for term in (-39916800.0, 362880.0, -5040.0, 120.0, -6.0, 1.0):
        sine = sine * square + 1.0 / term
    for term in (479001600.0, -3628800.0, 40320.0, -720.0, 24.0, -2.0, 1.0):
        cosine = cosine * square + 1.0 / term
    sine = sine * half
    return 1.0 - 2.0 * sine * sine, 2.0 * sine * cosine


def layer_kernel(
    tokens_hbm,
    attn_gain_hbm,
    moe_gain_hbm,
    lengths_hbm,
    routes_hbm,
    router_hbm,
    qkv_hbm,
    keys_hbm,
    values_hbm,
    out_w_hbm,
    gate_hbm,
    up_hbm,
    down_hbm,
    out_ref,
    tokens_ref,
    attn_gain_ref,
    moe_gain_ref,
    lengths_ref,
    routes_t_ref,
    router_ref,
    routes_ref,
    qkv_ref,
    keys_ref,
    values_ref,
    out_w_ref,
    down_ref,
    att_send,
    att_recv,
    att_all,
    res_own,
    res_all,
    pair_w,
    dense,
    onehot,
    shifted,
    picks,
    picks_recv,
    picks_half,
    picks_far,
    logit_rows,
    sums,
    sums_recv,
    sums_half,
    sums_far,
    gate_scale,
    queries_ref,
    new_keys_ref,
    new_values_ref,
    lens_ref,
    scaled,
    spread,
    total,
    part_send,
    part_recv,
    out_own,
    local_sem,
    seq_send,
    seq_recv,
    tp_send,
    tp_recv,
):
    me = lax.axis_index("seq")
    tp = lax.axis_index("tp")
    core = lax.rem(tp, 2)
    core_peer = tp + 1 - 2 * core
    far_peer = lax.rem(tp + 2, TP)
    f32, bf16 = jnp.float32, jnp.bfloat16

    barrier = pltpu.get_barrier_semaphore()
    for step in range(1, SEQ):
        pl.semaphore_signal(
            barrier, inc=1, device_id=(lax.rem(me + step, SEQ), tp), device_id_type=MESH
        )
    for step in range(1, TP):
        pl.semaphore_signal(
            barrier, inc=1, device_id=(me, lax.rem(tp + step, TP)), device_id_type=MESH
        )

    depth = qkv_ref.shape[0] // 3
    hidden = gate_hbm.shape[1]
    wanted = [
        (lengths_hbm, lengths_ref),
        (tokens_hbm, tokens_ref),
        (attn_gain_hbm, attn_gain_ref),
        (qkv_hbm.at[0:depth], qkv_ref.at[0:depth]),
        (qkv_hbm.at[depth : 2 * depth], qkv_ref.at[depth : 2 * depth]),
        (qkv_hbm.at[2 * depth :], qkv_ref.at[2 * depth :]),
        (keys_hbm, keys_ref),
        (values_hbm, values_ref),
        (routes_hbm, routes_t_ref),
        (moe_gain_hbm, moe_gain_ref),
        (router_hbm, router_ref),
        (out_w_hbm, out_w_ref),
        (gate_hbm, pair_w.at[:, 0:hidden, :]),
        (up_hbm, pair_w.at[:, hidden:, :]),
        (down_hbm, down_ref),
    ]
    loads = [
        pltpu.make_async_copy(src, dst, local_sem.at[n]) for n, (src, dst) in enumerate(wanted)
    ]
    for load in loads[:8]:
        load.start()

    def seq_copies(phase, source, target):
        copies = []
        for step in (4, 3, 5, 2, 6, 7, 1):
            peer = lax.rem(me + step, SEQ)
            copies.append(
                pltpu.make_async_remote_copy(
                    src_ref=source(peer),
                    dst_ref=target(me),
                    send_sem=seq_send.at[phase, step],
                    recv_sem=seq_recv.at[phase, step],
                    device_id=(peer, tp),
                    device_id_type=MESH,
                )
            )
        for copy in copies:
            copy.start()
        return copies

    def tp_copy(slot, source, target, peer):
        copy = pltpu.make_async_remote_copy(
            src_ref=source,
            dst_ref=target,
            send_sem=tp_send.at[slot],
            recv_sem=tp_recv.at[slot],
            device_id=(me, peer),
            device_id_type=MESH,
        )
        copy.start()
        return copy

    def rows_of(index):
        return pl.ds(pl.multiple_of(index * TILE, TILE), TILE)

    loads[0].wait()
    request = lax.broadcasted_iota(jnp.int32, (128, 32), 0) // NEW
    picked = request == lane_of((128, 32))
    lens = jnp.sum(
        jnp.where(picked, lengths_ref[...].astype(f32), 0.0), axis=-1, keepdims=True
    )
    lane = lane_of((128, LANES))
    low = lane < 64
    token = lax.broadcasted_iota(jnp.int32, (128, LANES), 0)
    half = HEAD // 2
    table = np.exp(-np.log(np.float32(ROPE_BASE)) * np.arange(half, dtype=np.float32) / half)
    lane1 = lane_of((1, LANES)) % half
    freqs = jnp.zeros((1, LANES), f32)
    for n in range(half):
        freqs = jnp.where(lane1 == n, float(table[n]), freqs)
    angles = (lens + (token % NEW).astype(f32)) * freqs
    turns = jnp.floor(angles * (1.0 / (2 * np.pi)) + 0.5)
    angles = ((angles - turns * TURN) - turns * TURN_MIDDLE) - turns * TURN_REST
    cosine, sine = circle(angles)
    sine = jnp.where(lane % HEAD < half, -sine, sine)

    loads[1].wait()
    loads[2].wait()
    token_full = tokens_ref[...].astype(f32)
    normed = rms_scale(token_full, attn_gain_ref[...].reshape(1, -1)).astype(bf16)
    projected = jnp.zeros((128, qkv_ref.shape[1]), f32)
    for n in range(3):
        at = slice(depth * n, depth * (n + 1))
        loads[3 + n].wait()
        projected = projected + jnp.dot(normed[:, at], qkv_ref[at, :], preferred_element_type=f32)
    for load in loads[8:]:
        load.start()
    tiles = [projected[:, LANES * n : LANES * (n + 1)] for n in range(5)]

    def turned(x):
        swapped = jnp.where(lane % 64 < 32, pltpu.roll(x, 96, 1), pltpu.roll(x, 32, 1))
        return x * cosine + swapped * sine

    turn = [turned(x) for x in tiles]
    factor = 1.0 / HEAD**0.5
    queries = [
        jnp.where(low, turn[0], 0.0),
        jnp.where(low, swap_half(turn[0]), 0.0),
        jnp.where(low, turn[1], 0.0),
        jnp.where(low, 0.0, turn[2]),
        jnp.where(low, 0.0, swap_half(turn[3])),
        jnp.where(low, 0.0, turn[3]),
    ]
    for n in range(6):
        queries_ref[n] = (queries[n] * factor).astype(bf16)
    new_keys_ref[...] = jnp.where(low, swap_half(turn[1]), swap_half(turn[4])).astype(bf16)
    new_values_ref[...] = jnp.where(low, tiles[2], tiles[4]).astype(bf16)
    lens_ref[...] = jnp.broadcast_to(lens, (128, LANES))

    loads[6].wait()
    loads[7].wait()
    slot_count = keys_hbm.shape[0] // 32
    window = float(slot_count * SEQ - SINK)
    col256 = lane_of((32, 8 * slot_count))
    row256 = lax.broadcasted_iota(jnp.int32, (32, 8 * slot_count), 0)
    same = row256 // NEW == col256 // slot_count
    slot = (me * slot_count + col256 % slot_count).astype(f32)
    offset = (row256 % NEW).astype(f32)
    row32 = lax.broadcasted_iota(jnp.int32, (32, 32), 0)
    col32 = lax.broadcasted_iota(jnp.int32, (32, 32), 1)
    own = (row32 // NEW == col32 // NEW) & (col32 <= row32) & (me == 0)
    own_bias = jnp.where(own, 0.0, FLOOR_SCORE).astype(f32)
    own_bias = jnp.concatenate([own_bias] * 6, axis=0)
    contract = (((1,), (1,)), ((), ()))
    place, side = me // 2, lax.rem(me, 2)

    def send_parts(shift):
        sent = []
        for turned_side in range(2):
            if shift == 0 and turned_side == 0:
                continue
            peer = 2 * lax.rem(place + shift, 4) + lax.rem(side + turned_side, 2)
            copy = pltpu.make_async_remote_copy(
                src_ref=att_send.at[rows_of(peer), :],
                dst_ref=att_recv.at[me],
                send_sem=seq_send.at[0, 2 * shift + turned_side],
                recv_sem=seq_recv.at[0, 2 * shift + turned_side],
                device_id=(peer, tp),
                device_id_type=MESH,
            )
            copy.start()
            sent.append(copy)
        return sent

    copies = []
    for block in (2, 1, 3, 0):
        number = lax.rem(place + block, 4)
        at = pl.ds(pl.multiple_of(32 * number, 32), 32)
        slots = pl.ds(pl.multiple_of(256 * number, 256), 256)
        query = queries_ref[:, at, :].reshape(192, LANES)
        last = lens_ref[at, 0:1] - 1.0
        back = last - slot
        older = last - (back - window * jnp.floor((back + 0.5) * (1.0 / window)))
        seen = (slot <= last) & ((slot < SINK) | (older > last + offset - window))
        old_bias = jnp.where(seen & same, 0.0, FLOOR_SCORE).astype(f32)
        old_bias = jnp.concatenate([old_bias] * 6, axis=0)
        old = lax.dot_general(query, keys_ref[slots, :], contract, preferred_element_type=f32)
        new = lax.dot_general(query, new_keys_ref[at, :], contract, preferred_element_type=f32)
        old = old + old_bias
        new = new + own_bias
        top = jnp.maximum(
            jnp.max(old, axis=-1, keepdims=True), jnp.max(new, axis=-1, keepdims=True)
        )
        old = jnp.exp(old - top)
        new = jnp.exp(new - top)
        mass = jnp.sum(old, axis=-1, keepdims=True) + jnp.sum(new, axis=-1, keepdims=True)
        mixed = jnp.dot(
            old.astype(bf16), values_ref[slots, :], preferred_element_type=f32
        ) + jnp.dot(new.astype(bf16), new_values_ref[at, :], preferred_element_type=f32)
        mixed = mixed / mass
        level = top + jnp.log(mass)
        head = [mixed[32 * n : 32 * n + 32] for n in range(6)]
        lane32 = lane_of((32, LANES))
        low32 = lane32 < 64
        att_send[at, 0:128] = jnp.where(low32, head[0], swap_half(head[1])).astype(bf16)
        att_send[at, 128:256] = jnp.where(low32, head[2], head[3]).astype(bf16)
        att_send[at, 256:384] = jnp.where(low32, swap_half(head[4]), head[5]).astype(bf16)
        levels = jnp.zeros((32, LANES), f32)
        for n in range(6):
            levels = jnp.where(lane32 % 8 == n, level[32 * n : 32 * n + 32], levels)
        high = levels.astype(bf16).astype(f32)
        rest = levels - high
        middle = rest.astype(bf16).astype(f32)
        levels = jnp.where(
            lane32 < 8, high, jnp.where(lane32 < 16, middle, rest - middle)
        )
        att_send[at, 384:512] = jnp.where(lane32 < 24, levels, 0.0).astype(bf16)

        if block == 1:
            pl.semaphore_wait(barrier, SEQ + TP - 2)
            copies += send_parts(2) + send_parts(1)
    copies += send_parts(3) + send_parts(0)
    att_recv[me] = att_send[rows_of(me), :]

    loads[8].wait()
    routes_ref[...] = jnp.transpose(
        jnp.concatenate([routes_t_ref[...], jnp.zeros((120, 128), jnp.int32)], axis=0)
    )
    spread_col = lax.broadcasted_iota(jnp.int32, (TILE, EXPERTS * TILE), 1)
    spread_row = lax.broadcasted_iota(jnp.int32, (TILE, EXPERTS * TILE), 0)
    expert_at = jnp.where(spread_col % TILE == spread_row, spread_col // TILE, -1)

    def mark(n, carry):
        routes = routes_ref[rows_of(n), 0:TOP]
        for k in range(TOP):
            hit = routes[:, k : k + 1] == expert_at
            onehot[n, TILE * k : TILE * (k + 1), :] = jnp.where(hit, 1.0, 0.0).astype(bf16)
        return carry

    lax.fori_loop(0, 8, mark, 0, unroll=2)
    half_lane = jnp.where(low, 0, 1)
    for k in range(TOP):
        shifted[k] = routes_ref[:, k : k + 1] - half_lane

    for copy in copies:
        copy.wait()
    own_level = []
    for n in range(SEQ):
        packed = att_recv[n, :, 384:512].astype(f32)
        own_level.append(packed + pltpu.roll(packed, 120, 1) + pltpu.roll(packed, 112, 1))
    top = own_level[0]
    for n in range(1, SEQ):
        top = jnp.maximum(top, own_level[n])
    weights = [jnp.exp(x - top) for x in own_level]
    mass = weights[0]
    for n in range(1, SEQ):
        mass = mass + weights[n]
    low16 = lane_of((TILE, LANES)) < 64
    parts = [jnp.zeros((TILE, LANES), f32) for _ in range(3)]
    for n in range(SEQ):
        share = weights[n] / mass
        for j in range(3):
            wide = jnp.where(low16, share[:, 2 * j : 2 * j + 1], share[:, 2 * j + 1 : 2 * j + 2])
            parts[j] = parts[j] + wide * att_recv[n, :, 128 * j : 128 * j + 128].astype(f32)
    att_all[tp] = jnp.concatenate(parts, axis=-1).astype(bf16)

    copies = [
        tp_copy(step, att_all.at[tp], att_all.at[tp], peer)
        for step, peer in enumerate((core_peer, far_peer, lax.rem(core_peer + 2, TP)))
    ]
    loads[11].wait()
    width = out_w_ref.shape[1]
    residual = tokens_ref[rows_of(me), pl.ds(pl.multiple_of(tp * width, 128), width)].astype(f32)
    for step, group in enumerate((tp, core_peer, far_peer, lax.rem(core_peer + 2, TP))):
        if step > 0:
            copies[step - 1].wait()
        at = pl.ds(pl.multiple_of(group * width, 128), width)
        residual = residual + jnp.dot(
            att_all[group], out_w_ref[at, :], preferred_element_type=f32
        )
    res_own[...] = residual
    res_all[me] = residual.astype(bf16)
    copies = seq_copies(1, lambda peer: res_all.at[me], lambda index: res_all.at[index])
    for copy in copies:
        copy.wait()

    full = res_all[...].reshape(SEQ * TILE, width).astype(f32)
    loads[9].wait()
    loads[10].wait()
    gained = full * moe_gain_ref[...].reshape(1, -1)
    gained_b = gained.astype(bf16)
    rest = (gained - gained_b.astype(f32)).astype(bf16)
    router = router_ref[...]
    logits = lax.dot_general(
        gained_b, router, contract, preferred_element_type=f32
    ) + lax.dot_general(rest, router, contract, preferred_element_type=f32)
    squares = jnp.sum(full * full, axis=-1, keepdims=True)
    logit_rows[...] = jnp.zeros_like(logit_rows)
    logit_rows[:, 0:EXPERTS] = logits
    rows = jnp.where(lane == EXPERTS, squares, logit_rows[...])
    rows = split_pair(jnp.where(low, rows, swap_half(rows)))
    sums[...] = rows
    sums_copy = tp_copy(
        4 + 3 * CHUNKS,
        sums.at[pl.ds(pl.multiple_of(64 * (1 - core), 64), 64), :],
        sums_recv,
        core_peer,
    )

    loads[12].wait()
    loads[13].wait()

    def experts(n, carry):
        weight = pair_w[pl.ds(2 * n, 2)].reshape(2 * LANES, width)
        both = lax.dot_general(
            gained_b, weight, contract, preferred_element_type=f32
        ).astype(bf16)
        dense[2 * n] = both[:, :LANES]
        dense[2 * n + 1] = both[:, LANES:]
        return carry

    lax.fori_loop(0, EXPERTS // 2, experts, 0, unroll=10)

    def pick(n, carry):
        group = dense[:, rows_of(n), :].reshape(EXPERTS * TILE, LANES)
        picks[n, 0 : TOP * TILE, :] = jnp.dot(
            onehot[n], group, preferred_element_type=f32
        ).astype(bf16)
        return carry

    groups = 4 // CHUNKS
    count = groups * TILE
    near, far, back = [], [], []

    def pick_theirs(chunk):
        first = 4 * (1 - core) + groups * chunk
        for n in range(groups):
            pick(first + n, 0)
        at = slice(groups * chunk, groups * (chunk + 1))
        near.append(
            tp_copy(4 + chunk, picks.at[pl.ds(first, groups)], picks_recv.at[at], core_peer)
        )

    def pick_ours(chunk):
        for n in range(groups):
            pick(4 * core + groups * chunk + n, 0)

    def add_near(chunk):
        at = slice(groups * chunk, groups * (chunk + 1))
        mine = pl.ds(4 * core + groups * chunk, groups)
        near[chunk].wait()
        picks_half[at] = (picks[mine].astype(f32) + picks_recv[at].astype(f32)).astype(bf16)
        far.append(
            tp_copy(4 + CHUNKS + chunk, picks_half.at[at], picks_far.at[at], far_peer)
        )

    ours = pl.ds(pl.multiple_of(64 * core, 64), 64)
    pick_theirs(0)
    pick_ours(0)
    for chunk in range(1, CHUNKS):
        pick_theirs(chunk)
        add_near(chunk - 1)
        pick_ours(chunk)
    sums_copy.wait()
    sums_half[...] = split_pair(join_pair(sums[ours, :]) + join_pair(sums_recv[...]))
    sums_copy = tp_copy(5 + 3 * CHUNKS, sums_half, sums_far, far_peer)
    add_near(CHUNKS - 1)

    sums_copy.wait()
    rows = join_pair(sums_half[...]) + join_pair(sums_far[...])
    lanes = lane_of((64, LANES))
    scales = lax.rsqrt(rows[:, EXPERTS : EXPERTS + 1] / D + EPSILON)
    routes = routes_ref[ours, 0:TOP]
    hits = [lanes == routes[:, k : k + 1] for k in range(TOP)]
    routed = hits[0]
    for k in range(1, TOP):
        routed = routed | hits[k]
    scores = jnp.where(routed, rows * scales, FLOOR_SCORE)
    prob = jnp.exp(scores - jnp.max(scores, axis=-1, keepdims=True))
    prob = jnp.where(routed, prob, 0.0)
    prob = prob / jnp.sum(prob, axis=-1, keepdims=True)
    probs = [jnp.sum(jnp.where(hits[k], prob, 0.0), axis=-1, keepdims=True) for k in range(TOP)]
    for k in range(TOP):
        gate_scale[k] = jnp.broadcast_to(probs[k], (64, LANES))
    gate_scale[TOP] = jnp.broadcast_to(scales, (64, LANES))
    low_part = lane_of((count, LANES)) < 64
    for chunk in range(CHUNKS):
        at = slice(groups * chunk, groups * (chunk + 1))
        mine = pl.ds(4 * core + groups * chunk, groups)
        part = slice(count * chunk, count * (chunk + 1))
        far[chunk].wait()
        scale = gate_scale[TOP, part, :]
        for k in range(TOP):
            of = slice(TILE * k, TILE * (k + 1))
            both = (picks_half[at, of, :].astype(f32) + picks_far[at, of, :].astype(f32)).reshape(
                count, LANES
            ) * scale
            active = both / (1.0 + jnp.exp(-both)) * swap_half(both)
            active = active.astype(bf16).astype(f32) * gate_scale[k, part, :]
            active = jnp.where(low_part, active, swap_half(active))
            scaled[mine, of, :] = active.astype(bf16).reshape(groups, TILE, LANES)
        back.append(
            tp_copy(4 + 2 * CHUNKS + chunk, scaled.at[mine], scaled.at[mine], core_peer)
        )

    def spread_rows(n):
        values = [
            scaled[n, TILE * k : TILE * (k + 1), :].astype(f32) for k in range(TOP)
        ]
        routes = [shifted[k, rows_of(n), :] for k in range(TOP)]
        for pair in range(EXPERTS // 2):
            one = jnp.zeros((TILE, LANES), f32)
            for k in range(TOP):
                one = jnp.where(routes[k] == 2 * pair, values[k], one)
            spread[rows_of(n), LANES * pair : LANES * (pair + 1)] = one.astype(bf16)

    for n in range(4):
        spread_rows(4 * core + n)
    loads[14].wait()
    for chunk in range(CHUNKS):
        back[chunk].wait()
        for n in range(groups):
            spread_rows(4 * (1 - core) + groups * chunk + n)
    total[...] = jnp.dot(
        spread[...], down_ref[...].reshape(EXPERTS * hidden, width), preferred_element_type=f32
    )
    part_send[...] = total[...].astype(bf16)

    copies = seq_copies(
        2, lambda peer: part_send.at[rows_of(peer), :], lambda index: part_recv.at[index]
    )
    result = res_own[...] + total[rows_of(me), :]
    for copy in copies:
        copy.wait()
    part_recv[me] = jnp.zeros((TILE, width), bf16)
    for n in range(SEQ):
        result = result + part_recv[n].astype(f32)
    out_own[...] = result.astype(bf16)
    out_ref[rows_of(me), :] = out_own[...]
    copies = seq_copies(3, lambda peer: out_own, lambda index: out_ref.at[rows_of(index), :])
    for copy in copies:
        copy.wait()


def fused_device(
    tokens,
    attn_gain,
    qkv_weight,
    out_weight,
    moe_gain,
    router_weight,
    expert_gate,
    expert_up,
    expert_down,
    cache_keys,
    cache_values,
    lengths,
    routes,
):
    count = tokens.shape[0]
    width = out_weight.shape[1]
    requests, slot_count = cache_keys.shape[:2]
    vmem = pl.BlockSpec(memory_space=pltpu.VMEM)
    hbm = pl.BlockSpec(memory_space=pltpu.HBM)
    bf16, f32 = jnp.bfloat16, jnp.float32
    hidden = expert_gate.shape[2]
    return pl.pallas_call(
        layer_kernel,
        out_shape=pltpu.VMEM((count, width), bf16),
        in_specs=[hbm] * 13,
        out_specs=vmem,
        scratch_shapes=[
            pltpu.VMEM(tokens.shape, bf16),
            pltpu.VMEM((D,), f32),
            pltpu.VMEM((width,), f32),
            pltpu.VMEM((1, requests), jnp.int32),
            pltpu.VMEM((TOP, count), jnp.int32),
            pltpu.VMEM((EXPERTS, width), bf16),
            pltpu.VMEM((count, count), jnp.int32),
            pltpu.VMEM(qkv_weight.shape, bf16),
            pltpu.VMEM((requests * slot_count, LANES), bf16),
            pltpu.VMEM((requests * slot_count, LANES), bf16),
            pltpu.VMEM(out_weight.shape, bf16),
            pltpu.VMEM(expert_down.shape, bf16),
            pltpu.VMEM((count, 512), bf16),
            pltpu.VMEM((SEQ, TILE, 512), bf16),
            pltpu.VMEM((TP, TILE, width), bf16),
            pltpu.VMEM((TILE, width), f32),
            pltpu.VMEM((SEQ, TILE, width), bf16),
            pltpu.VMEM((EXPERTS, 2 * hidden, width), bf16),
            pltpu.VMEM((EXPERTS, count, LANES), bf16),
            pltpu.VMEM((8, TOP * TILE, EXPERTS * TILE), bf16),
            pltpu.VMEM((TOP, count, LANES), jnp.int32),
            pltpu.VMEM((8, TOP * TILE, LANES), bf16),
            pltpu.VMEM((4, TOP * TILE, LANES), bf16),
            pltpu.VMEM((4, TOP * TILE, LANES), bf16),
            pltpu.VMEM((4, TOP * TILE, LANES), bf16),
            pltpu.VMEM((count, LANES), f32),
            pltpu.VMEM((count, LANES), bf16),
            pltpu.VMEM((64, LANES), bf16),
            pltpu.VMEM((64, LANES), bf16),
            pltpu.VMEM((64, LANES), bf16),
            pltpu.VMEM((TOP + 1, 64, LANES), f32),
            pltpu.VMEM((6, count, LANES), bf16),
            pltpu.VMEM((count, LANES), bf16),
            pltpu.VMEM((count, LANES), bf16),
            pltpu.VMEM((count, LANES), f32),
            pltpu.VMEM((8, TOP * TILE, LANES), bf16),
            pltpu.VMEM((count, EXPERTS * hidden), bf16),
            pltpu.VMEM((count, width), f32),
            pltpu.VMEM((count, width), bf16),
            pltpu.VMEM((SEQ, TILE, width), bf16),
            pltpu.VMEM((TILE, width), bf16),
            pltpu.SemaphoreType.DMA((15,)),
            pltpu.SemaphoreType.DMA((4, SEQ)),
            pltpu.SemaphoreType.DMA((4, SEQ)),
            pltpu.SemaphoreType.DMA((6 + 3 * CHUNKS,)),
            pltpu.SemaphoreType.DMA((6 + 3 * CHUNKS,)),
        ],
        compiler_params=pltpu.CompilerParams(
            collective_id=0, has_side_effects=True, vmem_limit_bytes=VMEM_LIMIT
        ),
        cost_estimate=pl.CostEstimate(
            flops=2_000_000_000, bytes_accessed=20_000_000, transcendentals=1_000_000
        ),
        name="layer",
    )(
        tokens,
        attn_gain,
        moe_gain,
        lengths.reshape(1, -1),
        routes.T,
        router_weight.T,
        qkv_weight,
        cache_keys.reshape(-1, LANES),
        cache_values.reshape(-1, LANES),
        out_weight,
        jnp.swapaxes(expert_gate, 1, 2),
        jnp.swapaxes(expert_up, 1, 2),
        expert_down,
    )


def solution(mesh):
    in_specs = (
        P(),
        P(),
        P(None, "tp"),
        P(None, "tp"),
        P("tp"),
        P("tp", None),
        P(None, "tp", "seq"),
        P(None, "tp", "seq"),
        P(None, "seq", "tp"),
        P(None, "seq", "tp"),
        P(None, "seq", "tp"),
        P(),
        P(),
    )
    out_specs = P(None, "tp")
    body = fused_device if fits_fused(mesh) else on_device
    return jax.shard_map(
        body, mesh=mesh, in_specs=in_specs, out_specs=out_specs, check_vma=False
    )
```

```python
import jax
import jax.numpy as jnp
import numpy as np
from jax import lax
from jax.experimental import pallas as pl
from jax.experimental.pallas import tpu as pltpu
from jax.sharding import PartitionSpec as P

D = 1536
HEAD = 64
EXPERTS = 40
SINK = 4
NEW = 4
GROUP = 3


EPSILON = 1e-06
ROPE_BASE = 10000.0
FLOOR_SCORE = -1e30


def joined(shard, axis, combine):
    everything = jax.tree.map(lambda part: lax.all_gather(part, axis), shard)
    initial = jax.tree.map(lambda part: part[0], everything)

    def lap(k, so_far):
        return combine(so_far, jax.tree.map(lambda part: part[k], everything))

    return lax.fori_loop(1, lax.axis_size(axis), lap, initial)


def rms_scale(values, gain):
    return values * lax.rsqrt(jnp.mean(values * values, axis=-1, keepdims=True) + EPSILON) * gain


def rotate(values, places):
    half_dim = values.shape[-1] // 2
    freqs = jnp.exp(-jnp.log(ROPE_BASE) * jnp.arange(half_dim, dtype=jnp.float32) / half_dim)
    angles = places.reshape((-1,) + (1,) * (values.ndim - 1)) * freqs
    cosine = jnp.cos(angles)
    sine = jnp.sin(angles)
    first = values[..., :half_dim]
    second = values[..., half_dim:]
    return jnp.concatenate(
        [first * cosine - second * sine, first * sine + second * cosine], axis=-1
    )


def visible(slots, lengths, window):
    lens = lengths[:, None]
    slot_row = slots[None, :]
    live = slot_row < lens
    older = lens - 1 - jnp.mod(lens - 1 - slot_row, window)
    placed = jnp.where(slot_row < SINK, slot_row, older)
    offsets = jnp.arange(NEW, dtype=jnp.int32)
    inside = (slot_row[:, None, :] < SINK) | (
        placed[:, None, :] >= lens[:, :, None] + offsets[None, :, None] - window
    )
    return live[:, None, :] & inside


def combine_parts(earlier, later):
    top_a, mass_a, weighted_a = earlier
    top_b, mass_b, weighted_b = later
    top_both = jnp.maximum(top_a, top_b)
    factor_a = jnp.exp(top_a - top_both)
    factor_b = jnp.exp(top_b - top_both)
    return (
        top_both,
        mass_a * factor_a + mass_b * factor_b,
        weighted_a * factor_a[..., None] + weighted_b * factor_b[..., None],
    )


def on_device(
    tokens,
    attn_gain,
    qkv_weight,
    out_weight,
    moe_gain,
    router_weight,
    expert_gate,
    expert_up,
    expert_down,
    cache_keys,
    cache_values,
    lengths,
    routes,
):
    seq_count = lax.axis_size("seq")
    seq_index = lax.axis_index("seq")
    tp_index = lax.axis_index("tp")
    token_count = tokens.shape[0]
    requests = cache_keys.shape[0]
    slot_count = cache_keys.shape[1]
    window = slot_count * seq_count - SINK
    local_kv = cache_keys.shape[2] // HEAD
    token_full = tokens.astype(jnp.float32)
    normed = rms_scale(token_full, attn_gain).astype(jnp.bfloat16)
    projected = jnp.dot(normed, qkv_weight, preferred_element_type=jnp.float32)
    projected = projected.reshape(token_count, local_kv, GROUP + 2, HEAD)
    places = (
        (lengths[:, None] + jnp.arange(NEW, dtype=jnp.int32)[None, :])
        .reshape(token_count)
        .astype(jnp.float32)
    )
    queries = rotate(projected[:, :, :GROUP], places).astype(jnp.bfloat16)
    new_keys = rotate(projected[:, :, GROUP], places).astype(jnp.bfloat16)
    new_values = projected[:, :, GROUP + 1].astype(jnp.bfloat16)
    query_b = queries.reshape(requests, NEW, local_kv, GROUP, HEAD)
    key_new = new_keys.reshape(requests, NEW, local_kv, HEAD)
    value_new = new_values.reshape(requests, NEW, local_kv, HEAD)
    slots = seq_index * slot_count + jnp.arange(slot_count, dtype=jnp.int32)
    seen = visible(slots, lengths, window)[:, :, None, None, :]
    factor = 1.0 / HEAD**0.5
    key_old = cache_keys.reshape(requests, slot_count, local_kv, HEAD)
    value_old = cache_values.reshape(requests, slot_count, local_kv, HEAD)
    old_scores = (
        jnp.einsum("rtgqd,rsgd->rtgqs", query_b, key_old, preferred_element_type=jnp.float32)
        * factor
    )
    new_scores = (
        jnp.einsum("rtgqd,rugd->rtgqu", query_b, key_new, preferred_element_type=jnp.float32)
        * factor
    )
    causal = jnp.arange(NEW)[:, None] >= jnp.arange(NEW)[None, :]
    own_mask = causal[None, :, None, None, :] & (seq_index == 0)
    old_masked = jnp.where(seen, old_scores, FLOOR_SCORE)
    new_masked = jnp.where(own_mask, new_scores, FLOOR_SCORE)
    top_score = jnp.maximum(jnp.max(old_masked, axis=-1), jnp.max(new_masked, axis=-1))
    old_weights = jnp.where(seen, jnp.exp(old_masked - top_score[..., None]), 0.0)
    new_weights = jnp.where(own_mask, jnp.exp(new_masked - top_score[..., None]), 0.0)
    mass = jnp.sum(old_weights, axis=-1) + jnp.sum(new_weights, axis=-1)
    weighted = jnp.einsum(
        "rtgqs,rsgd->rtgqd", old_weights, value_old.astype(jnp.float32)
    ) + jnp.einsum("rtgqu,rugd->rtgqd", new_weights, value_new.astype(jnp.float32))
    top_score, mass, weighted = joined((top_score, mass, weighted), "seq", combine_parts)
    attended = (weighted / mass[..., None]).reshape(token_count, -1).astype(jnp.bfloat16)
    feature_part = out_weight.shape[1]
    attn_out = jnp.dot(
        lax.all_gather(attended, "tp", axis=1, tiled=True),
        out_weight,
        preferred_element_type=jnp.float32,
    )
    residual = (
        lax.dynamic_slice_in_dim(token_full, tp_index * feature_part, feature_part, 1) + attn_out
    )
    gained = residual * moe_gain
    squares_local = jnp.sum(residual * residual, axis=-1)
    router_f = router_weight.astype(jnp.float32)
    squares_total = lax.psum(squares_local, "tp")
    scale = lax.rsqrt(squares_total / D + EPSILON)
    logits = lax.psum(
        jnp.dot(gained * scale[:, None], router_f, precision=lax.Precision.HIGHEST), "tp"
    )
    moe_in = (gained * scale[:, None]).astype(jnp.bfloat16)
    chosen = jnp.take_along_axis(logits, routes, axis=1)
    gate_prob = jax.nn.softmax(chosen, axis=-1)
    gate_part = jnp.einsum("td,edf->tef", moe_in, expert_gate, preferred_element_type=jnp.float32)
    up_part = jnp.einsum("td,edf->tef", moe_in, expert_up, preferred_element_type=jnp.float32)
    gate_pick = jnp.take_along_axis(gate_part, routes[:, :, None], axis=1)
    up_pick = jnp.take_along_axis(up_part, routes[:, :, None], axis=1)
    gate_sum, up_sum = (
        lax.psum(gate_pick.astype(jnp.bfloat16), "tp").astype(jnp.float32),
        lax.psum(up_pick.astype(jnp.bfloat16), "tp").astype(jnp.float32),
    )
    activated = (jax.nn.silu(gate_sum) * up_sum).astype(jnp.bfloat16)
    scaled = (gate_prob[:, :, None] * activated.astype(jnp.float32)).astype(jnp.bfloat16)
    onehot = (routes[:, :, None] == jnp.arange(EXPERTS, dtype=jnp.int32)[None, None, :]).astype(
        jnp.bfloat16
    )
    spread = jnp.einsum("tke,tkf->tef", onehot, scaled, preferred_element_type=jnp.float32).astype(
        jnp.bfloat16
    )
    moe_part = jnp.einsum("tef,efd->td", spread, expert_down, preferred_element_type=jnp.float32)
    moe_out = lax.psum(moe_part, "seq")
    return (residual + moe_out).astype(jnp.bfloat16)


TOP = 8
TILE = 16
LANES = 128
SEQ = 8
TP = 4
MESH = pl.DeviceIdType.MESH
CHUNKS = 2
VMEM_LIMIT = 61 * 1024 * 1024
TURN = 6.28125
TURN_MIDDLE = 0.0019350051879882812
TURN_REST = 3.0199159819568123e-07


def fits_fused(mesh):
    return mesh.shape["seq"] == SEQ and mesh.shape["tp"] == TP


def lane_of(shape):
    return lax.broadcasted_iota(jnp.int32, shape, len(shape) - 1)


def swap_half(values):
    return pltpu.roll(values, 64, 1)


def split_pair(values):
    high = values.astype(jnp.bfloat16).astype(jnp.float32)
    return jnp.where(lane_of(values.shape) < 64, high, values - high).astype(jnp.bfloat16)


def join_pair(packed):
    values = packed.astype(jnp.float32)
    return values + swap_half(values)


def circle(angles):
    half = angles * 0.5
    square = half * half
    sine = jnp.full_like(square, 1.0 / 6227020800.0)
    cosine = jnp.full_like(square, -1.0 / 87178291200.0)
    for term in (-39916800.0, 362880.0, -5040.0, 120.0, -6.0, 1.0):
        sine = sine * square + 1.0 / term
    for term in (479001600.0, -3628800.0, 40320.0, -720.0, 24.0, -2.0, 1.0):
        cosine = cosine * square + 1.0 / term
    sine = sine * half
    return 1.0 - 2.0 * sine * sine, 2.0 * sine * cosine


def layer_kernel(
    tokens_hbm,
    attn_gain_hbm,
    moe_gain_hbm,
    lengths_hbm,
    routes_hbm,
    router_hbm,
    qkv_hbm,
    keys_hbm,
    values_hbm,
    out_w_hbm,
    gate_hbm,
    up_hbm,
    down_hbm,
    out_ref,
    tokens_ref,
    attn_gain_ref,
    moe_gain_ref,
    lengths_ref,
    routes_t_ref,
    router_ref,
    routes_ref,
    qkv_ref,
    keys_ref,
    values_ref,
    out_w_ref,
    down_ref,
    att_send,
    att_recv,
    att_all,
    res_own,
    res_all,
    pair_w,
    turned_w,
    dense,
    onehot,
    shifted,
    picks,
    picks_recv,
    picks_half,
    picks_far,
    logit_rows,
    sums,
    sums_recv,
    sums_half,
    sums_far,
    gate_scale,
    queries_ref,
    new_keys_ref,
    new_values_ref,
    lens_ref,
    scaled,
    spread,
    total,
    part_send,
    part_recv,
    out_own,
    local_sem,
    seq_send,
    seq_recv,
    tp_send,
    tp_recv,
):
    me = lax.axis_index("seq")
    tp = lax.axis_index("tp")
    core = lax.rem(tp, 2)
    core_peer = tp + 1 - 2 * core
    far_peer = lax.rem(tp + 2, TP)
    f32, bf16 = jnp.float32, jnp.bfloat16

    barrier = pltpu.get_barrier_semaphore()
    for step in range(1, SEQ):
        pl.semaphore_signal(
            barrier, inc=1, device_id=(lax.rem(me + step, SEQ), tp), device_id_type=MESH
        )
    for step in range(1, TP):
        pl.semaphore_signal(
            barrier, inc=1, device_id=(me, lax.rem(tp + step, TP)), device_id_type=MESH
        )

    depth = qkv_ref.shape[0] // 3
    hidden = gate_hbm.shape[1]
    wanted = [
        (lengths_hbm, lengths_ref),
        (tokens_hbm, tokens_ref),
        (attn_gain_hbm, attn_gain_ref),
        (qkv_hbm.at[0:depth], qkv_ref.at[0:depth]),
        (qkv_hbm.at[depth : 2 * depth], qkv_ref.at[depth : 2 * depth]),
        (qkv_hbm.at[2 * depth :], qkv_ref.at[2 * depth :]),
        (keys_hbm, keys_ref),
        (values_hbm, values_ref),
        (routes_hbm, routes_t_ref),
        (moe_gain_hbm, moe_gain_ref),
        (router_hbm, router_ref),
        (out_w_hbm, out_w_ref),
        (gate_hbm, pair_w.at[:, 0:hidden, :]),
        (up_hbm, pair_w.at[:, hidden:, :]),
        (down_hbm, down_ref),
    ]
    loads = [
        pltpu.make_async_copy(src, dst, local_sem.at[n]) for n, (src, dst) in enumerate(wanted)
    ]
    for load in loads[:8]:
        load.start()

    def seq_copies(phase, source, target):
        copies = []
        for step in range(1, SEQ):
            peer = lax.rem(me + step, SEQ)
            copies.append(
                pltpu.make_async_remote_copy(
                    src_ref=source(peer),
                    dst_ref=target(me),
                    send_sem=seq_send.at[phase, step],
                    recv_sem=seq_recv.at[phase, step],
                    device_id=(peer, tp),
                    device_id_type=MESH,
                )
            )
        for copy in copies:
            copy.start()
        return copies

    def tp_copy(slot, source, target, peer):
        copy = pltpu.make_async_remote_copy(
            src_ref=source,
            dst_ref=target,
            send_sem=tp_send.at[slot],
            recv_sem=tp_recv.at[slot],
            device_id=(me, peer),
            device_id_type=MESH,
        )
        copy.start()
        return copy

    def rows_of(index):
        return pl.ds(pl.multiple_of(index * TILE, TILE), TILE)

    loads[0].wait()
    request = lax.broadcasted_iota(jnp.int32, (128, 32), 0) // NEW
    picked = request == lane_of((128, 32))
    lens = jnp.sum(
        jnp.where(picked, lengths_ref[...].astype(f32), 0.0), axis=-1, keepdims=True
    )
    lane = lane_of((128, LANES))
    low = lane < 64
    token = lax.broadcasted_iota(jnp.int32, (128, LANES), 0)
    half = HEAD // 2
    table = np.exp(-np.log(np.float32(ROPE_BASE)) * np.arange(half, dtype=np.float32) / half)
    lane1 = lane_of((1, LANES)) % half
    freqs = jnp.zeros((1, LANES), f32)
    for n in range(half):
        freqs = jnp.where(lane1 == n, float(table[n]), freqs)
    angles = (lens + (token % NEW).astype(f32)) * freqs
    turns = jnp.floor(angles * (1.0 / (2 * np.pi)) + 0.5)
    angles = ((angles - turns * TURN) - turns * TURN_MIDDLE) - turns * TURN_REST
    cosine, sine = circle(angles)
    sine = jnp.where(lane % HEAD < half, -sine, sine)

    loads[1].wait()
    loads[2].wait()
    token_full = tokens_ref[...].astype(f32)
    normed = rms_scale(token_full, attn_gain_ref[...].reshape(1, -1)).astype(bf16)
    projected = jnp.zeros((128, qkv_ref.shape[1]), f32)
    for n in range(3):
        at = slice(depth * n, depth * (n + 1))
        loads[3 + n].wait()
        projected = projected + jnp.dot(normed[:, at], qkv_ref[at, :], preferred_element_type=f32)
    for load in loads[8:]:
        load.start()
    tiles = [projected[:, LANES * n : LANES * (n + 1)] for n in range(5)]

    def turned(x):
        swapped = jnp.where(lane % 64 < 32, pltpu.roll(x, 96, 1), pltpu.roll(x, 32, 1))
        return x * cosine + swapped * sine

    turn = [turned(x) for x in tiles]
    factor = 1.0 / HEAD**0.5
    queries = [
        jnp.where(low, turn[0], 0.0),
        jnp.where(low, swap_half(turn[0]), 0.0),
        jnp.where(low, turn[1], 0.0),
        jnp.where(low, 0.0, turn[2]),
        jnp.where(low, 0.0, swap_half(turn[3])),
        jnp.where(low, 0.0, turn[3]),
    ]
    for n in range(6):
        queries_ref[n] = (queries[n] * factor).astype(bf16)
    new_keys_ref[...] = jnp.where(low, swap_half(turn[1]), swap_half(turn[4])).astype(bf16)
    new_values_ref[...] = jnp.where(low, tiles[2], tiles[4]).astype(bf16)
    lens_ref[...] = jnp.broadcast_to(lens, (128, LANES))

    loads[6].wait()
    loads[7].wait()
    slot_count = keys_hbm.shape[0] // 32
    window = float(slot_count * SEQ - SINK)
    col256 = lane_of((32, 8 * slot_count))
    row256 = lax.broadcasted_iota(jnp.int32, (32, 8 * slot_count), 0)
    same = row256 // NEW == col256 // slot_count
    slot = (me * slot_count + col256 % slot_count).astype(f32)
    offset = (row256 % NEW).astype(f32)
    row32 = lax.broadcasted_iota(jnp.int32, (32, 32), 0)
    col32 = lax.broadcasted_iota(jnp.int32, (32, 32), 1)
    own = (row32 // NEW == col32 // NEW) & (col32 <= row32) & (me == 0)
    own_bias = jnp.where(own, 0.0, FLOOR_SCORE).astype(f32)
    own_bias = jnp.concatenate([own_bias] * 6, axis=0)
    contract = (((1,), (1,)), ((), ()))
    place, side = me // 2, lax.rem(me, 2)

    def send_parts(shift):
        sent = []
        for turned_side in range(2):
            if shift == 0 and turned_side == 0:
                continue
            peer = 2 * lax.rem(place + shift, 4) + lax.rem(side + turned_side, 2)
            copy = pltpu.make_async_remote_copy(
                src_ref=att_send.at[rows_of(peer), :],
                dst_ref=att_recv.at[me],
                send_sem=seq_send.at[0, 2 * shift + turned_side],
                recv_sem=seq_recv.at[0, 2 * shift + turned_side],
                device_id=(peer, tp),
                device_id_type=MESH,
            )
            copy.start()
            sent.append(copy)
        return sent

    copies = []
    for block in (2, 1, 3, 0):
        number = lax.rem(place + block, 4)
        at = pl.ds(pl.multiple_of(32 * number, 32), 32)
        slots = pl.ds(pl.multiple_of(256 * number, 256), 256)
        query = queries_ref[:, at, :].reshape(192, LANES)
        last = lens_ref[at, 0:1] - 1.0
        back = last - slot
        older = last - (back - window * jnp.floor((back + 0.5) * (1.0 / window)))
        seen = (slot <= last) & ((slot < SINK) | (older > last + offset - window))
        old_bias = jnp.where(seen & same, 0.0, FLOOR_SCORE).astype(f32)
        old_bias = jnp.concatenate([old_bias] * 6, axis=0)
        old = lax.dot_general(query, keys_ref[slots, :], contract, preferred_element_type=f32)
        new = lax.dot_general(query, new_keys_ref[at, :], contract, preferred_element_type=f32)
        old = old + old_bias
        new = new + own_bias
        top = jnp.maximum(
            jnp.max(old, axis=-1, keepdims=True), jnp.max(new, axis=-1, keepdims=True)
        )
        old = jnp.exp(old - top)
        new = jnp.exp(new - top)
        mass = jnp.sum(old, axis=-1, keepdims=True) + jnp.sum(new, axis=-1, keepdims=True)
        mixed = jnp.dot(
            old.astype(bf16), values_ref[slots, :], preferred_element_type=f32
        ) + jnp.dot(new.astype(bf16), new_values_ref[at, :], preferred_element_type=f32)
        mixed = mixed / mass
        level = top + jnp.log(mass)
        head = [mixed[32 * n : 32 * n + 32] for n in range(6)]
        lane32 = lane_of((32, LANES))
        low32 = lane32 < 64
        att_send[at, 0:128] = jnp.where(low32, head[0], swap_half(head[1])).astype(bf16)
        att_send[at, 128:256] = jnp.where(low32, head[2], head[3]).astype(bf16)
        att_send[at, 256:384] = jnp.where(low32, swap_half(head[4]), head[5]).astype(bf16)
        levels = jnp.zeros((32, LANES), f32)
        for n in range(6):
            levels = jnp.where(lane32 % 8 == n, level[32 * n : 32 * n + 32], levels)
        high = levels.astype(bf16).astype(f32)
        rest = levels - high
        middle = rest.astype(bf16).astype(f32)
        levels = jnp.where(
            lane32 < 8, high, jnp.where(lane32 < 16, middle, rest - middle)
        )
        att_send[at, 384:512] = jnp.where(lane32 < 24, levels, 0.0).astype(bf16)

        if block == 1:
            pl.semaphore_wait(barrier, SEQ + TP - 2)
            copies += send_parts(2) + send_parts(1)
    copies += send_parts(3) + send_parts(0)
    att_recv[me] = att_send[rows_of(me), :]

    loads[8].wait()
    routes_ref[...] = jnp.transpose(
        jnp.concatenate([routes_t_ref[...], jnp.zeros((120, 128), jnp.int32)], axis=0)
    )
    spread_col = lax.broadcasted_iota(jnp.int32, (TILE, EXPERTS * TILE), 1)
    spread_row = lax.broadcasted_iota(jnp.int32, (TILE, EXPERTS * TILE), 0)
    expert_at = jnp.where(spread_col % TILE == spread_row, spread_col // TILE, -1)

    def mark(n, carry):
        routes = routes_ref[rows_of(n), 0:TOP]
        for k in range(TOP):
            hit = routes[:, k : k + 1] == expert_at
            onehot[n, TILE * k : TILE * (k + 1), :] = jnp.where(hit, 1.0, 0.0).astype(bf16)
        return carry

    lax.fori_loop(0, 8, mark, 0, unroll=2)
    loads[12].wait()
    loads[13].wait()

    def turn_pair(n, carry):
        turned_w[n] = jnp.transpose(pair_w[pl.ds(2 * n, 2)].reshape(2 * LANES, -1))
        return carry

    lax.fori_loop(0, EXPERTS // 4, turn_pair, 0, unroll=2)
    half_lane = jnp.where(low, 0, 1)
    for k in range(TOP):
        shifted[k] = routes_ref[:, k : k + 1] - half_lane

    for copy in copies:
        copy.wait()
    own_level = []
    for n in range(SEQ):
        packed = att_recv[n, :, 384:512].astype(f32)
        own_level.append(packed + pltpu.roll(packed, 120, 1) + pltpu.roll(packed, 112, 1))
    top = own_level[0]
    for n in range(1, SEQ):
        top = jnp.maximum(top, own_level[n])
    weights = [jnp.exp(x - top) for x in own_level]
    mass = weights[0]
    for n in range(1, SEQ):
        mass = mass + weights[n]
    low16 = lane_of((TILE, LANES)) < 64
    parts = [jnp.zeros((TILE, LANES), f32) for _ in range(3)]
    for n in range(SEQ):
        share = weights[n] / mass
        for j in range(3):
            wide = jnp.where(low16, share[:, 2 * j : 2 * j + 1], share[:, 2 * j + 1 : 2 * j + 2])
            parts[j] = parts[j] + wide * att_recv[n, :, 128 * j : 128 * j + 128].astype(f32)
    att_all[tp] = jnp.concatenate(parts, axis=-1).astype(bf16)

    copies = [
        tp_copy(step, att_all.at[tp], att_all.at[tp], peer)
        for step, peer in enumerate((core_peer, far_peer, lax.rem(core_peer + 2, TP)))
    ]
    loads[11].wait()
    width = out_w_ref.shape[1]
    residual = tokens_ref[rows_of(me), pl.ds(pl.multiple_of(tp * width, 128), width)].astype(f32)
    for step, group in enumerate((tp, core_peer, far_peer, lax.rem(core_peer + 2, TP))):
        if step > 0:
            copies[step - 1].wait()
        at = pl.ds(pl.multiple_of(group * width, 128), width)
        residual = residual + jnp.dot(
            att_all[group], out_w_ref[at, :], preferred_element_type=f32
        )
    res_own[...] = residual
    res_all[me] = residual.astype(bf16)
    copies = seq_copies(1, lambda peer: res_all.at[me], lambda index: res_all.at[index])
    lax.fori_loop(EXPERTS // 4, EXPERTS // 2, turn_pair, 0, unroll=2)
    for copy in copies:
        copy.wait()

    full = res_all[...].reshape(SEQ * TILE, width).astype(f32)
    loads[9].wait()
    loads[10].wait()
    gained = full * moe_gain_ref[...].reshape(1, -1)
    gained_b = gained.astype(bf16)
    rest = (gained - gained_b.astype(f32)).astype(bf16)
    router = router_ref[...]
    logits = lax.dot_general(
        gained_b, router, contract, preferred_element_type=f32
    ) + lax.dot_general(rest, router, contract, preferred_element_type=f32)
    squares = jnp.sum(full * full, axis=-1, keepdims=True)
    logit_rows[...] = jnp.zeros_like(logit_rows)
    logit_rows[:, 0:EXPERTS] = logits
    rows = jnp.where(lane == EXPERTS, squares, logit_rows[...])
    rows = split_pair(jnp.where(low, rows, swap_half(rows)))
    sums[...] = rows
    sums_copy = tp_copy(
        4 + 3 * CHUNKS,
        sums.at[pl.ds(pl.multiple_of(64 * (1 - core), 64), 64), :],
        sums_recv,
        core_peer,
    )

    def experts(n, carry):
        both = jnp.dot(gained_b, turned_w[n], preferred_element_type=f32).astype(bf16)
        dense[2 * n] = both[:, :LANES]
        dense[2 * n + 1] = both[:, LANES:]
        return carry

    lax.fori_loop(0, EXPERTS // 2, experts, 0, unroll=10)

    def pick(n, carry):
        group = dense[:, rows_of(n), :].reshape(EXPERTS * TILE, LANES)
        picks[n, 0 : TOP * TILE, :] = jnp.dot(
            onehot[n], group, preferred_element_type=f32
        ).astype(bf16)
        return carry

    groups = 4 // CHUNKS
    count = groups * TILE
    near, far, back = [], [], []

    def pick_theirs(chunk):
        first = 4 * (1 - core) + groups * chunk
        for n in range(groups):
            pick(first + n, 0)
        at = slice(groups * chunk, groups * (chunk + 1))
        near.append(
            tp_copy(4 + chunk, picks.at[pl.ds(first, groups)], picks_recv.at[at], core_peer)
        )

    def pick_ours(chunk):
        for n in range(groups):
            pick(4 * core + groups * chunk + n, 0)

    def add_near(chunk):
        at = slice(groups * chunk, groups * (chunk + 1))
        mine = pl.ds(4 * core + groups * chunk, groups)
        near[chunk].wait()
        picks_half[at] = (picks[mine].astype(f32) + picks_recv[at].astype(f32)).astype(bf16)
        far.append(
            tp_copy(4 + CHUNKS + chunk, picks_half.at[at], picks_far.at[at], far_peer)
        )

    ours = pl.ds(pl.multiple_of(64 * core, 64), 64)
    pick_theirs(0)
    pick_ours(0)
    for chunk in range(1, CHUNKS):
        pick_theirs(chunk)
        add_near(chunk - 1)
        pick_ours(chunk)
    sums_copy.wait()
    sums_half[...] = split_pair(join_pair(sums[ours, :]) + join_pair(sums_recv[...]))
    sums_copy = tp_copy(5 + 3 * CHUNKS, sums_half, sums_far, far_peer)
    add_near(CHUNKS - 1)

    sums_copy.wait()
    rows = join_pair(sums_half[...]) + join_pair(sums_far[...])
    lanes = lane_of((64, LANES))
    scales = lax.rsqrt(rows[:, EXPERTS : EXPERTS + 1] / D + EPSILON)
    routes = routes_ref[ours, 0:TOP]
    hits = [lanes == routes[:, k : k + 1] for k in range(TOP)]
    routed = hits[0]
    for k in range(1, TOP):
        routed = routed | hits[k]
    scores = jnp.where(routed, rows * scales, FLOOR_SCORE)
    prob = jnp.exp(scores - jnp.max(scores, axis=-1, keepdims=True))
    prob = jnp.where(routed, prob, 0.0)
    prob = prob / jnp.sum(prob, axis=-1, keepdims=True)
    probs = [jnp.sum(jnp.where(hits[k], prob, 0.0), axis=-1, keepdims=True) for k in range(TOP)]
    for k in range(TOP):
        gate_scale[k] = jnp.broadcast_to(probs[k], (64, LANES))
    gate_scale[TOP] = jnp.broadcast_to(scales, (64, LANES))
    low_part = lane_of((count, LANES)) < 64
    for chunk in range(CHUNKS):
        at = slice(groups * chunk, groups * (chunk + 1))
        mine = pl.ds(4 * core + groups * chunk, groups)
        part = slice(count * chunk, count * (chunk + 1))
        far[chunk].wait()
        scale = gate_scale[TOP, part, :]
        for k in range(TOP):
            of = slice(TILE * k, TILE * (k + 1))
            both = (picks_half[at, of, :].astype(f32) + picks_far[at, of, :].astype(f32)).reshape(
                count, LANES
            ) * scale
            active = both / (1.0 + jnp.exp(-both)) * swap_half(both)
            active = active.astype(bf16).astype(f32) * gate_scale[k, part, :]
            active = jnp.where(low_part, active, swap_half(active))
            scaled[mine, of, :] = active.astype(bf16).reshape(groups, TILE, LANES)
        back.append(
            tp_copy(4 + 2 * CHUNKS + chunk, scaled.at[mine], scaled.at[mine], core_peer)
        )

    def spread_rows(n):
        values = [
            scaled[n, TILE * k : TILE * (k + 1), :].astype(f32) for k in range(TOP)
        ]
        routes = [shifted[k, rows_of(n), :] for k in range(TOP)]
        for pair in range(EXPERTS // 2):
            one = jnp.zeros((TILE, LANES), f32)
            for k in range(TOP):
                one = jnp.where(routes[k] == 2 * pair, values[k], one)
            spread[rows_of(n), LANES * pair : LANES * (pair + 1)] = one.astype(bf16)

    for n in range(4):
        spread_rows(4 * core + n)
    loads[14].wait()
    for chunk in range(CHUNKS):
        back[chunk].wait()
        for n in range(groups):
            spread_rows(4 * (1 - core) + groups * chunk + n)
    total[...] = jnp.dot(
        spread[...], down_ref[...].reshape(EXPERTS * hidden, width), preferred_element_type=f32
    )
    part_send[...] = total[...].astype(bf16)

    copies = seq_copies(
        2, lambda peer: part_send.at[rows_of(peer), :], lambda index: part_recv.at[index]
    )
    result = res_own[...] + total[rows_of(me), :]
    for copy in copies:
        copy.wait()
    part_recv[me] = jnp.zeros((TILE, width), bf16)
    for n in range(SEQ):
        result = result + part_recv[n].astype(f32)
    out_own[...] = result.astype(bf16)
    out_ref[rows_of(me), :] = out_own[...]
    copies = seq_copies(3, lambda peer: out_own, lambda index: out_ref.at[rows_of(index), :])
    for copy in copies:
        copy.wait()


def fused_device(
    tokens,
    attn_gain,
    qkv_weight,
    out_weight,
    moe_gain,
    router_weight,
    expert_gate,
    expert_up,
    expert_down,
    cache_keys,
    cache_values,
    lengths,
    routes,
):
    count = tokens.shape[0]
    width = out_weight.shape[1]
    requests, slot_count = cache_keys.shape[:2]
    vmem = pl.BlockSpec(memory_space=pltpu.VMEM)
    hbm = pl.BlockSpec(memory_space=pltpu.HBM)
    bf16, f32 = jnp.bfloat16, jnp.float32
    hidden = expert_gate.shape[2]
    return pl.pallas_call(
        layer_kernel,
        out_shape=pltpu.VMEM((count, width), bf16),
        in_specs=[hbm] * 13,
        out_specs=vmem,
        scratch_shapes=[
            pltpu.VMEM(tokens.shape, bf16),
            pltpu.VMEM((D,), f32),
            pltpu.VMEM((width,), f32),
            pltpu.VMEM((1, requests), jnp.int32),
            pltpu.VMEM((TOP, count), jnp.int32),
            pltpu.VMEM((EXPERTS, width), bf16),
            pltpu.VMEM((count, count), jnp.int32),
            pltpu.VMEM(qkv_weight.shape, bf16),
            pltpu.VMEM((requests * slot_count, LANES), bf16),
            pltpu.VMEM((requests * slot_count, LANES), bf16),
            pltpu.VMEM(out_weight.shape, bf16),
            pltpu.VMEM(expert_down.shape, bf16),
            pltpu.VMEM((count, 512), bf16),
            pltpu.VMEM((SEQ, TILE, 512), bf16),
            pltpu.VMEM((TP, TILE, width), bf16),
            pltpu.VMEM((TILE, width), f32),
            pltpu.VMEM((SEQ, TILE, width), bf16),
            pltpu.VMEM((EXPERTS, 2 * hidden, width), bf16),
            pltpu.VMEM((EXPERTS // 2, width, 4 * hidden), bf16),
            pltpu.VMEM((EXPERTS, count, LANES), bf16),
            pltpu.VMEM((8, TOP * TILE, EXPERTS * TILE), bf16),
            pltpu.VMEM((TOP, count, LANES), jnp.int32),
            pltpu.VMEM((8, TOP * TILE, LANES), bf16),
            pltpu.VMEM((4, TOP * TILE, LANES), bf16),
            pltpu.VMEM((4, TOP * TILE, LANES), bf16),
            pltpu.VMEM((4, TOP * TILE, LANES), bf16),
            pltpu.VMEM((count, LANES), f32),
            pltpu.VMEM((count, LANES), bf16),
            pltpu.VMEM((64, LANES), bf16),
            pltpu.VMEM((64, LANES), bf16),
            pltpu.VMEM((64, LANES), bf16),
            pltpu.VMEM((TOP + 1, 64, LANES), f32),
            pltpu.VMEM((6, count, LANES), bf16),
            pltpu.VMEM((count, LANES), bf16),
            pltpu.VMEM((count, LANES), bf16),
            pltpu.VMEM((count, LANES), f32),
            pltpu.VMEM((8, TOP * TILE, LANES), bf16),
            pltpu.VMEM((count, EXPERTS * hidden), bf16),
            pltpu.VMEM((count, width), f32),
            pltpu.VMEM((count, width), bf16),
            pltpu.VMEM((SEQ, TILE, width), bf16),
            pltpu.VMEM((TILE, width), bf16),
            pltpu.SemaphoreType.DMA((15,)),
            pltpu.SemaphoreType.DMA((4, SEQ)),
            pltpu.SemaphoreType.DMA((4, SEQ)),
            pltpu.SemaphoreType.DMA((6 + 3 * CHUNKS,)),
            pltpu.SemaphoreType.DMA((6 + 3 * CHUNKS,)),
        ],
        compiler_params=pltpu.CompilerParams(
            collective_id=0, has_side_effects=True, vmem_limit_bytes=VMEM_LIMIT
        ),
        cost_estimate=pl.CostEstimate(
            flops=2_000_000_000, bytes_accessed=20_000_000, transcendentals=1_000_000
        ),
        name="layer",
    )(
        tokens,
        attn_gain,
        moe_gain,
        lengths.reshape(1, -1),
        routes.T,
        router_weight.T,
        qkv_weight,
        cache_keys.reshape(-1, LANES),
        cache_values.reshape(-1, LANES),
        out_weight,
        jnp.swapaxes(expert_gate, 1, 2),
        jnp.swapaxes(expert_up, 1, 2),
        expert_down,
    )


def solution(mesh):
    in_specs = (
        P(),
        P(),
        P(None, "tp"),
        P(None, "tp"),
        P("tp"),
        P("tp", None),
        P(None, "tp", "seq"),
        P(None, "tp", "seq"),
        P(None, "seq", "tp"),
        P(None, "seq", "tp"),
        P(None, "seq", "tp"),
        P(),
        P(),
    )
    out_specs = P(None, "tp")
    body = fused_device if fits_fused(mesh) else on_device
    return jax.shard_map(
        body, mesh=mesh, in_specs=in_specs, out_specs=out_specs, check_vma=False
    )
```
